32 devices in a mesh: dp: 8 (over z, x), tensor: 4 (over y, core).
Axes of the slice: x: 2, y: 2, z: 4, core: 2. Of those that a mesh axis runs over, the one named last changes fastest.
Arguments:
- piece_table: bfloat16 [32768, 512], P('dp', 'tensor'), may hold values from -6 to 6
- piece_ids: int32 [2, 512, 8], P(None, 'dp'), may hold values from 0 to 32767
- piece_counts: int32 [2, 512], P(None, 'dp'), may hold values from 1 to 7, as said below
- text_ids: int32 [2, 8192], P(None, 'dp'), may hold values from 0 to 63
- cotangent: float32 [2, 8192, 2048], P(None, ('dp', 'tensor')), may hold values from -6 to 6
- rms_gain_one: bfloat16 [2048], replicated, may hold values from 0.25 to 1.75
- w_query: bfloat16 [2048, 2048], P(None, 'tensor'), may hold values from -0.125 to 0.125
- w_key: bfloat16 [2048, 256], P(None, 'tensor'), may hold values from -0.125 to 0.125
- w_value: bfloat16 [2048, 256], P(None, 'tensor'), may hold values from -0.125 to 0.125
- w_output: bfloat16 [2048, 2048], P('tensor'), may hold values from -0.5 to 0.5
- rms_gain_two: bfloat16 [2048], replicated, may hold values from 0.25 to 1.75
- w_gate: bfloat16 [2048, 5632], P(None, 'tensor'), may hold values from -0.125 to 0.125
- w_up: bfloat16 [2048, 5632], P(None, 'tensor'), may hold values from -0.125 to 0.125
- w_down: bfloat16 [5632, 2048], P('tensor'), may hold values from -0.15625 to 0.15625
- ln_gain_one: bfloat16 [2, 512], P(None, ('dp', 'tensor')), may hold values from 0.25 to 1.75
- ln_bias_one: bfloat16 [2, 512], P(None, ('dp', 'tensor')), may hold values from -2.390625 to 2.390625
- w_qkv: bfloat16 [2, 512, 1536], P(None, ('dp', 'tensor')), may hold values from -0.25 to 0.25
- bias_query: bfloat16 [2, 512], P(None, ('dp', 'tensor')), may hold values from -3 to 3
- bias_value: bfloat16 [2, 512], P(None, ('dp', 'tensor')), may hold values from -3 to 3
- w_attn_out: bfloat16 [2, 512, 512], P(None, ('dp', 'tensor')), may hold values from -0.375 to 0.375
- bias_attn_out: bfloat16 [2, 512], P(None, ('dp', 'tensor')), may hold values from -3 to 3
- ln_gain_two: bfloat16 [2, 512], P(None, ('dp', 'tensor')), may hold values from 0.25 to 1.75
- ln_bias_two: bfloat16 [2, 512], P(None, ('dp', 'tensor')), may hold values from -2.390625 to 2.390625
- w_inner: bfloat16 [2, 512, 2048], P(None, ('dp', 'tensor')), may hold values from -0.25 to 0.25
- bias_inner: bfloat16 [2, 2048], P(None, ('dp', 'tensor')), may hold values from -3 to 3
- w_outer: bfloat16 [2, 2048, 512], P(None, ('dp', 'tensor')), may hold values from -0.1875 to 0.1875
- bias_outer: bfloat16 [2, 512], P(None, ('dp', 'tensor')), may hold values from -3 to 3
- final_gain: bfloat16 [512], P(('dp', 'tensor')), may hold values from 0.25 to 1.75
- final_bias: bfloat16 [512], P(('dp', 'tensor')), may hold values from -2.390625 to 2.390625
- w_proj: bfloat16 [512, 2048], P(('dp', 'tensor')), may hold values from -0.25 to 0.25
Outputs:
- lm_out: bfloat16 [2, 8192, 2048], P(None, ('dp', 'tensor'))
- table_grad: float32 [32768, 512], P('dp', 'tensor')
- grad_ln_gain_one: float32 [2, 512], P(None, ('dp', 'tensor'))
- grad_ln_bias_one: float32 [2, 512], P(None, ('dp', 'tensor'))
- grad_w_qkv: float32 [2, 512, 1536], P(None, ('dp', 'tensor'))
- grad_bias_query: float32 [2, 512], P(None, ('dp', 'tensor'))
- grad_bias_value: float32 [2, 512], P(None, ('dp', 'tensor'))
- grad_w_attn_out: float32 [2, 512, 512], P(None, ('dp', 'tensor'))
- grad_bias_attn_out: float32 [2, 512], P(None, ('dp', 'tensor'))
- grad_ln_gain_two: float32 [2, 512], P(None, ('dp', 'tensor'))
- grad_ln_bias_two: float32 [2, 512], P(None, ('dp', 'tensor'))
- grad_w_inner: float32 [2, 512, 2048], P(None, ('dp', 'tensor'))
- grad_bias_inner: float32 [2, 2048], P(None, ('dp', 'tensor'))
- grad_w_outer: float32 [2, 2048, 512], P(None, ('dp', 'tensor'))
- grad_bias_outer: float32 [2, 512], P(None, ('dp', 'tensor'))
- grad_final_gain: float32 [512], P(('dp', 'tensor'))
- grad_final_bias: float32 [512], P(('dp', 'tensor'))
- grad_w_proj: float32 [512, 2048], P(('dp', 'tensor'))
The draws below stay inside these ranges and needn't reach their ends.
Inputs may be any that keep to these rules, and one draw needn't show every extreme that they name: text_ids address entries of the same micro-batch and the same group of 64 entries as the step on tokens states. `piece_counts`: every micro-batch has an entry with 7 filled slots.
All inputs are finite; a program needn't handle non-finite values.
Results may differ from the reference program's by a relative error of at most 0.028.
Values may be sent and summed in bfloat16 or wider, within the bound.
No kernel may reach another device: no remote copies, remote signals or barrier semaphores. Data moves between devices by JAX's collectives and lax.ppermute only.
A program may use at most 448 MiB of HBM per device.

```python
import math
import jax
import jax.numpy as jnp
import numpy as np
from jax import lax

D_H = 512
HYPER_FF = 2048
HEAD_DIM = 64
SLOTS = 8
LAYERS = 2
MICRO = 2
PIECE_VOCAB = 32768
LM_WIDTH = 2048
Q_HEADS = 32
KV_HEADS = 4
LM_FF = 5632
ENT_DEV = 16
SEQ = 1024
HYPER_HEADS = 8
ENTRIES = 512
TEXT = 8192
N_TENSOR = 4


def draw_piece_counts(key, part):
    key = jax.random.fold_in(key, 11)
    first_key, second_key = jax.random.split(key)
    levels = jax.random.randint(first_key, (MICRO, ENTRIES), 0, 64)
    counts = 1 + (levels >= 26).astype(jnp.int32) + (levels >= 42).astype(jnp.int32) + (levels >= 52).astype(jnp.int32)
    counts = counts + (levels >= 57).astype(jnp.int32) + (levels >= 60).astype(jnp.int32) + (levels >= 62).astype(jnp.int32)
    spots = jax.random.randint(second_key, (MICRO,), 0, ENTRIES)
    return counts.at[jnp.arange(MICRO), spots].set(7)


def set_ends(values, stream_key, low, largest):
    shape = values.shape
    place = [jax.random.randint(jax.random.fold_in(stream_key, axis), (), 0, shape[axis]) for axis in range(len(shape))]
    values = values.at[tuple(place)].set(low)
    longest = shape.index(max(shape))
    place[longest] = (place[longest] + 1) % shape[longest]
    return values.at[tuple(place)].set(largest)


def level_of(own_key, dims, pieces, low, high):
    def one(position, shards_of):
        draws = jax.random.uniform(jax.random.fold_in(jax.random.fold_in(own_key, 6), position), (shards_of,), jnp.float32, low / len(pieces), high / len(pieces))
        return jnp.repeat(jnp.exp(draws), dims[position] // shards_of).reshape((-1,) + (1,) * (len(dims) - position - 1))

    level = one(*pieces[0])
    for cut in pieces[1:]:
        level = level * one(*cut)
    return level


def cumulative_ranks(count, lean):
    loads = [(1 << 20) // math.isqrt(rank ** lean) + 1 for rank in range(1, count + 1)]
    width = 1 + sum(loads) // (1 << 30)
    return np.cumsum(np.array([max(1, weight // width) for weight in loads]))


def ranked(key, dims, amount, skew):
    listing = cumulative_ranks(amount, skew)
    ticket = jax.random.randint(jax.random.fold_in(key, 1), dims, 0, int(listing[amount - 1]))
    standing = jnp.searchsorted(jnp.asarray(listing, jnp.int32), ticket, side="right")
    return jax.random.permutation(jax.random.fold_in(key, 2), amount)[standing].astype(jnp.int32)


def scatter_about(rng, shape, deviation, most, pieces=(), kind=jnp.bfloat16):
    loudness = level_of(rng, shape, pieces, -0.22, 0.18) if pieces else 1.0
    drawn = jax.random.normal(rng, shape, jnp.float32) * deviation * loudness
    return jnp.minimum(jnp.maximum(drawn, -most), most).astype(kind)


def setup_inputs(seed: int = 0) -> dict:
    keys = jax.random.split(jax.random.key(seed), 31)
    piece_table = scatter_about(keys[0], (PIECE_VOCAB, D_H), 1.0, 6.0, ((0, 8), (1, 4)))
    piece_ids = set_ends(ranked(keys[1], (MICRO, ENTRIES, SLOTS), PIECE_VOCAB, 2), jax.random.fold_in(keys[1], 3), 0, PIECE_VOCAB - 1).astype(jnp.int32)
    piece_counts = draw_piece_counts(jax.random.fold_in(keys[30], 71), 0)
    text_ids = set_ends(ranked(keys[3], (MICRO, TEXT), N_TENSOR * ENT_DEV, 1), jax.random.fold_in(keys[3], 3), 0, (N_TENSOR * ENT_DEV) - 1).astype(jnp.int32)
    cotangent = scatter_about(keys[4], (MICRO, TEXT, LM_WIDTH), 1.0, 6.0, ((1, 32),), jnp.float32)
    rms_gain_one = jnp.clip(1.0 + 0.15 * jax.random.normal(keys[5], (LM_WIDTH,), jnp.float32), 0.25, 1.75).astype(jnp.bfloat16)
    w_query = scatter_about(keys[6], (LM_WIDTH, Q_HEADS * HEAD_DIM), LM_WIDTH ** -0.5, 0.125, ((1, 4),))
    w_key = scatter_about(keys[7], (LM_WIDTH, KV_HEADS * HEAD_DIM), LM_WIDTH ** -0.5, 0.125, ((1, 4),))
    w_value = scatter_about(keys[8], (LM_WIDTH, KV_HEADS * HEAD_DIM), LM_WIDTH ** -0.5, 0.125, ((1, 4),))
    w_output = scatter_about(keys[9], (Q_HEADS * HEAD_DIM, LM_WIDTH), (LM_WIDTH // 16) ** -0.5, 0.5, ((0, 4),))
    rms_gain_two = jnp.clip(1.0 + 0.15 * jax.random.normal(keys[10], (LM_WIDTH,), jnp.float32), 0.25, 1.75).astype(jnp.bfloat16)
    w_gate = scatter_about(keys[11], (LM_WIDTH, LM_FF), LM_WIDTH ** -0.5, 0.125, ((1, 4),))
    w_up = scatter_about(keys[12], (LM_WIDTH, LM_FF), LM_WIDTH ** -0.5, 0.125, ((1, 4),))
    w_down = scatter_about(keys[13], (LM_FF, LM_WIDTH), (LM_FF // 4) ** -0.5, 0.15625, ((0, 4),))
    ln_gain_one = jnp.clip(1.0 + 0.15 * jax.random.normal(keys[14], (LAYERS, D_H), jnp.float32), 0.25, 1.75).astype(jnp.bfloat16)
    ln_bias_one = scatter_about(keys[15], (LAYERS, D_H), 0.4, 2.390625, ((1, 32),))
    w_qkv = scatter_about(keys[16], (LAYERS, D_H, 3 * D_H), D_H ** -0.5, 0.25, ((1, 32),))
    bias_query = scatter_about(keys[17], (LAYERS, D_H), 0.5, 3.0, ((1, 32),))
    bias_value = scatter_about(keys[18], (LAYERS, D_H), 0.5, 3.0, ((1, 32),))
    w_attn_out = scatter_about(keys[19], (LAYERS, D_H, D_H), (D_H // 2) ** -0.5, 0.375, ((1, 32),))
    bias_attn_out = scatter_about(keys[20], (LAYERS, D_H), 0.5, 3.0, ((1, 32),))
    ln_gain_two = jnp.clip(1.0 + 0.15 * jax.random.normal(keys[21], (LAYERS, D_H), jnp.float32), 0.25, 1.75).astype(jnp.bfloat16)
    ln_bias_two = scatter_about(keys[22], (LAYERS, D_H), 0.4, 2.390625, ((1, 32),))
    w_inner = scatter_about(keys[23], (LAYERS, D_H, HYPER_FF), D_H ** -0.5, 0.25, ((1, 32),))
    bias_inner = scatter_about(keys[24], (LAYERS, HYPER_FF), 0.5, 3.0, ((1, 32),))
    w_outer = scatter_about(keys[25], (LAYERS, HYPER_FF, D_H), (HYPER_FF // 2) ** -0.5, 0.1875, ((1, 32),))
    bias_outer = scatter_about(keys[26], (LAYERS, D_H), 0.5, 3.0, ((1, 32),))
    final_gain = jnp.clip(1.0 + 0.15 * jax.random.normal(keys[27], (D_H,), jnp.float32), 0.25, 1.75).astype(jnp.bfloat16)
    final_bias = scatter_about(keys[28], (D_H,), 0.4, 2.390625, ((0, 32),))
    w_proj = scatter_about(keys[29], (D_H, LM_WIDTH), D_H ** -0.5, 0.25, ((0, 32),))
    return {"piece_table": piece_table, "piece_ids": piece_ids, "piece_counts": piece_counts, "text_ids": text_ids, "cotangent": cotangent, "rms_gain_one": rms_gain_one, "w_query": w_query, "w_key": w_key, "w_value": w_value, "w_output": w_output, "rms_gain_two": rms_gain_two, "w_gate": w_gate, "w_up": w_up, "w_down": w_down, "ln_gain_one": ln_gain_one, "ln_bias_one": ln_bias_one, "w_qkv": w_qkv, "bias_query": bias_query, "bias_value": bias_value, "w_attn_out": w_attn_out, "bias_attn_out": bias_attn_out, "ln_gain_two": ln_gain_two, "ln_bias_two": ln_bias_two, "w_inner": w_inner, "bias_inner": bias_inner, "w_outer": w_outer, "bias_outer": bias_outer, "final_gain": final_gain, "final_bias": final_bias, "w_proj": w_proj}


EPS_NORM = 1e-05
HIGH = lax.Precision.HIGHEST

@jax.custom_vjp
def low(v):
    return lax.optimization_barrier(v.astype(jnp.bfloat16)).astype(jnp.float32)

@jax.custom_vjp
def low_back(v):
    return v

def low_keep(v):
    return (low(v), None)

def low_pass(kept, grad):
    return (grad,)

def back_keep(v):
    return (v, None)

def back_low(kept, grad):
    return (low(grad),)
low.defvjp(low_keep, low_pass)
low_back.defvjp(back_keep, back_low)

def mult(left, right):
    return jnp.dot(left, right, precision=HIGH, preferred_element_type=jnp.float32)

def layer_norm(values, gain, bias):
    centered = values - lax.optimization_barrier(jnp.mean(values, axis=-1, keepdims=True))
    inverse = lax.rsqrt(lax.optimization_barrier(jnp.mean(centered * centered, axis=-1, keepdims=True)) + EPS_NORM)
    return centered * inverse * gain + bias

def rms_norm(values, gain):
    return values * lax.rsqrt(lax.optimization_barrier(jnp.mean(values * values, axis=-1, keepdims=True)) + EPS_NORM) * gain

def rotary_tables(seq_length):
    half_dim = HEAD_DIM // 2
    freqs = 10000.0 ** (-jnp.arange(half_dim, dtype=jnp.float32) * 2.0 / HEAD_DIM)
    angles = jnp.arange(seq_length, dtype=jnp.float32)[:, None] * freqs[None, :]
    angles = jnp.concatenate([angles, angles], axis=-1)
    return (jnp.cos(angles), jnp.sin(angles))

def rotate(values, cosine, sine):
    half_dim = HEAD_DIM // 2
    turned = jnp.concatenate([-values[..., half_dim:], values[..., :half_dim]], axis=-1)
    return values * cosine[:, None, :] + turned * sine[:, None, :]

def hyper_layer(hidden_rows, valid_keys, weights):
    gain_one, shift_one, qkv_weight, query_bias, value_bias, out_weight, out_bias, gain_two, shift_two, inner_weight, inner_bias, outer_weight, outer_bias = weights
    batch_rows = hidden_rows.shape[0]
    normed_in = low(layer_norm(hidden_rows, gain_one, shift_one))
    mixed = low_back(mult(normed_in, qkv_weight))
    queries = (mixed[..., :D_H] + query_bias).reshape(batch_rows, SLOTS, HYPER_HEADS, HEAD_DIM)
    keys_all = mixed[..., D_H:2 * D_H].reshape(batch_rows, SLOTS, HYPER_HEADS, HEAD_DIM)
    values_all = (mixed[..., 2 * D_H:] + value_bias).reshape(batch_rows, SLOTS, HYPER_HEADS, HEAD_DIM)
    scores = jnp.einsum('bqhd,bkhd->bhqk', queries, keys_all, precision=HIGH) * HEAD_DIM ** (-0.5)
    scores = jnp.where(valid_keys[:, None, None, :], scores, -1e+30)
    weights_soft = jnp.exp(scores - lax.optimization_barrier(jnp.max(scores, axis=-1, keepdims=True)))
    weights_soft = weights_soft / lax.optimization_barrier(jnp.sum(weights_soft, axis=-1, keepdims=True))
    context = jnp.einsum('bhqk,bkhd->bqhd', weights_soft, values_all, precision=HIGH).reshape(batch_rows, SLOTS, D_H)
    middle = hidden_rows + low_back(mult(low(context), out_weight)) + out_bias
    normed_mid = low(layer_norm(middle, gain_two, shift_two))
    inner = low_back(mult(normed_mid, inner_weight)) + inner_bias
    activated = low(jax.nn.gelu(inner, approximate=False))
    return middle + low_back(mult(activated, outer_weight)) + outer_bias

def lm_block(tokens, frozen):
    gain_one, query_weight, key_weight, value_weight, out_weight, gain_two, gate_weight, up_weight, down_weight = frozen
    seq_length = tokens.shape[0]
    cosine, sine = rotary_tables(seq_length)
    normed_one = low(rms_norm(tokens, gain_one))
    queries = low(rotate(low_back(mult(normed_one, query_weight)).reshape(seq_length, Q_HEADS, HEAD_DIM), cosine, sine))
    keys_all = low(rotate(low_back(mult(normed_one, key_weight)).reshape(seq_length, KV_HEADS, HEAD_DIM), cosine, sine))
    values_all = low(low_back(mult(normed_one, value_weight))).reshape(seq_length, KV_HEADS, HEAD_DIM)
    queries = queries.reshape(seq_length, KV_HEADS, Q_HEADS // KV_HEADS, HEAD_DIM)
    scores = low_back(jnp.einsum('sjgd,tjd->jgst', queries, keys_all, precision=HIGH) * HEAD_DIM ** (-0.5))
    positions = jnp.arange(seq_length)
    causal = positions[:, None] >= positions[None, :]
    scores = jnp.where(causal, scores, -1e+30)
    soft = jnp.exp(scores - lax.optimization_barrier(jnp.max(scores, axis=-1, keepdims=True)))
    soft = soft / lax.optimization_barrier(jnp.sum(soft, axis=-1, keepdims=True))
    context = jnp.einsum('jgst,tjd->sjgd', low(soft), values_all, precision=HIGH)
    context = low(low_back(context)).reshape(seq_length, LM_WIDTH)
    hidden = tokens + low_back(mult(context, out_weight))
    normed_two = low(rms_norm(hidden, gain_two))
    gate = low_back(mult(normed_two, gate_weight))
    upward = low_back(mult(normed_two, up_weight))
    activated = low(jax.nn.silu(gate) * upward)
    return hidden + low_back(mult(activated, down_weight))

def reference(piece_table, piece_ids, piece_counts, text_ids, cotangent, rms_gain_one, w_query, w_key, w_value, w_output, rms_gain_two, w_gate, w_up, w_down, ln_gain_one, ln_bias_one, w_qkv, bias_query, bias_value, w_attn_out, bias_attn_out, ln_gain_two, ln_bias_two, w_inner, bias_inner, w_outer, bias_outer, final_gain, final_bias, w_proj):
    frozen = tuple((a.astype(jnp.float32) for a in (rms_gain_one, w_query, w_key, w_value, w_output, rms_gain_two, w_gate, w_up, w_down)))
    hyper = tuple((a.astype(jnp.float32) for a in (ln_gain_one, ln_bias_one, w_qkv, bias_query, bias_value, w_attn_out, bias_attn_out, ln_gain_two, ln_bias_two, w_inner, bias_inner, w_outer, bias_outer, final_gain, final_bias, w_proj)))
    table = piece_table.astype(jnp.float32)
    valid_keys = (jnp.arange(SLOTS)[None, None, :] < piece_counts[..., None]).reshape(MICRO * ENTRIES, SLOTS)
    group_count = TEXT // SEQ
    token_ids = text_ids.reshape(MICRO, group_count, SEQ)

    def forward(table_rows, params):
        rows = low_back(table_rows[piece_ids])
        hidden_rows = rows.reshape(MICRO * ENTRIES, SLOTS, D_H)
        for layer_index in range(LAYERS):
            hidden_rows = hyper_layer(hidden_rows, valid_keys, [stack[layer_index] for stack in params[:13]])
        pooled_norm = low(layer_norm(hidden_rows[:, 0], params[13], params[14]))
        embeds = low(low_back(mult(pooled_norm, params[15])))
        embeds = embeds.reshape(MICRO, group_count, ENTRIES // group_count, LM_WIDTH)
        tokens = jnp.take_along_axis(embeds, token_ids[..., None], axis=2)
        block = lax.map(jax.checkpoint(lambda seq_tokens: lm_block(seq_tokens, frozen)), tokens.reshape(MICRO * group_count, SEQ, LM_WIDTH))
        return block.reshape(MICRO, TEXT, LM_WIDTH)
    block_out, pull = jax.vjp(forward, table, hyper)
    grad_table, grad_hyper = pull(cotangent.astype(jnp.float32))
    return (block_out.astype(jnp.bfloat16), grad_table, grad_hyper[0], grad_hyper[1], grad_hyper[2], grad_hyper[3], grad_hyper[4], grad_hyper[5], grad_hyper[6], grad_hyper[7], grad_hyper[8], grad_hyper[9], grad_hyper[10], grad_hyper[11], grad_hyper[12], grad_hyper[13], grad_hyper[14], grad_hyper[15])
```

```python
import jax
import jax.numpy as jnp
from jax import lax
from jax.experimental import pallas as pl
from jax.experimental.pallas import tpu as pltpu
from jax.sharding import PartitionSpec as P

HEAD_DIM = 64
EPS_NORM = 1e-05
HIGH = lax.Precision.HIGHEST
SQRT_HALF = 0.7071067811865476
INV_SQRT_TAU = 0.3989422804014327
BOTH = ("dp", "tensor")
F32 = jnp.float32
BF16 = jnp.bfloat16


def matmul(left, right):
    return jnp.dot(left, right, preferred_element_type=F32)


def matmul_right_t(left, right):
    return lax.dot_general(left, right, (((1,), (1,)), ((), ())), preferred_element_type=F32)


def matmul_left_t(left, right):
    return lax.dot_general(left, right, (((0,), (0,)), ((), ())), preferred_element_type=F32)


def split_two(values):
    high = lax.reduce_precision(values, 8, 7)
    return high.astype(BF16), (values - high).astype(BF16)


def norm_parts(values):
    centered = values - jnp.mean(values, axis=-1, keepdims=True)
    inverse = lax.rsqrt(jnp.mean(centered * centered, axis=-1, keepdims=True) + EPS_NORM)
    return (centered * inverse, inverse)


def norm_back(normed, inverse, grad_scaled):
    return inverse * (
        grad_scaled
        - jnp.mean(grad_scaled, axis=-1, keepdims=True)
        - normed * jnp.mean(grad_scaled * normed, axis=-1, keepdims=True)
    )


def rms_parts(values):
    return lax.rsqrt(jnp.mean(values * values, axis=-1, keepdims=True) + EPS_NORM)


def rms_back(values, inverse, grad_scaled):
    return inverse * grad_scaled - values * inverse**3 * jnp.mean(
        grad_scaled * values, axis=-1, keepdims=True
    )


def rotary_tables(seq_length):
    half_dim = HEAD_DIM // 2
    freqs = 10000.0 ** (-jnp.arange(half_dim, dtype=F32) * 2.0 / HEAD_DIM)
    angles = jnp.arange(seq_length, dtype=F32)[:, None] * freqs[None, :]
    angles = jnp.concatenate([angles, angles], axis=-1)
    return (jnp.cos(angles), jnp.sin(angles))


def half_turn(values):
    half_dim = HEAD_DIM // 2
    return jnp.concatenate([-values[..., half_dim:], values[..., :half_dim]], axis=-1)


def rotate(values, cosine, sine):
    return values * cosine[:, None, :] + half_turn(values) * sine[:, None, :]


def unrotate(grads, cosine, sine):
    return grads * cosine[:, None, :] - half_turn(grads * sine[:, None, :])


def swap(values, axis, bit):
    size = lax.axis_size(axis)
    return lax.ppermute(values, axis, [(i, i ^ bit) for i in range(size)])


def ordered_pair(own, other, index):
    first = jnp.where(index == 0, own, other)
    second = jnp.where(index == 0, other, own)
    return jnp.stack([first, second])


def gather_tensor(values, core):
    from_core = swap(values, "tensor", 1)
    from_chip = swap(values, "tensor", 2)
    from_both = swap(from_chip, "tensor", 1)
    return ordered_pair(values, from_core, core), ordered_pair(from_chip, from_both, core)


def scatter_chip(partial, core):
    sent = lax.dynamic_index_in_dim(partial, 1 - core, 0, keepdims=False)
    kept = lax.dynamic_index_in_dim(partial, core, 0, keepdims=False)
    return kept.astype(F32) + swap(sent, "tensor", 1).astype(F32)


def scatter_tensor(own_chip, other_chip, core):
    away = scatter_chip(other_chip, core).astype(BF16)
    arrived = swap(away, "tensor", 2)
    return scatter_chip(own_chip, core) + arrived.astype(F32)


def gather_dp(values):
    size = lax.axis_size("dp")
    index = lax.axis_index("dp")
    bits = size.bit_length() - 1
    held = values[(None,) * bits]
    for bit in range(bits - 1, -1, -1):
        axis = bits - 1 - bit
        other = swap(held, "dp", 1 << bit)
        side = (index >> bit) & 1
        low = jnp.where(side == 0, held, other)
        high = jnp.where(side == 0, other, held)
        held = jnp.concatenate([low, high], axis=axis)
    return held.reshape((size,) + values.shape)


def lookup_kernel(ids_ref, table_ref, out_ref):
    rows = ids_ref.shape[0]
    height = table_ref.shape[0]
    places = lax.broadcasted_iota(jnp.int32, (rows, height), 1)
    chosen = jnp.where(ids_ref[...] == places, 1.0, 0.0).astype(BF16)
    out_ref[...] = matmul(chosen, table_ref[...]).astype(BF16)


def lookup(ids, table):
    count = ids.shape[0]
    height, width = table.shape
    rows = 512
    return pl.pallas_call(
        lookup_kernel,
        grid=(count // rows,),
        in_specs=[
            pl.BlockSpec((rows, 1), lambda i: (i, 0)),
            pl.BlockSpec((height, width), lambda i: (0, 0)),
        ],
        out_specs=pl.BlockSpec((rows, width), lambda i: (i, 0)),
        out_shape=jax.ShapeDtypeStruct((count, width), BF16),
        compiler_params=pltpu.CompilerParams(vmem_limit_bytes=48 << 20),
        cost_estimate=pl.CostEstimate(
            flops=2 * count * height * width, bytes_accessed=4 * count * width, transcendentals=0
        ),
        name="lookup",
    )(ids[:, None], table)


def collect_kernel(ids_ref, rows_ref, out_ref):
    @pl.when(pl.program_id(0) == 0)
    def _():
        out_ref[...] = jnp.zeros_like(out_ref)

    height = out_ref.shape[0]
    places = lax.broadcasted_iota(jnp.int32, (height, ids_ref.shape[1]), 0)
    chosen = jnp.where(ids_ref[...] == places, 1.0, 0.0).astype(BF16)
    out_ref[...] += matmul(chosen, rows_ref[...])


def collect(ids, values, height):
    count, width = values.shape
    rows = 512
    return pl.pallas_call(
        collect_kernel,
        grid=(count // rows,),
        in_specs=[
            pl.BlockSpec((1, rows), lambda i: (0, i)),
            pl.BlockSpec((rows, width), lambda i: (i, 0)),
        ],
        out_specs=pl.BlockSpec((height, width), lambda i: (0, 0)),
        out_shape=jax.ShapeDtypeStruct((height, width), F32),
        compiler_params=pltpu.CompilerParams(vmem_limit_bytes=48 << 20),
        cost_estimate=pl.CostEstimate(
            flops=2 * count * height * width, bytes_accessed=4 * count * width, transcendentals=0
        ),
        name="collect",
    )(ids[None, :], values)


def hyper_forward(hidden_rows, valid_keys, weights):
    (
        gain_one,
        shift_one,
        qkv_weight,
        query_bias,
        value_bias,
        out_weight,
        out_bias,
        gain_two,
        shift_two,
        inner_weight,
        inner_bias,
        outer_weight,
        outer_bias,
    ) = weights
    entry_count, slot_count = valid_keys.shape
    width = hidden_rows.shape[1]
    normed_one, inverse_one = norm_parts(hidden_rows)
    normed_in = (normed_one * gain_one.astype(jnp.float32) + shift_one.astype(jnp.float32)).astype(
        jnp.bfloat16
    )
    mixed = matmul(normed_in, qkv_weight)
    queries = (mixed[:, :width] + query_bias.astype(jnp.float32)).reshape(
        entry_count, slot_count, -1, HEAD_DIM
    )
    keys_all = mixed[:, width : 2 * width].reshape(entry_count, slot_count, -1, HEAD_DIM)
    values_all = (mixed[:, 2 * width :] + value_bias.astype(jnp.float32)).reshape(
        entry_count, slot_count, -1, HEAD_DIM
    )
    scores = jnp.einsum("bqhd,bkhd->bhqk", queries, keys_all, precision=HIGH) * HEAD_DIM ** (-0.5)
    scores = jnp.where(valid_keys[:, None, None, :], scores, -1e30)
    weights_soft = jnp.exp(scores - jnp.max(scores, axis=-1, keepdims=True))
    weights_soft = weights_soft / jnp.sum(weights_soft, axis=-1, keepdims=True)
    context = jnp.einsum("bhqk,bkhd->bqhd", weights_soft, values_all, precision=HIGH).reshape(
        entry_count * slot_count, width
    )
    context_low = context.astype(jnp.bfloat16)
    middle = hidden_rows + matmul(context_low, out_weight) + out_bias.astype(jnp.float32)
    normed_two, inverse_two = norm_parts(middle)
    normed_mid = (normed_two * gain_two.astype(jnp.float32) + shift_two.astype(jnp.float32)).astype(
        jnp.bfloat16
    )
    inner = matmul(normed_mid, inner_weight) + inner_bias.astype(jnp.float32)
    activated = jax.nn.gelu(inner, approximate=False).astype(jnp.bfloat16)
    result = middle + matmul(activated, outer_weight) + outer_bias.astype(jnp.float32)
    kept = (
        normed_one,
        inverse_one,
        normed_in,
        queries,
        keys_all,
        values_all,
        weights_soft,
        context_low,
        normed_two,
        inverse_two,
        normed_mid,
        inner,
        activated,
    )
    return (result, kept)


def hyper_backward(grad_rows, kept, weights):
    (
        gain_one,
        shift_one,
        qkv_weight,
        query_bias,
        value_bias,
        out_weight,
        out_bias,
        gain_two,
        shift_two,
        inner_weight,
        inner_bias,
        outer_weight,
        outer_bias,
    ) = weights
    (
        normed_one,
        inverse_one,
        normed_in,
        queries,
        keys_all,
        values_all,
        weights_soft,
        context_low,
        normed_two,
        inverse_two,
        normed_mid,
        inner,
        activated,
    ) = kept
    width = grad_rows.shape[1]
    grad_outer_bias = jnp.sum(grad_rows, axis=0)
    grad_rows_low = grad_rows.astype(jnp.bfloat16)
    grad_outer = matmul_left_t(activated, grad_rows_low)
    grad_active = matmul_right_t(grad_rows_low, outer_weight)
    slope = (
        0.5 * (1.0 + lax.erf(inner * SQRT_HALF))
        + inner * jnp.exp(-0.5 * inner * inner) * INV_SQRT_TAU
    )
    grad_inner = grad_active * slope
    grad_inner_bias = jnp.sum(grad_inner, axis=0)
    grad_inner_low = grad_inner.astype(jnp.bfloat16)
    grad_inner_weight = matmul_left_t(normed_mid, grad_inner_low)
    grad_normed_mid = matmul_right_t(grad_inner_low, inner_weight)
    grad_gain_two = jnp.sum(grad_normed_mid * normed_two, axis=0)
    grad_shift_two = jnp.sum(grad_normed_mid, axis=0)
    grad_middle = grad_rows + norm_back(
        normed_two, inverse_two, grad_normed_mid * gain_two.astype(jnp.float32)
    )
    grad_out_bias = jnp.sum(grad_middle, axis=0)
    grad_middle_low = grad_middle.astype(jnp.bfloat16)
    grad_out_weight = matmul_left_t(context_low, grad_middle_low)
    grad_context = matmul_right_t(grad_middle_low, out_weight).reshape(queries.shape)
    grad_soft = jnp.einsum("bqhd,bkhd->bhqk", grad_context, values_all, precision=HIGH)
    grad_scores = (
        weights_soft
        * (grad_soft - jnp.sum(weights_soft * grad_soft, axis=-1, keepdims=True))
        * HEAD_DIM ** (-0.5)
    )
    grad_values = jnp.einsum("bhqk,bqhd->bkhd", weights_soft, grad_context, precision=HIGH).reshape(
        -1, width
    )
    grad_queries = jnp.einsum("bhqk,bkhd->bqhd", grad_scores, keys_all, precision=HIGH).reshape(
        -1, width
    )
    grad_keys = jnp.einsum("bhqk,bqhd->bkhd", grad_scores, queries, precision=HIGH).reshape(
        -1, width
    )
    grad_query_bias = jnp.sum(grad_queries, axis=0)
    grad_value_bias = jnp.sum(grad_values, axis=0)
    grad_mixed_low = jnp.concatenate([grad_queries, grad_keys, grad_values], axis=1).astype(
        jnp.bfloat16
    )
    grad_qkv = matmul_left_t(normed_in, grad_mixed_low)
    grad_normed_in = matmul_right_t(grad_mixed_low, qkv_weight)
    grad_gain_one = jnp.sum(grad_normed_in * normed_one, axis=0)
    grad_shift_one = jnp.sum(grad_normed_in, axis=0)
    grad_below = grad_middle + norm_back(
        normed_one, inverse_one, grad_normed_in * gain_one.astype(jnp.float32)
    )
    return (
        grad_below,
        (
            grad_gain_one,
            grad_shift_one,
            grad_qkv,
            grad_query_bias,
            grad_value_bias,
            grad_out_weight,
            grad_out_bias,
            grad_gain_two,
            grad_shift_two,
            grad_inner_weight,
            grad_inner_bias,
            grad_outer,
            grad_outer_bias,
        ),
    )


VECTORS = 8


def pack_params(shards):
    (g1, b1, w_qkv, bq, bv, w_ao, bao, g2, b2, w_in, bin_, w_out, bout, fg, fb, w_proj) = shards
    layers, own, _ = w_qkv.shape
    width = w_ao.shape[2]
    pieces = []
    for layer in range(layers):
        pieces += [w_qkv[layer, :, i * width : (i + 1) * width] for i in range(3)]
        pieces += [w_ao[layer]]
        pieces += [w_in[layer, :, i * width : (i + 1) * width] for i in range(4)]
        pieces += [w_out[layer]]
    pieces += [w_proj[:, i * width : (i + 1) * width] for i in range(4)]
    small = jnp.concatenate(
        [jnp.stack([g1, b1, bq, bv, bao, g2, b2, bout]).reshape(-1), fg, fb, bin_.reshape(-1)]
    )
    small = jnp.pad(small, (0, 16 * width - small.shape[0])).reshape(16, width)
    return jnp.concatenate(pieces + [small], axis=0)


def unpack_params(gathered, own, layers):
    devices, _, width = gathered.shape
    at = [0]

    def take(rows):
        part = gathered[:, at[0] : at[0] + rows].reshape(devices * rows, width)
        at[0] += rows
        return part

    weights = []
    for layer in range(layers):
        qkv = [take(own) for _ in range(3)]
        attn_out = take(own)
        inner = [take(own) for _ in range(4)]
        outer = take(4 * own)
        weights.append((qkv, attn_out, inner, outer))
    proj = [take(own) for _ in range(4)]
    small = gathered[:, at[0] : at[0] + 16].reshape(devices, 16 * width)
    count = VECTORS * layers + 2
    vectors = small[:, : count * own].reshape(devices, count, own).transpose(1, 0, 2)
    vectors = vectors.reshape(count, devices * own)
    inner_bias = small[:, count * own : count * own + layers * 4 * own]
    inner_bias = inner_bias.reshape(devices, layers, 4 * own).transpose(1, 0, 2)
    return weights, proj, vectors, inner_bias.reshape(layers, -1)


def local(
    piece_table,
    piece_ids,
    piece_counts,
    text_ids,
    cotangent,
    rms_gain_one,
    w_query,
    w_key,
    w_value,
    w_output,
    rms_gain_two,
    w_gate,
    w_up,
    w_down,
    *shard_params,
):
    tensor_index = lax.axis_index("tensor")
    dp_index = lax.axis_index("dp")
    tensor_size = lax.axis_size("tensor")
    dp_size = lax.axis_size("dp")
    devices = tensor_size * dp_size
    chip = tensor_index // 2
    core = tensor_index % 2
    micro_count, group_entries, slot_count = piece_ids.shape
    own_entries = group_entries // tensor_size
    seq_length = text_ids.shape[1]
    share = cotangent.shape[1]
    layer_count, own, _ = shard_params[2].shape
    width = shard_params[5].shape[2]
    lm_width = cotangent.shape[2]
    table_rows, table_cols = piece_table.shape
    gain_first = rms_gain_one.astype(F32)
    gain_second = rms_gain_two.astype(F32)
    cosine, sine = rotary_tables(seq_length)
    positions = jnp.arange(seq_length)
    causal = positions[:, None] >= positions[None, :]
    scale = HEAD_DIM ** (-0.5)

    gathered = lax.all_gather(pack_params(shard_params), BOTH, axis=0)

    ids_all = gather_dp(piece_ids)
    ids_all = ids_all.reshape(dp_size, micro_count, tensor_size, own_entries, slot_count)
    ids_all = ids_all.transpose(0, 2, 1, 3, 4).reshape(-1) - dp_index * table_rows
    own_rows = micro_count * own_entries * slot_count
    looked = lookup(ids_all, piece_table).reshape(devices, own_rows, table_cols)
    looked = lax.all_to_all(looked, BOTH, split_axis=0, concat_axis=0, tiled=True)
    looked = jnp.sum(
        looked.reshape(dp_size, tensor_size, own_rows, table_cols).astype(F32), axis=0
    )
    hidden_rows = looked.transpose(1, 0, 2).reshape(own_rows, width)

    weights, proj, vectors, inner_bias = unpack_params(gathered, own, layer_count)
    layer_weights = []
    for layer in range(layer_count):
        qkv, attn_out, inner, outer = weights[layer]
        vec = [vectors[i * layer_count + layer] for i in range(VECTORS)]
        layer_weights.append(
            (
                vec[0],
                vec[1],
                jnp.concatenate(qkv, axis=1),
                vec[2],
                vec[3],
                attn_out,
                vec[4],
                vec[5],
                vec[6],
                jnp.concatenate(inner, axis=1),
                inner_bias[layer],
                outer,
                vec[7],
            )
        )
    final_gain = vectors[VECTORS * layer_count].astype(F32)
    final_bias = vectors[VECTORS * layer_count + 1].astype(F32)
    proj = jnp.concatenate(proj, axis=1)

    counts_own = lax.dynamic_slice_in_dim(piece_counts, tensor_index * own_entries, own_entries, 1)
    valid_keys = jnp.arange(slot_count)[None, :] < counts_own.reshape(-1)[:, None]
    saved = []
    for layer in range(layer_count):
        hidden_rows, kept = hyper_forward(hidden_rows, valid_keys, layer_weights[layer])
        saved.append(kept)
    pooled = hidden_rows.reshape(micro_count * own_entries, slot_count, width)[:, 0]
    normed_final, inverse_final = norm_parts(pooled)
    pooled_norm = (normed_final * final_gain + final_bias).astype(BF16)
    embeds = matmul(pooled_norm, proj).astype(BF16)
    own_pair, other_pair = gather_tensor(embeds, core)
    embeds_all = ordered_pair(own_pair, other_pair, chip)
    embeds_all = embeds_all.reshape(tensor_size, micro_count, own_entries, lm_width)

    chip_rows = 2 * share
    out_parts = []
    grad_embeds = []
    for micro in range(micro_count):
        embeds_group = embeds_all[:, micro].reshape(group_entries, lm_width)
        token_ids = text_ids[micro]
        onehot = token_ids[:, None] == jnp.arange(group_entries)[None, :]
        onehot_low = onehot.astype(BF16)
        onehot_share = lax.dynamic_slice_in_dim(onehot_low, tensor_index * share, share, 0)
        embeds_wide = embeds_group.astype(F32)
        inverse_first = rms_parts(embeds_wide)
        normed_first = (embeds_wide * inverse_first * gain_first).astype(BF16)
        mixed = jnp.concatenate(
            [matmul(normed_first, w_query), matmul(normed_first, w_key), matmul(normed_first, w_value)],
            axis=1,
        )
        mixed_high, mixed_low = split_two(mixed)
        mixed = matmul(onehot_low, mixed_high) + matmul(onehot_low, mixed_low)
        q_width = w_query.shape[1]
        k_width = w_key.shape[1]
        queries = rotate(
            mixed[:, :q_width].reshape(seq_length, -1, HEAD_DIM), cosine, sine
        ).astype(BF16)
        keys_rot = rotate(
            mixed[:, q_width : q_width + k_width].reshape(seq_length, -1, HEAD_DIM), cosine, sine
        ).astype(BF16)
        values_lm = mixed[:, q_width + k_width :].astype(BF16).reshape(seq_length, -1, HEAD_DIM)
        kv_local = keys_rot.shape[1]
        queries = queries.reshape(seq_length, kv_local, -1, HEAD_DIM)
        scores = (
            jnp.einsum("sjgd,tjd->jgst", queries, keys_rot, preferred_element_type=F32) * scale
        )
        scores = jnp.where(causal, scores, -1e30)
        row_max = jnp.max(scores, axis=-1, keepdims=True)
        expon = jnp.exp(scores - row_max)
        row_total = jnp.sum(expon, axis=-1, keepdims=True)
        log_total = row_max + jnp.log(row_total)
        soft_low = (expon / row_total).astype(BF16)
        context = (
            jnp.einsum("jgst,tjd->sjgd", soft_low, values_lm, preferred_element_type=F32)
            .astype(BF16)
            .reshape(2, chip_rows, -1)
        )

        def by_core(values):
            return values.astype(BF16).reshape(2, share, -1)

        def half(values, which):
            return lax.dynamic_index_in_dim(values, which, 0, keepdims=False)

        other_part = by_core(matmul(half(context, 1 - chip), w_output))
        own_part = by_core(matmul(half(context, chip), w_output))
        attn_share = scatter_tensor(own_part, other_part, core)
        tokens_share = matmul(onehot_share, embeds_group)
        hidden_share = tokens_share + attn_share
        inverse_second = rms_parts(hidden_share)
        normed_second = (hidden_share * inverse_second * gain_second).astype(BF16)
        grad_output = cotangent[micro]
        normed_halves = gather_tensor(normed_second, core)
        output_halves = gather_tensor(grad_output.astype(BF16), core)
        mlp_parts = []
        grad_parts = []
        for normed_half, grad_half in zip(normed_halves, output_halves):
            normed_half = normed_half.reshape(chip_rows, lm_width)
            grad_half = grad_half.reshape(chip_rows, lm_width)
            grad_active = matmul_right_t(grad_half, w_down)
            gate = matmul(normed_half, w_gate)
            upward = matmul(normed_half, w_up)
            sigmoid_gate = jax.nn.sigmoid(gate)
            silu_gate = gate * sigmoid_gate
            activated = (silu_gate * upward).astype(BF16)
            mlp_parts.append(by_core(matmul(activated, w_down)))
            slope_silu = sigmoid_gate * (1.0 + gate * (1.0 - sigmoid_gate))
            grad_gate = (grad_active * upward * slope_silu).astype(BF16)
            grad_upward = (grad_active * silu_gate).astype(BF16)
            grad_parts.append(
                by_core(matmul_right_t(grad_gate, w_gate) + matmul_right_t(grad_upward, w_up))
            )
        grad_normed_second = scatter_tensor(grad_parts[0], grad_parts[1], core)
        mlp_share = scatter_tensor(mlp_parts[0], mlp_parts[1], core)
        out_parts.append((hidden_share + mlp_share).astype(BF16))
        grad_hidden = grad_output + rms_back(
            hidden_share, inverse_second, grad_normed_second * gain_second
        )
        grad_hidden_low = grad_hidden.astype(BF16)
        attn_halves = gather_tensor(grad_hidden_low, core)
        context_halves = [
            matmul_right_t(part.reshape(chip_rows, lm_width), w_output).astype(BF16)
            for part in attn_halves
        ]
        grad_context = ordered_pair(context_halves[0], context_halves[1], chip)
        grad_context = grad_context.reshape(queries.shape)
        scores_again = (
            jnp.einsum("sjgd,tjd->jgst", queries, keys_rot, preferred_element_type=F32) * scale
        )
        soft_again = jnp.where(causal, jnp.exp(scores_again - log_total), 0.0)
        grad_soft = jnp.einsum(
            "sjgd,tjd->jgst", grad_context, values_lm, preferred_element_type=F32
        )
        grad_scores = (
            soft_again * (grad_soft - jnp.sum(soft_again * grad_soft, axis=-1, keepdims=True))
        ).astype(BF16)
        grad_values = jnp.einsum(
            "jgst,sjgd->tjd", soft_again.astype(BF16), grad_context, preferred_element_type=F32
        )
        grad_queries = (
            jnp.einsum("jgst,tjd->sjgd", grad_scores, keys_rot, preferred_element_type=F32) * scale
        )
        grad_keys = (
            jnp.einsum("jgst,sjgd->tjd", grad_scores, queries, preferred_element_type=F32) * scale
        )
        grad_queries = unrotate(grad_queries.reshape(seq_length, -1, HEAD_DIM), cosine, sine)
        grad_keys = unrotate(grad_keys, cosine, sine)
        grad_mixed = jnp.concatenate(
            [
                grad_queries.reshape(seq_length, -1).astype(BF16),
                grad_keys.reshape(seq_length, -1).astype(BF16),
                grad_values.reshape(seq_length, -1).astype(BF16),
            ],
            axis=1,
        )
        grad_mixed = jnp.concatenate(split_two(matmul_left_t(onehot_low, grad_mixed)), axis=0)
        grad_normed_first = (
            matmul_right_t(grad_mixed[:, :q_width], w_query)
            + matmul_right_t(grad_mixed[:, q_width : q_width + k_width], w_key)
            + matmul_right_t(grad_mixed[:, q_width + k_width :], w_value)
        )
        grad_normed_first = grad_normed_first[:group_entries] + grad_normed_first[group_entries:]
        grad_entries = rms_back(
            embeds_wide, inverse_first, grad_normed_first * gain_first
        ) + matmul_left_t(onehot_share, grad_hidden_low)
        grad_entries = grad_entries.astype(BF16).reshape(2, 2, own_entries, lm_width)
        grad_embeds.append(
            scatter_tensor(half(grad_entries, chip), half(grad_entries, 1 - chip), core).astype(BF16)
        )

    grad_embeds = jnp.concatenate(grad_embeds, axis=0)
    grad_projection = matmul_left_t(pooled_norm, grad_embeds)
    grad_pooled_norm = matmul_right_t(grad_embeds, proj)
    grad_gain_final = jnp.sum(grad_pooled_norm * normed_final, axis=0)
    grad_bias_final = jnp.sum(grad_pooled_norm, axis=0)
    grad_pooled = norm_back(normed_final, inverse_final, grad_pooled_norm * final_gain)
    grad_rows = jnp.concatenate(
        [
            grad_pooled[:, None, :],
            jnp.zeros((micro_count * own_entries, slot_count - 1, width), F32),
        ],
        axis=1,
    ).reshape(own_rows, width)
    layer_grads = [None] * layer_count
    for layer in range(layer_count - 1, -1, -1):
        grad_rows, layer_grads[layer] = hyper_backward(grad_rows, saved[layer], layer_weights[layer])

    pieces = grad_rows.astype(BF16).reshape(own_rows, tensor_size, table_cols).transpose(1, 0, 2)
    arrived = lax.all_to_all(pieces, "tensor", split_axis=0, concat_axis=0, tiled=True)
    arrived = gather_dp(arrived).reshape(-1, table_cols)
    table_grad = collect(ids_all, arrived, table_rows)

    def rows_of(values):
        return values.astype(BF16).reshape(devices, -1, values.shape[-1])

    pieces = []
    for layer in range(layer_count):
        grads = layer_grads[layer]
        pieces += [rows_of(grads[2][:, i * width : (i + 1) * width]) for i in range(3)]
        pieces += [rows_of(grads[5])]
        pieces += [rows_of(grads[9][:, i * width : (i + 1) * width]) for i in range(4)]
        pieces += [rows_of(grads[11])]
    pieces += [rows_of(grad_projection[:, i * width : (i + 1) * width]) for i in range(4)]
    small = [layer_grads[layer][i] for i in (0, 1, 3, 4, 6, 7, 8, 12) for layer in range(layer_count)]
    small = jnp.stack(small + [grad_gain_final, grad_bias_final])
    small = small.reshape(-1, devices, own).transpose(1, 0, 2).reshape(devices, -1)
    inner_small = jnp.stack([layer_grads[layer][10] for layer in range(layer_count)])
    inner_small = inner_small.reshape(layer_count, devices, -1).transpose(1, 0, 2)
    small = jnp.concatenate([small, inner_small.reshape(devices, -1)], axis=1).astype(BF16)
    small = jnp.pad(small, ((0, 0), (0, 16 * width - small.shape[1])))
    pieces += [small.reshape(devices, 16, width)]
    reduced = lax.psum_scatter(
        jnp.concatenate(pieces, axis=1), BOTH, scatter_dimension=0, tiled=True
    )[0]
    reduced = reduced.astype(F32)
    at = 0
    outs = {"qkv": [], "attn_out": [], "inner": [], "outer": []}
    for layer in range(layer_count):
        for name, count, rows in (("qkv", 3, own), ("attn_out", 1, own), ("inner", 4, own), ("outer", 1, 4 * own)):
            outs[name].append(
                jnp.concatenate([reduced[at + i * rows : at + (i + 1) * rows] for i in range(count)], axis=1)
            )
            at += count * rows
    out_proj = jnp.concatenate([reduced[at + i * own : at + (i + 1) * own] for i in range(4)], axis=1)
    at += 4 * own
    small = reduced[at : at + 16].reshape(-1)
    count = VECTORS * layer_count
    vec = small[: count * own].reshape(VECTORS, layer_count, own)
    out_final_gain = small[count * own : (count + 1) * own]
    out_final_bias = small[(count + 1) * own : (count + 2) * own]
    out_inner_bias = small[(count + 2) * own : (count + 2 + 4 * layer_count) * own].reshape(layer_count, 4 * own)
    stacked = {name: jnp.stack(value) for name, value in outs.items()}
    return (
        jnp.stack(out_parts),
        table_grad,
        vec[0],
        vec[1],
        stacked["qkv"],
        vec[2],
        vec[3],
        stacked["attn_out"],
        vec[4],
        vec[5],
        vec[6],
        stacked["inner"],
        out_inner_bias,
        stacked["outer"],
        vec[7],
        out_final_gain,
        out_final_bias,
        out_proj,
    )


def solution(mesh):
    return jax.shard_map(
        local,
        mesh=mesh,
        in_specs=(
            P("dp", "tensor"),
            P(None, "dp", None),
            P(None, "dp"),
            P(None, "dp"),
            P(None, ("dp", "tensor"), None),
            P(),
            P(None, "tensor"),
            P(None, "tensor"),
            P(None, "tensor"),
            P("tensor", None),
            P(),
            P(None, "tensor"),
            P(None, "tensor"),
            P("tensor", None),
            P(None, ("dp", "tensor")),
            P(None, ("dp", "tensor")),
            P(None, ("dp", "tensor"), None),
            P(None, ("dp", "tensor")),
            P(None, ("dp", "tensor")),
            P(None, ("dp", "tensor"), None),
            P(None, ("dp", "tensor")),
            P(None, ("dp", "tensor")),
            P(None, ("dp", "tensor")),
            P(None, ("dp", "tensor"), None),
            P(None, ("dp", "tensor")),
            P(None, ("dp", "tensor"), None),
            P(None, ("dp", "tensor")),
            P(("dp", "tensor")),
            P(("dp", "tensor")),
            P(("dp", "tensor"), None),
        ),
        out_specs=(
            P(None, ("dp", "tensor"), None),
            P("dp", "tensor"),
            P(None, ("dp", "tensor")),
            P(None, ("dp", "tensor")),
            P(None, ("dp", "tensor"), None),
            P(None, ("dp", "tensor")),
            P(None, ("dp", "tensor")),
            P(None, ("dp", "tensor"), None),
            P(None, ("dp", "tensor")),
            P(None, ("dp", "tensor")),
            P(None, ("dp", "tensor")),
            P(None, ("dp", "tensor"), None),
            P(None, ("dp", "tensor")),
            P(None, ("dp", "tensor"), None),
            P(None, ("dp", "tensor")),
            P(("dp", "tensor")),
            P(("dp", "tensor")),
            P(("dp", "tensor"), None),
        ),
        check_vma=False,
    )
```

```python
import jax
import jax.numpy as jnp
from jax import lax
from jax.experimental import pallas as pl
from jax.experimental.pallas import tpu as pltpu
from jax.sharding import PartitionSpec as P

HEAD_DIM = 64
EPS_NORM = 1e-05
HIGH = lax.Precision.HIGHEST
SQRT_HALF = 0.7071067811865476
INV_SQRT_TAU = 0.3989422804014327
BOTH = ("dp", "tensor")
F32 = jnp.float32
BF16 = jnp.bfloat16


def matmul(left, right):
    return jnp.dot(left, right, preferred_element_type=F32)


def matmul_right_t(left, right):
    return lax.dot_general(left, right, (((1,), (1,)), ((), ())), preferred_element_type=F32)


def matmul_left_t(left, right):
    return lax.dot_general(left, right, (((0,), (0,)), ((), ())), preferred_element_type=F32)


def norm_parts(values):
    centered = values - jnp.mean(values, axis=-1, keepdims=True)
    inverse = lax.rsqrt(jnp.mean(centered * centered, axis=-1, keepdims=True) + EPS_NORM)
    return (centered * inverse, inverse)


def norm_back(normed, inverse, grad_scaled):
    return inverse * (
        grad_scaled
        - jnp.mean(grad_scaled, axis=-1, keepdims=True)
        - normed * jnp.mean(grad_scaled * normed, axis=-1, keepdims=True)
    )


def rms_parts(values):
    return lax.rsqrt(jnp.mean(values * values, axis=-1, keepdims=True) + EPS_NORM)


def rms_back(values, inverse, grad_scaled):
    return inverse * grad_scaled - values * inverse**3 * jnp.mean(
        grad_scaled * values, axis=-1, keepdims=True
    )


def rotary_tables(seq_length):
    half_dim = HEAD_DIM // 2
    freqs = 10000.0 ** (-jnp.arange(half_dim, dtype=F32) * 2.0 / HEAD_DIM)
    angles = jnp.arange(seq_length, dtype=F32)[:, None] * freqs[None, :]
    angles = jnp.concatenate([angles, angles], axis=-1)
    return (jnp.cos(angles), jnp.sin(angles))


def swap(values, axis, bit):
    size = lax.axis_size(axis)
    return lax.ppermute(values, axis, [(i, i ^ bit) for i in range(size)])


def lookup_kernel(ids_ref, table_ref, out_ref):
    rows = ids_ref.shape[0]
    height = table_ref.shape[0]
    places = lax.broadcasted_iota(jnp.int32, (rows, height), 1)
    chosen = jnp.where(ids_ref[...] == places, 1.0, 0.0).astype(BF16)
    out_ref[...] = matmul(chosen, table_ref[...]).astype(BF16)


def lookup(ids, table):
    count = ids.shape[0]
    height, width = table.shape
    rows = 512
    return pl.pallas_call(
        lookup_kernel,
        grid=(count // rows,),
        in_specs=[
            pl.BlockSpec((rows, 1), lambda i: (i, 0)),
            pl.BlockSpec((height, width), lambda i: (0, 0)),
        ],
        out_specs=pl.BlockSpec((rows, width), lambda i: (i, 0)),
        out_shape=jax.ShapeDtypeStruct((count, width), BF16),
        compiler_params=pltpu.CompilerParams(vmem_limit_bytes=48 << 20),
        cost_estimate=pl.CostEstimate(
            flops=4 * count * height * width, bytes_accessed=4 * count * width, transcendentals=0
        ),
        name="lookup",
    )(ids[:, None], table)


def collect_kernel(ids_ref, rows_ref, base_ref, out_ref):
    @pl.when(pl.program_id(0) == 0)
    def _():
        out_ref[...] = jnp.zeros_like(out_ref) if base_ref is None else base_ref[...]

    height = out_ref.shape[0]
    places = lax.broadcasted_iota(jnp.int32, (height, ids_ref.shape[1]), 0)
    chosen = jnp.where(ids_ref[...] == places, 1.0, 0.0).astype(BF16)
    out_ref[...] += matmul(chosen, rows_ref[...])


def collect(ids, values, height, base):
    count, width = values.shape
    rows = 512
    whole = pl.BlockSpec((height, width), lambda i: (0, 0))
    kernel = collect_kernel
    if base is None:
        kernel = lambda ids_ref, rows_ref, out_ref: collect_kernel(ids_ref, rows_ref, None, out_ref)
    return pl.pallas_call(
        kernel,
        grid=(count // rows,),
        in_specs=[
            pl.BlockSpec((1, rows), lambda i: (0, i)),
            pl.BlockSpec((rows, width), lambda i: (i, 0)),
        ]
        + ([] if base is None else [whole]),
        out_specs=whole,
        out_shape=jax.ShapeDtypeStruct((height, width), F32),
        compiler_params=pltpu.CompilerParams(vmem_limit_bytes=48 << 20),
        cost_estimate=pl.CostEstimate(
            flops=4 * count * height * width, bytes_accessed=4 * count * width, transcendentals=0
        ),
        name="collect",
    )(ids[None, :], values, *([] if base is None else [base]))


QUERY_ROWS = 256
ENTRY_LANES = 64
VMEM_LIMIT = 56 << 20


def turn_rows(values):
    half_dim = HEAD_DIM // 2
    return jnp.concatenate([-values[half_dim:], values[:half_dim]], axis=0)


def two_parts(values):
    high = values.astype(BF16)
    return jnp.concatenate([high, (values - high.astype(F32)).astype(BF16)], axis=1)


def entry_table(columns):
    return two_parts(jnp.concatenate([columns, turn_rows(columns)], axis=0))


def spread(table, onehot, trig):
    both = matmul(table, onehot) * trig
    return both[:HEAD_DIM] + both[HEAD_DIM:]


def ahead_mask(rows):
    shape = (rows, rows)
    return lax.broadcasted_iota(jnp.int32, shape, 0) <= lax.broadcasted_iota(jnp.int32, shape, 1)


def attend_kernel(
    place, part0, part1, part2, part3, gain, w_query, w_kv, ids, trig, _after_one, _after_two,
    near, far, context_t, log_total, table_q, table_kv, embeds,
    normed, onehot, keys, values_t,
):
    tokens = ids.shape[1]

    @pl.when(pl.program_id(0) == 0)
    def _():
        own = part0.shape[1]
        for k, part in enumerate((part0, part1, part2, part3)):
            embeds[k * own : (k + 1) * own, :] = part[0]
        wide = embeds[...].astype(F32)
        normed[...] = (wide * rms_parts(wide) * gain[...].astype(F32)).astype(BF16)
        places = lax.broadcasted_iota(jnp.int32, onehot.shape, 0)
        places = jnp.where(places >= ENTRY_LANES, places - ENTRY_LANES, places)
        onehot[...] = jnp.where(places == ids[...], 1.0, 0.0).astype(BF16)
        mixed = matmul(normed[...], w_kv[...]).T
        table_kv[0] = entry_table(mixed[:HEAD_DIM])
        table_kv[1] = entry_table(mixed[HEAD_DIM:])
        keys[...] = spread(table_kv[0], onehot[...], trig[...]).T.astype(BF16)
        values_t[...] = matmul(table_kv[1], onehot[...])[:HEAD_DIM].astype(BF16)

    queries = matmul(normed[...], w_query[...]).T * HEAD_DIM ** (-0.5)
    ahead = ahead_mask(QUERY_ROWS)
    turned = []
    for j in range(2):
        table_q[0, j] = entry_table(queries[j * HEAD_DIM : (j + 1) * HEAD_DIM])
        turned.append(spread(table_q[0, j], onehot[...], trig[...]).astype(BF16))
    odd = place[0] % 2
    rows_out = []
    for block in range(tokens // QUERY_ROWS):
        start, stop = block * QUERY_ROWS, (block + 1) * QUERY_ROWS
        done = []
        for j in range(2):
            scores = matmul(keys[:stop], turned[j][:, start:stop])
            last = jnp.where(ahead, scores[start:], -1e30)
            highest = jnp.max(last, axis=0, keepdims=True)
            if block:
                highest = jnp.maximum(highest, jnp.max(scores[:start], axis=0, keepdims=True))
            last = jnp.exp(last - highest)
            total = jnp.sum(last, axis=0, keepdims=True)
            summed = matmul(values_t[:, start:stop], last.astype(BF16))
            if block:
                first = jnp.exp(scores[:start] - highest)
                total = total + jnp.sum(first, axis=0, keepdims=True)
                summed = summed + matmul(values_t[:, :start], first.astype(BF16))
            done.append(summed / total)
            log_total[0, j : j + 1, start:stop] = highest + jnp.log(total)
        done = jnp.concatenate(done, axis=0)
        context_t[:, start:stop] = done.astype(BF16)
        rows_out.append(done.T.astype(BF16))
        if block % 2:
            even_rows, odd_rows = rows_out[-2:]
            target = (block // 2) ^ (place[0] // 2)
            near[target] = jnp.where(odd == 0, even_rows, odd_rows)
            far[target] = jnp.where(odd == 0, odd_rows, even_rows)


def attend(place, micro, parts, gain, w_query, w_kv, ids, trig, after):
    assert ids.shape[1] == 4 * QUERY_ROWS
    _, own, width = parts[0].shape
    entries = own * len(parts)
    tokens = ids.shape[1]
    pairs = w_query.shape[1] // (2 * HEAD_DIM)
    lanes = 2 * HEAD_DIM
    whole = lambda *shape: pl.BlockSpec(shape, lambda i: (0,) * len(shape))
    return pl.pallas_call(
        attend_kernel,
        grid=(pairs,),
        in_specs=[pl.BlockSpec(memory_space=pltpu.SMEM)]
        + [pl.BlockSpec((1, own, width), lambda i: (micro, 0, 0))] * len(parts)
        + [
            whole(1, width),
            pl.BlockSpec((width, lanes), lambda i: (0, i)),
            whole(width, lanes),
            whole(1, tokens),
            whole(lanes, tokens),
        ]
        + [pl.BlockSpec(memory_space=pl.ANY)] * 2,
        out_specs=[
            pl.BlockSpec((2, QUERY_ROWS, lanes), lambda i: (0, 0, i)),
            pl.BlockSpec((2, QUERY_ROWS, lanes), lambda i: (0, 0, i)),
            pl.BlockSpec((lanes, tokens), lambda i: (i, 0)),
            pl.BlockSpec((1, 2, tokens), lambda i: (i, 0, 0)),
            pl.BlockSpec((1, 2, lanes, lanes), lambda i: (i, 0, 0, 0)),
            whole(2, lanes, lanes),
            whole(entries, width),
        ],
        out_shape=[
            jax.ShapeDtypeStruct((2, QUERY_ROWS, pairs * lanes), BF16),
            jax.ShapeDtypeStruct((2, QUERY_ROWS, pairs * lanes), BF16),
            jax.ShapeDtypeStruct((pairs * lanes, tokens), BF16),
            jax.ShapeDtypeStruct((pairs, 2, tokens), F32),
            jax.ShapeDtypeStruct((pairs, 2, lanes, lanes), BF16),
            jax.ShapeDtypeStruct((2, lanes, lanes), BF16),
            jax.ShapeDtypeStruct((entries, width), BF16),
        ],
        scratch_shapes=[
            pltpu.VMEM((entries, width), BF16),
            pltpu.VMEM((lanes, tokens), BF16),
            pltpu.VMEM((tokens, HEAD_DIM), BF16),
            pltpu.VMEM((HEAD_DIM, tokens), BF16),
        ],
        compiler_params=pltpu.CompilerParams(vmem_limit_bytes=VMEM_LIMIT),
        cost_estimate=pl.CostEstimate(
            flops=12 * 10**9, bytes_accessed=8 * 10**6, transcendentals=5 * 10**6
        ),
        name="attend",
    )(place, *parts, gain, w_query, w_kv, ids, trig, *after)


def attend_back_kernel(
    place, part0, part1, part2, part3, context_t, log_total, table_q, table_kv, ids, ids_share, trig,
    w_query, w_kv, embeds, gain, grad_hidden, _after_one, _after_two, _after_three, grad_entries,
    onehot, columns, keys, keys_t, values, grad_keys, grad_values, total, grad_context,
):
    tokens = ids.shape[1]
    share = part0.shape[0]
    for k, part in enumerate((part0, part1, part2, part3)):
        first = pl.multiple_of((place[0] ^ k) * share, share)
        grad_context[pl.ds(first, share), :] = part[...]
    entries = embeds.shape[0]
    cosine, sine = trig[:HEAD_DIM], trig[HEAD_DIM:]

    @pl.when(pl.program_id(0) == 0)
    def _():
        places = lax.broadcasted_iota(jnp.int32, onehot.shape, 0)
        places = jnp.where(places >= ENTRY_LANES, places - ENTRY_LANES, places)
        chosen = jnp.where(places == ids[...], 1.0, 0.0)
        onehot[...] = chosen.astype(BF16)
        columns[...] = chosen.T.astype(BF16)
        turned = spread(table_kv[0], onehot[...], trig[...])
        keys_t[...] = turned.astype(BF16)
        keys[...] = turned.T.astype(BF16)
        values[...] = matmul(table_kv[1], onehot[...])[:HEAD_DIM].T.astype(BF16)
        grad_keys[...] = jnp.zeros_like(grad_keys)
        grad_values[...] = jnp.zeros_like(grad_values)
        total[...] = jnp.zeros_like(total)

    def to_entries(grads, cos_part, sin_part, rows):
        straight = matmul((grads * cos_part).astype(BF16), rows)
        crossed = matmul((grads * sin_part).astype(BF16), rows)
        return straight, crossed

    def two_stacked(grads):
        high = grads.astype(BF16)
        rest = (grads - high.astype(F32)).astype(BF16)
        lane = lax.broadcasted_iota(jnp.int32, grads.shape, 1)
        return jnp.where(lane < ENTRY_LANES, high.astype(F32), rest.astype(F32)).T.astype(BF16)

    ahead = ahead_mask(QUERY_ROWS)
    grad_t = grad_context[...].astype(F32).T
    products = grad_t * context_t[...].astype(F32)
    grad_t = grad_t.astype(BF16)
    per_head = []
    for j in range(2):
        head = slice(j * HEAD_DIM, (j + 1) * HEAD_DIM)
        turned = spread(table_q[0, j], onehot[...], trig[...])
        queries_t = turned.astype(BF16)
        queries = turned.T.astype(BF16)
        offset = jnp.sum(products[head], axis=0, keepdims=True)
        straight = jnp.zeros((HEAD_DIM, columns.shape[1]), F32)
        crossed = jnp.zeros((HEAD_DIM, columns.shape[1]), F32)
        for block in range(tokens // QUERY_ROWS):
            start, stop = block * QUERY_ROWS, (block + 1) * QUERY_ROWS
            scores = matmul(keys[:stop], queries_t[:, start:stop])
            soft = jnp.exp(scores - log_total[0, j : j + 1, start:stop])
            last = jnp.where(ahead, soft[start:], 0.0)
            soft = jnp.concatenate([soft[:start], last], axis=0) if block else last
            grad_soft = matmul(values[:stop], grad_t[head, start:stop])
            grad_scores = (soft * (grad_soft - offset[:, start:stop])).astype(BF16)
            grad_values[:stop] += matmul(soft.astype(BF16), grad_context[start:stop, head])
            grad_keys[:stop] += matmul(grad_scores, queries[start:stop])
            grad_queries = matmul(keys_t[:, :stop], grad_scores) * HEAD_DIM ** (-0.5)
            parts = to_entries(
                grad_queries, cosine[:, start:stop], sine[:, start:stop], columns[start:stop]
            )
            straight, crossed = straight + parts[0], crossed + parts[1]
        per_head.append(straight - turn_rows(crossed))
    total[...] += matmul_right_t(two_stacked(jnp.concatenate(per_head, axis=0)), w_query[...])

    @pl.when(pl.program_id(0) == pl.num_programs(0) - 1)
    def _():
        grads = jnp.concatenate([grad_keys[...], grad_values[...]], axis=1).T
        straight, crossed = to_entries(grads[:HEAD_DIM], cosine, sine, columns[...])
        summed = matmul(grads[HEAD_DIM:].astype(BF16), columns[...])
        both = jnp.concatenate([straight - turn_rows(crossed), summed], axis=0)
        full = total[...] + matmul_right_t(two_stacked(both), w_kv[...])
        scaled = (full[:entries] + full[entries:]) * gain[...].astype(F32)
        wide = embeds[...].astype(F32)
        places = lax.broadcasted_iota(jnp.int32, (entries, ids_share.shape[1]), 0)
        own = jnp.where(places == ids_share[...], 1.0, 0.0).astype(BF16)
        result = rms_back(wide, rms_parts(wide), scaled) + matmul(own, grad_hidden[...])
        grad_entries[...] = result.astype(BF16)


def attend_back(
    place, parts, kept, ids, ids_share, trig, w_query, w_kv, gain, grad_hidden, after
):
    context_t, log_total, table_q, table_kv, embeds = kept
    share = parts[0].shape[0]
    entries, width = embeds.shape
    tokens = ids.shape[1]
    pairs = w_query.shape[1] // (2 * HEAD_DIM)
    lanes = 2 * HEAD_DIM
    whole = lambda *shape: pl.BlockSpec(shape, lambda i: (0,) * len(shape))
    return pl.pallas_call(
        attend_back_kernel,
        grid=(pairs,),
        in_specs=[pl.BlockSpec(memory_space=pltpu.SMEM)]
        + [pl.BlockSpec((share, lanes), lambda i: (0, i))] * len(parts)
        + [
            pl.BlockSpec((lanes, tokens), lambda i: (i, 0)),
            pl.BlockSpec((1, 2, tokens), lambda i: (i, 0, 0)),
            pl.BlockSpec((1, 2, lanes, lanes), lambda i: (i, 0, 0, 0)),
            whole(2, lanes, lanes),
            whole(1, tokens),
            whole(*ids_share.shape),
            whole(lanes, tokens),
            pl.BlockSpec((width, lanes), lambda i: (0, i)),
            whole(width, lanes),
            whole(entries, width),
            whole(1, width),
            whole(*grad_hidden.shape),
        ]
        + [pl.BlockSpec(memory_space=pl.ANY)] * 3,
        out_specs=whole(entries, width),
        out_shape=jax.ShapeDtypeStruct((entries, width), BF16),
        scratch_shapes=[
            pltpu.VMEM((lanes, tokens), BF16),
            pltpu.VMEM((tokens, lanes), BF16),
            pltpu.VMEM((tokens, HEAD_DIM), BF16),
            pltpu.VMEM((HEAD_DIM, tokens), BF16),
            pltpu.VMEM((tokens, HEAD_DIM), BF16),
            pltpu.VMEM((tokens, HEAD_DIM), F32),
            pltpu.VMEM((tokens, HEAD_DIM), F32),
            pltpu.VMEM((2 * entries, width), F32),
            pltpu.VMEM((tokens, lanes), BF16),
        ],
        compiler_params=pltpu.CompilerParams(vmem_limit_bytes=VMEM_LIMIT),
        cost_estimate=pl.CostEstimate(
            flops=25 * 10**9, bytes_accessed=8 * 10**6, transcendentals=5 * 10**6
        ),
        name="attend_back",
    )(
        place, *parts, context_t, log_total, table_q, table_kv, ids, ids_share, trig,
        w_query, w_kv, embeds, gain, grad_hidden, *after,
    )


ANY_SPEC = pl.BlockSpec(memory_space=pl.ANY)


def pick_rows(ids, entries):
    places = lax.broadcasted_iota(jnp.int32, (entries, ids.shape[1]), 0)
    return jnp.where(places == ids[...], 1.0, 0.0).astype(BF16)


def hidden_kernel(
    embeds, ids_own, ids_peer, gain, c0, c1, c2, c3, w0, w1, w2, w3, _after_one, _after_two,
    normed_own, normed_peer, hidden,
):
    share = normed_own.shape[0]
    for own, ids, normed in ((False, ids_peer, normed_peer), (True, ids_own, normed_own)):
        total = matmul_left_t(pick_rows(ids, embeds.shape[0]), embeds[...])
        for k, (part, weight) in enumerate(((c0, w0), (c1, w1), (c2, w2), (c3, w3))):
            total = total + matmul(part[int(own == (k >= 2))], weight[...])
        normed[...] = (total * rms_parts(total) * gain[...].astype(F32)).astype(BF16)
        if own:
            hidden[...] = total


def hidden_rows_of(embeds, ids_own, ids_peer, gain, parts, weights, after):
    rows, width = ids_own.shape[1], embeds.shape[1]
    vmem = pl.BlockSpec(memory_space=pltpu.VMEM)
    return pl.pallas_call(
        hidden_kernel,
        in_specs=[vmem] * 12 + [ANY_SPEC] * 2,
        out_specs=[vmem] * 3,
        out_shape=[
            jax.ShapeDtypeStruct((rows, width), BF16),
            jax.ShapeDtypeStruct((rows, width), BF16),
            jax.ShapeDtypeStruct((rows, width), F32),
        ],
        compiler_params=pltpu.CompilerParams(vmem_limit_bytes=VMEM_LIMIT),
        cost_estimate=pl.CostEstimate(
            flops=6 * 10**9, bytes_accessed=18 * 10**6, transcendentals=0
        ),
        name="hidden",
    )(embeds, ids_own, ids_peer, gain, *parts, *weights, *after)


def hidden_back_kernel(
    cotangent, hidden, kept, from_core, from_chip, gain, w0, w1, w2, w3,
    low, p0, p1, p2, p3,
):
    grads = kept[...].astype(F32) + from_core[...].astype(F32) + from_chip[...].astype(F32)
    rows = hidden[...]
    scaled = grads * gain[...].astype(F32)
    total = cotangent[0] + rms_back(rows, rms_parts(rows), scaled)
    total = total.astype(BF16)
    low[...] = total
    for part, weight in ((p2, w2), (p3, w3), (p1, w1), (p0, w0)):
        part[...] = matmul_right_t(total, weight[...]).astype(BF16)


def hidden_back(micro, cotangent, hidden, kept, from_core, from_chip, gain, weights):
    rows, width = hidden.shape
    heads = weights[0].shape[0]
    whole = lambda *shape: pl.BlockSpec(shape, lambda i: (0,) * len(shape))
    return pl.pallas_call(
        hidden_back_kernel,
        grid=(1,),
        in_specs=[pl.BlockSpec((1, rows, width), lambda i: (micro, 0, 0))]
        + [whole(rows, width)] * 4
        + [whole(1, width)]
        + [whole(heads, width)] * 4,
        out_specs=[whole(rows, width)] + [whole(rows, heads)] * 4,
        out_shape=[jax.ShapeDtypeStruct((rows, width), BF16)]
        + [jax.ShapeDtypeStruct((rows, heads), BF16)] * 4,
        compiler_params=pltpu.CompilerParams(vmem_limit_bytes=VMEM_LIMIT),
        cost_estimate=pl.CostEstimate(
            flops=2 * 10**9, bytes_accessed=16 * 10**6, transcendentals=0
        ),
        name="hidden_back",
    )(cotangent, hidden, kept, from_core, from_chip, gain, *weights)


def mlp_kernel(
    x_mine, x_other, grad_mine_in, grad_other_in, gate_hbm, up_hbm, down_hbm, _after_one, _after_two, _after_three,
    out_mine, out_other, grad_mine, grad_other,
    w_gate, w_up, w_down, sems,
):
    copies = [
        pltpu.make_async_copy(source, target, sems.at[i])
        for i, (source, target) in enumerate(
            ((gate_hbm, w_gate), (up_hbm, w_up), (down_hbm, w_down))
        )
    ]
    for copy in copies:
        copy.start()
    for first, (rows, cots, out, grad) in enumerate(
        ((x_other, grad_other_in, out_other, grad_other), (x_mine, grad_mine_in, out_mine, grad_mine))
    ):
        if first == 0:
            copies[0].wait()
        gate = matmul(rows[...], w_gate[...])
        if first == 0:
            copies[1].wait()
        upward = matmul(rows[...], w_up[...])
        if first == 0:
            copies[2].wait()
        grad_active = matmul_right_t(cots[...], w_down[...])
        sigmoid = 1.0 / (1.0 + jnp.exp(-gate))
        silu = gate * sigmoid
        activated = (silu * upward).astype(BF16)
        grad_gate = grad_active * upward * (sigmoid * (1.0 + gate * (1.0 - sigmoid)))
        grad_up = (grad_active * silu).astype(BF16)
        out[...] = matmul(activated, w_down[...]).astype(BF16)
        total = matmul_right_t(grad_gate.astype(BF16), w_gate[...])
        grad[...] = (total + matmul_right_t(grad_up, w_up[...])).astype(BF16)


def mlp(x_mine, x_other, cot_mine, cot_other, w_gate, w_up, w_down, after):
    rows, width = x_mine.shape
    units = w_gate.shape[1]
    vmem = pl.BlockSpec(memory_space=pltpu.VMEM)
    return pl.pallas_call(
        mlp_kernel,
        in_specs=[vmem] * 4 + [ANY_SPEC] * 6,
        out_specs=[vmem] * 4,
        out_shape=[jax.ShapeDtypeStruct((rows, width), BF16)] * 4,
        scratch_shapes=[
            pltpu.VMEM((width, units), BF16),
            pltpu.VMEM((width, units), BF16),
            pltpu.VMEM((units, width), BF16),
            pltpu.SemaphoreType.DMA((3,)),
        ],
        compiler_params=pltpu.CompilerParams(vmem_limit_bytes=VMEM_LIMIT),
        cost_estimate=pl.CostEstimate(
            flops=24 * rows * width * units, bytes_accessed=26 * 10**6, transcendentals=2 * rows * units
        ),
        name="mlp",
    )(x_mine, x_other, cot_mine, cot_other, w_gate, w_up, w_down, *after)


def add_kernel(left, right, _after, out):
    out[...] = (left[...].astype(F32) + right[...].astype(F32)).astype(BF16)


def add_after(left, right, after):
    vmem = pl.BlockSpec(memory_space=pltpu.VMEM)
    return pl.pallas_call(
        add_kernel,
        in_specs=[vmem, vmem, ANY_SPEC],
        out_specs=vmem,
        out_shape=jax.ShapeDtypeStruct(left.shape, BF16),
        name="add_after",
    )(left, right, after)


def cast_kernel(values, _after, out):
    out[...] = values[0].astype(BF16)


def cast_after(micro, values, after):
    _, rows, width = values.shape
    return pl.pallas_call(
        cast_kernel,
        grid=(1,),
        in_specs=[pl.BlockSpec((1, rows, width), lambda i: (micro, 0, 0)), ANY_SPEC],
        out_specs=pl.BlockSpec((rows, width), lambda i: (0, 0)),
        out_shape=jax.ShapeDtypeStruct((rows, width), BF16),
        name="cast_after",
    )(values, after)


BLOCKS = 32
UNIT = 16
LAYER_UNITS = 12
VECTORS = 8


def square(ref):
    blocks, rows, width = ref.shape
    return ref[...].reshape(blocks * rows, width)


def entry_bias(valid, rows, slots):
    shape = (rows, rows)
    same = lax.broadcasted_iota(jnp.int32, shape, 0) // slots == lax.broadcasted_iota(
        jnp.int32, shape, 1
    ) // slots
    return jnp.where(jnp.logical_and(same, valid > 0.5), 0.0, -1e30)


def entry_soft(queries, keys, bias):
    scores = matmul_right_t(queries, keys) * HEAD_DIM ** (-0.5) + bias
    expon = jnp.exp(scores - jnp.max(scores, axis=1, keepdims=True))
    return expon / jnp.sum(expon, axis=1, keepdims=True)


def bell(values):
    return 0.5 * (1.0 + lax.erf(values * SQRT_HALF))


def hyper_kernel(
    slots, place, _after, part0, part1, part2, part3, valid, vectors, inner_bias, outer, w_q, w_k, w_v, w_o, in0, in1, in2, in3,
    pr0, pr1, pr2, pr3,
    below, mixed, context, middle, inner, pooled, pooled_norm, embeds,
    state, joined,
):
    layer = pl.program_id(0)
    layers = pl.num_programs(0)
    rows, width = state.shape

    @pl.when(layer == 0)
    def _():
        columns = part0.shape[1]
        for k, part in enumerate((part0, part1, part2, part3)):
            at = pl.multiple_of((place[0] ^ k) * columns, columns)
            state[:, pl.ds(at, columns)] = part[...].astype(F32)

    def vector(index):
        return vectors[pl.ds(index * layers + layer, 1), :]

    hidden = state[...]
    below[0] = hidden
    normed, _ = norm_parts(hidden)
    normed_in = (normed * vector(0) + vector(1)).astype(BF16)
    queries = (matmul(normed_in, square(w_q)) + vector(2)).astype(BF16)
    keys = matmul(normed_in, square(w_k)).astype(BF16)
    values = (matmul(normed_in, square(w_v)) + vector(3)).astype(BF16)
    mixed[0, :, :width] = queries
    mixed[0, :, width : 2 * width] = keys
    mixed[0, :, 2 * width :] = values
    bias = entry_bias(valid[...], rows, slots)
    for head in range(width // HEAD_DIM):
        at = slice(head * HEAD_DIM, (head + 1) * HEAD_DIM)
        soft = entry_soft(queries[:, at], keys[:, at], bias)
        joined[:, at] = matmul(soft.astype(BF16), values[:, at])
    context_low = joined[...].astype(BF16)
    context[0] = context_low
    centre = hidden + matmul(context_low, square(w_o)) + vector(4)
    middle[0] = centre
    normed, _ = norm_parts(centre)
    normed_mid = (normed * vector(5) + vector(6)).astype(BF16)
    total = centre + vector(7)
    for j, piece in enumerate((in0, in1, in2, in3)):
        at = slice(j * width, (j + 1) * width)
        part = matmul(normed_mid, square(piece)) + inner_bias[pl.ds(layer, 1), at]
        inner[0, :, at] = part
        activated = (part * bell(part)).astype(BF16)
        blocks = BLOCKS // 4
        total = total + matmul(
            activated, outer[j * blocks : (j + 1) * blocks].reshape(width, width)
        )
    state[...] = total

    @pl.when(layer == layers - 1)
    def _():
        slot = lax.broadcasted_iota(jnp.int32, (rows, width), 0) % slots
        first = jnp.where(slot == 0, total, 0.0).reshape(rows // slots, slots, width)
        first = jnp.sum(first, axis=1)
        pooled[...] = first
        normed, _ = norm_parts(first)
        low = (normed * vectors[VECTORS * layers : VECTORS * layers + 1, :]
               + vectors[VECTORS * layers + 1 : VECTORS * layers + 2, :]).astype(BF16)
        pooled_norm[...] = low
        for j, piece in enumerate((pr0, pr1, pr2, pr3)):
            embeds[:, j * width : (j + 1) * width] = matmul(low, square(piece)).astype(BF16)


def layer_specs(width, which):
    specs = [pl.BlockSpec((BLOCKS, 4 * UNIT, width), lambda i: (0, which(i) * LAYER_UNITS // 4, 0))]
    for j in range(4, LAYER_UNITS):
        specs.append(
            pl.BlockSpec((BLOCKS, UNIT, width), lambda i, j=j: (0, which(i) * LAYER_UNITS + j, 0))
        )
    return specs


def proj_specs(width, layers):
    return [
        pl.BlockSpec((BLOCKS, UNIT, width), lambda i, j=j: (0, layers * LAYER_UNITS + j, 0))
        for j in range(4)
    ]


def whole_spec(*shape):
    return pl.BlockSpec(shape, lambda i: (0,) * len(shape))


def hyper_forward(where, after, parts, valid, vectors, inner_bias, packed, slots):
    rows, width = parts[0].shape[0], len(parts) * parts[0].shape[1]
    layers, inner_width = inner_bias.shape
    entries = rows // slots
    by_layer = lambda *shape: pl.BlockSpec((1,) + shape, lambda i: (i,) + (0,) * len(shape))
    return pl.pallas_call(
        lambda *refs: hyper_kernel(slots, *refs),
        grid=(layers,),
        in_specs=[pl.BlockSpec(memory_space=pltpu.SMEM)]
        + [pl.BlockSpec(memory_space=pl.ANY)]
        + [whole_spec(*part.shape) for part in parts]
        + [
            whole_spec(1, rows),
            whole_spec(*vectors.shape),
            whole_spec(layers, inner_width),
        ]
        + layer_specs(width, lambda i: i)
        + proj_specs(width, layers),
        out_specs=[
            by_layer(rows, width),
            by_layer(rows, 3 * width),
            by_layer(rows, width),
            by_layer(rows, width),
            by_layer(rows, inner_width),
            whole_spec(entries, width),
            whole_spec(entries, width),
            whole_spec(entries, 4 * width),
        ],
        out_shape=[
            jax.ShapeDtypeStruct((layers, rows, width), F32),
            jax.ShapeDtypeStruct((layers, rows, 3 * width), BF16),
            jax.ShapeDtypeStruct((layers, rows, width), BF16),
            jax.ShapeDtypeStruct((layers, rows, width), F32),
            jax.ShapeDtypeStruct((layers, rows, inner_width), F32),
            jax.ShapeDtypeStruct((entries, width), F32),
            jax.ShapeDtypeStruct((entries, width), BF16),
            jax.ShapeDtypeStruct((entries, 4 * width), BF16),
        ],
        scratch_shapes=[pltpu.VMEM((rows, width), F32), pltpu.VMEM((rows, width), F32)],
        compiler_params=pltpu.CompilerParams(vmem_limit_bytes=VMEM_LIMIT),
        cost_estimate=pl.CostEstimate(
            flops=8 * 10**9, bytes_accessed=25 * 10**6, transcendentals=4 * 10**6
        ),
        name="hyper",
    )(where, after, *parts, valid, vectors, inner_bias, *([packed] * (LAYER_UNITS - 3 + 4)))


def hyper_back_kernel(
    slots, layer, layers, last,
    *refs,
):
    place, refs = refs[0], refs[1:]
    if last:
        grad_embeds, pooled, pooled_norm, pr0, pr1, pr2, pr3 = refs[:7]
        refs = refs[7:]
    else:
        grad_start = refs[0]
        refs = refs[1:]
    valid, vectors, below, mixed, context, middle, inner = refs[1:8]
    outer, w_q, w_k, w_v, w_o, in0, in1, in2, in3 = refs[8:17]
    refs = refs[17:]
    if layer == 0:
        small_above, inner_above = refs[:2]
        refs = refs[2:]
    packed = refs[:4]
    grad_below, small, inner_small, grad_mixed = refs[4:8]
    _, rows, width = below.shape
    blocks = BLOCKS // 4
    core, chip, side, line = place[0], place[1], place[2], place[3]
    half = packed[0].shape[3]

    def vector(index):
        at = index * layers + layer
        return vectors[at : at + 1, :]

    def put_rows(lines, at, rows_each, values):
        for i, z in enumerate(lines):
            for x in range(2):
                for y in range(2):
                    left, right = values[i, x, y, 0], values[i, x, y, 1]
                    mine = jnp.where(core == 0, left, right)
                    other = jnp.where(core == 0, right, left)
                    for kind, part in enumerate((mine, other)):
                        if at < half:
                            where = pl.ds(at, rows_each)
                            packed[kind][y ^ chip, x ^ side, (z - line) & 3, where, :] = part
                        else:
                            where = pl.ds(at - half, rows_each)
                            packed[2 + kind][x ^ side, y ^ chip, (z - line) & 3, where, :] = part

    def put(unit, grads):
        grads = grads.astype(BF16).reshape(4, 2, 2, 2, UNIT, width)
        put_rows(range(4), unit * UNIT, UNIT, grads)

    def column_sum(values):
        return jnp.sum(values, axis=0, keepdims=True)

    if last:
        normed, inverse = norm_parts(pooled[...])
        grad_norm = jnp.zeros(normed.shape, F32)
        for j, piece in enumerate((pr0, pr1, pr2, pr3)):
            part = grad_embeds[:, j * width : (j + 1) * width]
            put(LAYER_UNITS + j, matmul_left_t(pooled_norm[...], part))
            grad_norm = grad_norm + matmul_right_t(part, square(piece))
        small[VECTORS : VECTORS + 1, :] = column_sum(grad_norm * normed)
        small[VECTORS + 1 : VECTORS + 2, :] = column_sum(grad_norm)
        final_gain = vectors[VECTORS * layers : VECTORS * layers + 1, :]
        grad_pooled = norm_back(normed, inverse, grad_norm * final_gain)
        slot = lax.broadcasted_iota(jnp.int32, (rows, width), 0) % slots
        grad_rows = jnp.broadcast_to(grad_pooled[:, None, :], (rows // slots, slots, width))
        grad_rows = jnp.where(slot == 0, grad_rows.reshape(rows, width), 0.0)
    else:
        grad_rows = grad_start[...]

    low = grad_rows.astype(BF16)
    small[7:8, :] = column_sum(grad_rows)
    normed_two, inverse_two = norm_parts(middle[0])
    normed_mid = (normed_two * vector(5) + vector(6)).astype(BF16)
    grad_mid = jnp.zeros(grad_rows.shape, F32)
    for j, piece in enumerate((in0, in1, in2, in3)):
        at = slice(j * width, (j + 1) * width)
        part = inner[0, :, at]
        share = bell(part)
        activated = (part * share).astype(BF16)
        slope = share + part * jnp.exp(-0.5 * part * part) * INV_SQRT_TAU
        where = slice(j * blocks, (j + 1) * blocks)
        grad_outer = matmul_left_t(activated, low).astype(BF16)
        put_rows((j,), 0, 4 * UNIT, grad_outer.reshape(1, 2, 2, 2, 4 * UNIT, width))
        grad_part = matmul_right_t(low, outer[where].reshape(width, width)) * slope
        inner_small[:, at] = column_sum(grad_part)
        grad_part = grad_part.astype(BF16)
        put(8 + j, matmul_left_t(normed_mid, grad_part))
        grad_mid = grad_mid + matmul_right_t(grad_part, square(piece))
    small[5:6, :] = column_sum(grad_mid * normed_two)
    small[6:7, :] = column_sum(grad_mid)
    grad_rows = grad_rows + norm_back(normed_two, inverse_two, grad_mid * vector(5))
    small[4:5, :] = column_sum(grad_rows)
    low = grad_rows.astype(BF16)
    put(7, matmul_left_t(context[0], low))
    grad_context = matmul_right_t(low, square(w_o)).astype(BF16)
    bias = entry_bias(valid[...], rows, slots)
    for head in range(width // HEAD_DIM):
        at, key_at, value_at = (
            slice(i * width + head * HEAD_DIM, i * width + (head + 1) * HEAD_DIM) for i in range(3)
        )
        queries, keys, values = mixed[0, :, at], mixed[0, :, key_at], mixed[0, :, value_at]
        soft = entry_soft(queries, keys, bias)
        grad_head = grad_context[:, at]
        grad_soft = matmul_right_t(grad_head, values)
        offset = jnp.sum(soft * grad_soft, axis=1, keepdims=True)
        grad_scores = (soft * (grad_soft - offset) * HEAD_DIM ** (-0.5)).astype(BF16)
        grad_mixed[:, at] = matmul(grad_scores, keys)
        grad_mixed[:, key_at] = matmul_left_t(grad_scores, queries)
        grad_mixed[:, value_at] = matmul_left_t(soft.astype(BF16), grad_head)
    normed_one, inverse_one = norm_parts(below[0])
    normed_in = (normed_one * vector(0) + vector(1)).astype(BF16)
    grad_in = jnp.zeros(grad_rows.shape, F32)
    for i, piece in enumerate((w_q, w_k, w_v)):
        part = grad_mixed[:, i * width : (i + 1) * width]
        if i != 1:
            small[2 + i // 2 : 3 + i // 2, :] = column_sum(part)
        part = part.astype(BF16)
        put(4 + i, matmul_left_t(normed_in, part))
        grad_in = grad_in + matmul_right_t(part, square(piece))
    small[0:1, :] = column_sum(grad_in * normed_one)
    small[1:2, :] = column_sum(grad_in)
    grad_rows = grad_rows + norm_back(normed_one, inverse_one, grad_in * vector(0))
    if layer == 0:
        part = grad_rows.astype(BF16)
        columns = grad_below.shape[2]
        for t in range(grad_below.shape[0]):
            grad_below[t ^ (2 * chip + core)] = part[:, t * columns : (t + 1) * columns]
        wide = refs[8]
        wide[...] = jnp.zeros_like(wide)
        own = small[...]
        above = small_above[...]
        for b in range(BLOCKS):
            at = slice(b * UNIT, (b + 1) * UNIT)
            for i in range(layers):
                source = own if i == 0 else above
                wide[b, i * VECTORS : (i + 1) * VECTORS, 0:UNIT] = source[:VECTORS, at]
            wide[b, VECTORS * layers : VECTORS * layers + 2, 0:UNIT] = above[VECTORS:, at]
            at = slice(b * 4 * UNIT, (b + 1) * 4 * UNIT)
            wide[b, VECTORS * layers + 2 : VECTORS * layers + 3, 0 : 4 * UNIT] = inner_small[:, at]
            wide[b, VECTORS * layers + 3 : VECTORS * layers + 4, 0 : 4 * UNIT] = inner_above[:, at]
        base = LAYER_UNITS * UNIT
        spare = jnp.zeros((BLOCKS, 2 * UNIT, width - wide.shape[2]), F32)
        full = jnp.concatenate([wide[...], spare], axis=2).astype(BF16)
        put_rows(range(4), base, 2 * UNIT, full.reshape(4, 2, 2, 2, 2 * UNIT, width))
    else:
        grad_below[...] = grad_rows


def hyper_backward(place, layer, source, valid, vectors, kept, packed, slots, above, columns, after):
    below, mixed, context, middle, inner = kept
    layers, rows, width = below.shape
    inner_width = inner.shape[2]
    last = layer == layers - 1
    at_layer = lambda *shape: pl.BlockSpec((1,) + shape, lambda i: (layer,) + (0,) * len(shape))
    inputs, specs = [place], [pl.BlockSpec(memory_space=pltpu.SMEM)]
    if last:
        grad_embeds, pooled, pooled_norm = source
        inputs += [grad_embeds, pooled, pooled_norm] + [packed] * 4
        specs += [whole_spec(*grad_embeds.shape), whole_spec(*pooled.shape)]
        specs += [whole_spec(*pooled_norm.shape)] + proj_specs(width, layers)
    else:
        inputs += [source]
        specs += [whole_spec(rows, width)]
    inputs += [after, valid, vectors, below, mixed, context, middle, inner]
    specs += [pl.BlockSpec(memory_space=pl.ANY)]
    specs += [whole_spec(1, rows), whole_spec(*vectors.shape), at_layer(rows, width)]
    specs += [at_layer(rows, 3 * width), at_layer(rows, width), at_layer(rows, width)]
    specs += [at_layer(rows, inner_width)]
    inputs += [packed] * (LAYER_UNITS - 3)
    specs += layer_specs(width, lambda i: layer)
    scratch = [pltpu.VMEM((rows, 3 * width), F32)]
    units = LAYER_UNITS + (4 if last else 0) + (2 if layer == 0 else 0)
    below_shape = jax.ShapeDtypeStruct((rows, width), F32)
    if layer == 0:
        inputs += list(above)
        specs += [whole_spec(*part.shape) for part in above]
        below_shape = jax.ShapeDtypeStruct((width // columns, rows, columns), BF16)
        scratch.append(pltpu.VMEM((BLOCKS, 2 * UNIT, 128), F32))
    half = units // 2 * UNIT
    out_shape = [
        jax.ShapeDtypeStruct((2, 2, 4, half, width), BF16),
        jax.ShapeDtypeStruct((2, 2, 4, half, width), BF16),
        jax.ShapeDtypeStruct((2, 2, 4, units * UNIT - half, width), BF16),
        jax.ShapeDtypeStruct((2, 2, 4, units * UNIT - half, width), BF16),
        below_shape,
        jax.ShapeDtypeStruct((VECTORS + (2 if last else 0), width), F32),
        jax.ShapeDtypeStruct((1, inner_width), F32),
    ]
    return pl.pallas_call(
        lambda *refs: hyper_back_kernel(slots, layer, layers, last, *refs),
        grid=(1,),
        in_specs=specs,
        out_specs=[whole_spec(*shape.shape) for shape in out_shape],
        out_shape=out_shape,
        scratch_shapes=scratch,
        compiler_params=pltpu.CompilerParams(vmem_limit_bytes=VMEM_LIMIT),
        cost_estimate=pl.CostEstimate(
            flops=8 * 10**9, bytes_accessed=25 * 10**6, transcendentals=4 * 10**6
        ),
        name="hyper_back",
    )(*inputs)


def pack_kernel(layers, *refs):
    (g1, b1, w_qkv, bq, bv, w_ao, bao, g2, b2, w_in, b_in, w_out, bout, fg, fb, w_proj) = refs[:16]
    packed, wide = refs[16:]
    width = packed.shape[1]
    for layer in range(layers):
        base = layer * LAYER_UNITS * UNIT
        packed[base : base + 4 * UNIT] = w_out[layer]
        for j in range(3):
            at = base + (4 + j) * UNIT
            packed[at : at + UNIT] = w_qkv[layer, :, j * width : (j + 1) * width]
        packed[base + 7 * UNIT : base + 8 * UNIT] = w_ao[layer]
        for j in range(4):
            at = base + (8 + j) * UNIT
            packed[at : at + UNIT] = w_in[layer, :, j * width : (j + 1) * width]
    base = layers * LAYER_UNITS * UNIT
    for j in range(4):
        packed[base + j * UNIT : base + (j + 1) * UNIT] = w_proj[:, j * width : (j + 1) * width]
    wide[...] = jnp.zeros_like(wide)
    for j, ref in enumerate((g1, b1, bq, bv, bao, g2, b2, bout)):
        wide[j * layers : (j + 1) * layers, 0:UNIT] = ref[...].astype(F32)
    at = VECTORS * layers
    wide[at : at + 1, 0:UNIT] = fg[...].astype(F32)
    wide[at + 1 : at + 2, 0:UNIT] = fb[...].astype(F32)
    wide[at + 2 : at + 2 + layers, 0 : 4 * UNIT] = b_in[...].astype(F32)
    base = base + 4 * UNIT
    packed[base:] = jnp.zeros((2 * UNIT, width), BF16)
    packed[base:, : wide.shape[1]] = wide[...].astype(BF16)


def pack_shards(shards):
    (g1, b1, w_qkv, bq, bv, w_ao, bao, g2, b2, w_in, b_in, w_out, bout, fg, fb, w_proj) = shards
    layers, own, _ = w_qkv.shape
    width = w_ao.shape[2]
    if own == UNIT:
        inputs = list(shards)
        inputs[13], inputs[14] = fg[None], fb[None]
        return pl.pallas_call(
            lambda *refs: pack_kernel(layers, *refs),
            out_shape=jax.ShapeDtypeStruct(((layers * LAYER_UNITS + 6) * UNIT, width), BF16),
            scratch_shapes=[pltpu.VMEM((2 * UNIT, 128), F32)],
            name="pack",
        )(*inputs)
    pieces = []
    for layer in range(layers):
        pieces += [w_out[layer]]
        pieces += [w_qkv[layer, :, i * width : (i + 1) * width] for i in range(3)]
        pieces += [w_ao[layer]]
        pieces += [w_in[layer, :, i * width : (i + 1) * width] for i in range(4)]
    pieces += [w_proj[:, i * width : (i + 1) * width] for i in range(4)]
    small = [jnp.concatenate([g1, b1, bq, bv, bao, g2, b2, bout, fg[None], fb[None]]), b_in]
    small = [jnp.pad(part, ((0, 0), (0, width - part.shape[1]))) for part in small]
    small = jnp.concatenate(small)
    small = jnp.pad(small, ((0, 2 * UNIT - small.shape[0]), (0, 0)))
    return jnp.concatenate(pieces + [small])


def piece_rows(layers, own, first_layer=0, last_layer=None):
    return [4 * own] + [own] * (LAYER_UNITS - 4)


def canonical(gathered, own, layers):
    devices, _, width = gathered.shape
    count = VECTORS * layers + 2
    small = gathered[:, -2 * UNIT :]
    vectors = small[:, :count, :own].transpose(1, 0, 2).reshape(count, devices * own)
    inner_bias = small[:, count : count + layers, : 4 * own].transpose(1, 0, 2)
    inner_bias = inner_bias.reshape(layers, devices * 4 * own)
    if own != UNIT:
        pieces, at = [], 0
        for rows in piece_rows(layers, own) * layers + [own] * 4:
            part = gathered[:, at : at + rows].reshape(BLOCKS, -1, width)
            pieces.append(part)
            at += rows
        gathered = jnp.concatenate(pieces, axis=1)
    return gathered, vectors.astype(F32), inner_bias.astype(F32)


def to_devices(packed, devices, rows_list, vector_rows):
    if devices == BLOCKS:
        return packed
    width = packed.shape[2]
    split = devices // BLOCKS
    pieces, at = [], 0
    for rows in rows_list:
        pieces.append(packed[:, at : at + rows].reshape(devices, rows // split, width))
        at += rows
    if vector_rows:
        small = packed[:, at : at + vector_rows]
        narrow = small[:, : vector_rows - 14, :UNIT].reshape(BLOCKS, -1, split, UNIT // split)
        broad = small[:, vector_rows - 14 : vector_rows - 12, : 4 * UNIT]
        broad = broad.reshape(BLOCKS, -1, split, 4 * UNIT // split)
        parts = []
        for part in (narrow, broad):
            part = part.transpose(0, 2, 1, 3).reshape(devices, part.shape[1], part.shape[3])
            parts.append(jnp.pad(part, ((0, 0), (0, 0), (0, width - part.shape[2]))))
        small = jnp.concatenate(parts, axis=1)
        pieces.append(jnp.pad(small, ((0, 0), (0, vector_rows - small.shape[1]), (0, 0))))
    return jnp.concatenate(pieces, axis=1)


def unpack_kernel(layers, above, below, g_qkv, g_ao, g_in, g_out, g_proj, *vectors):
    width = above.shape[1]
    for layer, ref in ((0, below), (1, above)):
        g_out[layer] = ref[: 4 * UNIT].astype(F32)
        for j in range(3):
            at = (4 + j) * UNIT
            g_qkv[layer, :, j * width : (j + 1) * width] = ref[at : at + UNIT].astype(F32)
        g_ao[layer] = ref[7 * UNIT : 8 * UNIT].astype(F32)
        for j in range(4):
            at = (8 + j) * UNIT
            g_in[layer, :, j * width : (j + 1) * width] = ref[at : at + UNIT].astype(F32)
    base = LAYER_UNITS * UNIT
    for j in range(4):
        at = base + j * UNIT
        g_proj[:, j * width : (j + 1) * width] = above[at : at + UNIT].astype(F32)
    small = below[base : base + 2 * UNIT, :128].astype(F32)
    for j in range(VECTORS):
        for i in range(layers):
            vectors[j][i : i + 1, :] = small[i * VECTORS + j : i * VECTORS + j + 1, :UNIT]
    count = VECTORS * layers
    vectors[VECTORS][...] = small[count : count + 1, :UNIT]
    vectors[VECTORS + 1][...] = small[count + 1 : count + 2, :UNIT]
    vectors[VECTORS + 2][...] = small[count + 2 : count + 2 + layers, : 4 * UNIT]


def unpack_grads(above, below, own, layers):
    width = above.shape[1]
    count = VECTORS * layers
    if own == UNIT:
        shapes = [
            (layers, own, 3 * width),
            (layers, own, width),
            (layers, own, 4 * width),
            (layers, 4 * own, width),
            (own, 4 * width),
        ]
        shapes += [(layers, own)] * VECTORS + [(1, own), (1, own), (layers, 4 * own)]
        outs = pl.pallas_call(
            lambda *refs: unpack_kernel(layers, *refs),
            out_shape=[jax.ShapeDtypeStruct(shape, F32) for shape in shapes],
            name="unpack",
        )(above, below)
        return outs[:5], outs[5:13], outs[13][0], outs[14][0], outs[15]
    parts = []
    for ref in (below, above):
        cuts, at = [], 0
        for rows in piece_rows(layers, own):
            cuts.append(ref[at : at + rows].astype(F32))
            at += rows
        parts.append(cuts)
    mats = [
        jnp.stack([jnp.concatenate(cuts[1:4], axis=1) for cuts in parts]),
        jnp.stack([cuts[4] for cuts in parts]),
        jnp.stack([jnp.concatenate(cuts[5:9], axis=1) for cuts in parts]),
        jnp.stack([cuts[0] for cuts in parts]),
        jnp.concatenate(
            [above[at + i * own : at + (i + 1) * own].astype(F32) for i in range(4)], axis=1
        ),
    ]
    small = below[at : at + 2 * UNIT, :128].astype(F32)
    vectors = [
        jnp.stack([small[i * VECTORS + j, :own] for i in range(layers)]) for j in range(VECTORS)
    ]
    inner_bias = small[count + 2 : count + 2 + layers, : 4 * own]
    return mats, vectors, small[count, :own], small[count + 1, :own], inner_bias


def pair_swap(values, bit):
    return swap(values, "tensor", bit)


def scatter_start(mine, other, first):
    held = mine.astype(F32) + pair_swap(other, 1).astype(F32)
    return held, held[1].astype(BF16)


def scatter_rest(held, sent, first, second):
    held = held[0] + swap(sent, *first).astype(F32)
    return held[0] + swap(held[1].astype(BF16), *second).astype(F32)


def next_on_line(values):
    size = lax.axis_size("dp")
    return lax.ppermute(values, "dp", [(i, (i + 2) % size) for i in range(size)])


def scatter_line(held):
    total = held[3]
    for ahead in (2, 1, 0):
        total = held[ahead] + next_on_line(total.astype(BF16)).astype(F32)
    return total


def gather_line(values):
    parts = [values]
    for _ in range(lax.axis_size("dp") // 2 - 1):
        parts.append(next_on_line(parts[-1]))
    return jnp.stack(parts)


def sum_grads(packed, rows_list, vector_rows):
    dp_size = lax.axis_size("dp")
    if dp_size == 8:
        x, y = ("dp", 1), ("tensor", 2)
        held_a, sent_a = scatter_start(packed[0], packed[1], y)
        held_b, sent_b = scatter_start(packed[2], packed[3], x)

        def rest():
            halves = [scatter_rest(held_a, sent_a, y, x), scatter_rest(held_b, sent_b, x, y)]
            return scatter_line(jnp.concatenate(halves, axis=1))

        return sent_b, rest
    packed_a = jnp.stack(packed[:2]).transpose(3, 2, 1, 0, 4, 5)
    packed_b = jnp.stack(packed[2:]).transpose(3, 1, 2, 0, 4, 5)
    packed = jnp.concatenate([packed_a, packed_b], axis=4)
    packed = packed.reshape((BLOCKS,) + packed.shape[4:])
    packed = to_devices(packed, 4 * dp_size, rows_list, vector_rows)
    summed = lax.psum_scatter(packed, BOTH, scatter_dimension=0, tiled=True)[0]
    return packed, lambda: summed


def dp_bits():
    size = lax.axis_size("dp")
    return [1 << i for i in range(size.bit_length() - 1)]


def dp_places():
    bits = dp_bits()
    return [
        sum(bit for i, bit in enumerate(reversed(bits)) if (place >> i) & 1)
        for place in range(lax.axis_size("dp"))
    ]


def gather_relative(values, first, last):
    for bit in list(reversed(dp_bits()))[first:last]:
        values = jnp.concatenate([values, swap(values, "dp", bit)])
    return values


def reduce_relative(keep, send):
    bits = dp_bits()
    keep = keep + swap(send, "dp", bits[0])
    for bit in bits[1:]:
        half = keep.shape[0] // 2
        keep = keep[:half] + swap(keep[half:], "dp", bit)
    return keep[0]


def exchange_relative(first, second, third):
    return [pair_swap(first, 1), pair_swap(second, 2), pair_swap(third, 3)]


def local(
    piece_table,
    piece_ids,
    piece_counts,
    text_ids,
    cotangent,
    rms_gain_one,
    w_query,
    w_key,
    w_value,
    w_output,
    rms_gain_two,
    w_gate,
    w_up,
    w_down,
    *shard_params,
):
    tensor_index = lax.axis_index("tensor")
    dp_index = lax.axis_index("dp")
    tensor_size = lax.axis_size("tensor")
    dp_size = lax.axis_size("dp")
    devices = tensor_size * dp_size
    micro_count, group_entries, slot_count = piece_ids.shape
    own_entries = group_entries // tensor_size
    seq_length = text_ids.shape[1]
    share = cotangent.shape[1]
    layer_count, own, _ = shard_params[2].shape
    width = shard_params[5].shape[2]
    lm_width = cotangent.shape[2]
    table_rows, table_cols = piece_table.shape
    gain_first = rms_gain_one[None, :]
    gain_second = rms_gain_two[None, :]
    cosine, sine = rotary_tables(seq_length)
    trig = jnp.concatenate([cosine.T, sine.T], axis=0)
    w_kv = jnp.concatenate([w_key, w_value], axis=1)

    where = tensor_index.astype(jnp.int32)[None]

    gathered = lax.all_gather(pack_shards(shard_params), BOTH, axis=0)

    stages = len(dp_bits())
    ids_rel = gather_relative(piece_ids[None], 0, stages)
    ids_rel = ids_rel.reshape(dp_size, micro_count, tensor_size, own_entries, slot_count)
    ids_rel = jnp.take(ids_rel, tensor_index ^ jnp.arange(tensor_size), axis=2)
    ids_rel = ids_rel.transpose(0, 2, 1, 3, 4) - dp_index * table_rows
    places = jnp.asarray(dp_places())
    ids_back = jnp.zeros_like(ids_rel).at[dp_index ^ places].set(ids_rel)
    if dp_size == 8:
        behind = (dp_index + dp_size - 2 * jnp.arange(dp_size // 2)) % dp_size
        ids_back = jnp.take(ids_back, jnp.concatenate([behind, behind ^ 1]), axis=0)
    ids_back = ids_back.reshape(2, -1)
    ids_rel = ids_rel.reshape(2, -1)
    own_rows = micro_count * own_entries * slot_count
    looked = [
        lookup(ids_rel[i], piece_table).reshape(dp_size // 2, tensor_size, own_rows, table_cols)
        for i in (1, 0)
    ]
    looked = reduce_relative(looked[1], looked[0])
    pieces = [looked[0], *exchange_relative(*looked[1:])]

    packed, vectors, inner_bias = canonical(gathered, own, layer_count)
    counts_own = lax.dynamic_slice_in_dim(piece_counts, tensor_index * own_entries, own_entries, 1)
    valid = jnp.arange(slot_count)[None, :] < counts_own.reshape(-1)[:, None]
    valid = valid.astype(F32).reshape(1, own_rows)
    w_out = [w_output, pair_swap(w_output, 1), pair_swap(w_output, 2)]
    *kept_hyper, pooled, pooled_norm, embeds = hyper_forward(
        where, w_out[2], pieces, valid, vectors, inner_bias, packed, slot_count
    )

    w_out.append(pair_swap(w_out[2], 1))
    embeds = embeds.reshape(micro_count, own_entries, lm_width)
    embeds = [embeds, pair_swap(embeds, 1), pair_swap(embeds, 2)]
    embeds.append(pair_swap(embeds[2], 1))
    text_rel = text_ids ^ (tensor_index * own_entries)

    micros = range(micro_count)
    ids_row, ids_own, ids_peer = [], [], []
    for micro in micros:
        row = text_rel[micro][None, :]
        ids_row.append(row)
        ids_own.append(lax.dynamic_slice_in_dim(row, tensor_index * share, share, 1))
        ids_peer.append(lax.dynamic_slice_in_dim(row, (tensor_index ^ 2) * share, share, 1))

    def cots_of(micro, after):
        own = cast_after(micro, cotangent, after)
        peer = pair_swap(own, 2)
        return (own, pair_swap(own, 1)), (peer, pair_swap(peer, 1))

    kept_attn, contexts = [], []
    after = (embeds[0], embeds[0])
    cots_near, cots_peer = cots_of(0, embeds[3])
    for micro in micros:
        near, far, *kept = attend(
            where, micro, embeds, gain_first, w_query, w_kv, ids_row[micro], trig, after
        )
        kept_attn.append(kept)
        contexts.append([near, *exchange_relative(far, near, far)])
        after = (near, cots_peer[0])

    def after_attention(micro, after):
        own, peer, rows = hidden_rows_of(
            kept_attn[micro][-1], ids_own[micro], ids_peer[micro], gain_second,
            contexts[micro], w_out, after,
        )
        return (own, pair_swap(own, 1)), (peer, pair_swap(peer, 1)), rows

    def feed_forward(normed, cots, *after):
        after = (after + after[:1] * 2)[:3]
        return mlp(*normed, *cots, w_gate, w_up, w_down, after)

    def travel(part):
        away = (part[2].astype(F32) + pair_swap(part[3], 1).astype(F32)).astype(BF16)
        return away, pair_swap(away, 2)

    def back_of(micro, rows, near, arrived):
        low, *parts = hidden_back(
            micro, cotangent, rows, near[2], pair_swap(near[3], 1), arrived, gain_second, w_out
        )
        return low, [parts[0], *exchange_relative(*parts[1:])]

    def result_of(rows, near, peer, after):
        away = add_after(peer[0], pair_swap(peer[1], 1), after)
        total = rows + near[0].astype(F32) + pair_swap(near[1], 1).astype(F32)
        return (total + pair_swap(away, 2).astype(F32)).astype(BF16)

    near_in, peer_in, rows_a = after_attention(0, (contexts[1][0], contexts[1][0]))
    near_a = feed_forward(near_in, cots_near, rows_a)
    cots_near_b, cots_peer_b = cots_of(1, near_a[2])
    peer_a = feed_forward(peer_in, cots_peer, near_a[2], contexts[1][2], contexts[1][3])
    away_a, arrived_a = travel(peer_a)
    near_in, peer_in, rows_b = after_attention(1, (away_a, cots_peer_b[0]))
    out_a = result_of(rows_a, near_a, peer_a, rows_b)
    peer_b = feed_forward(peer_in, cots_peer_b, rows_b)
    away_b, arrived_b = travel(peer_b)
    low_a, parts_a = back_of(0, rows_a, near_a, arrived_a)
    near_b = feed_forward(near_in, cots_near_b, low_a, out_a, away_b)
    low_b, parts_b = back_of(1, rows_b, near_b, arrived_b)
    out_b = result_of(rows_b, near_b, peer_b, low_b)

    place = jnp.stack([tensor_index % 2, tensor_index // 2, dp_index % 2, dp_index // 2])
    place = place.astype(jnp.int32)
    grad_embeds = []
    after = (low_b, low_b, low_b)
    for micro, parts, low in ((0, parts_a, low_a), (1, parts_b, low_b)):
        grads = attend_back(
            where, parts, kept_attn[micro], ids_row[micro], ids_own[micro], trig,
            w_query, w_kv, gain_first, low, after,
        )
        after = (grads, out_b, out_b)
        grads = grads.reshape(2, 2, own_entries, lm_width)
        arrived = pair_swap(grads[:, 1], 1).astype(F32) + grads[:, 0].astype(F32)
        arrived = arrived[0] + pair_swap(arrived[1].astype(BF16), 2).astype(F32)
        grad_embeds.append(arrived.astype(BF16))

    if dp_size != 8:
        place = place * 0
    source = (jnp.concatenate(grad_embeds, axis=0), pooled, pooled_norm)
    above, after = (), pooled
    rest = [None] * layer_count
    for layer in range(layer_count - 1, -1, -1):
        *parts, source, small, inner_small = hyper_backward(
            place, layer, source, valid, vectors, kept_hyper, packed, slot_count, above,
            table_cols, after,
        )
        above = (small, inner_small)
        rows_list = piece_rows(layer_count, UNIT) + ([UNIT] * 4 if layer == layer_count - 1 else [])
        after, rest[layer] = sum_grads(parts, rows_list, 2 * UNIT if layer == 0 else 0)
    reduced = [part() for part in rest]

    if dp_size != 8:
        source = jnp.take(source, tensor_index ^ jnp.arange(tensor_size), axis=0)
    arrived = jnp.stack([source[0], *exchange_relative(*source[1:])])
    if dp_size == 8:
        arrived = gather_line(arrived)
        halves = [arrived, swap(arrived, "dp", 1)]
    else:
        halves = jnp.split(lax.all_gather(arrived, "dp", axis=0), 2)
    table_grad = None
    for ids, rows in zip(ids_back, halves):
        table_grad = collect(ids, rows.reshape(-1, table_cols), table_rows, table_grad)

    mats, vecs, out_final_gain, out_final_bias, out_inner_bias = unpack_grads(
        reduced[1], reduced[0], own, layer_count
    )
    return (
        jnp.stack([out_a, out_b]),
        table_grad,
        vecs[0],
        vecs[1],
        mats[0],
        vecs[2],
        vecs[3],
        mats[1],
        vecs[4],
        vecs[5],
        vecs[6],
        mats[2],
        out_inner_bias,
        mats[3],
        vecs[7],
        out_final_gain,
        out_final_bias,
        mats[4],
    )


def solution(mesh):
    return jax.shard_map(
        local,
        mesh=mesh,
        in_specs=(
            P("dp", "tensor"),
            P(None, "dp", None),
            P(None, "dp"),
            P(None, "dp"),
            P(None, ("dp", "tensor"), None),
            P(),
            P(None, "tensor"),
            P(None, "tensor"),
            P(None, "tensor"),
            P("tensor", None),
            P(),
            P(None, "tensor"),
            P(None, "tensor"),
            P("tensor", None),
            P(None, ("dp", "tensor")),
            P(None, ("dp", "tensor")),
            P(None, ("dp", "tensor"), None),
            P(None, ("dp", "tensor")),
            P(None, ("dp", "tensor")),
            P(None, ("dp", "tensor"), None),
            P(None, ("dp", "tensor")),
            P(None, ("dp", "tensor")),
            P(None, ("dp", "tensor")),
            P(None, ("dp", "tensor"), None),
            P(None, ("dp", "tensor")),
            P(None, ("dp", "tensor"), None),
            P(None, ("dp", "tensor")),
            P(("dp", "tensor")),
            P(("dp", "tensor")),
            P(("dp", "tensor"), None),
        ),
        out_specs=(
            P(None, ("dp", "tensor"), None),
            P("dp", "tensor"),
            P(None, ("dp", "tensor")),
            P(None, ("dp", "tensor")),
            P(None, ("dp", "tensor"), None),
            P(None, ("dp", "tensor")),
            P(None, ("dp", "tensor")),
            P(None, ("dp", "tensor"), None),
            P(None, ("dp", "tensor")),
            P(None, ("dp", "tensor")),
            P(None, ("dp", "tensor")),
            P(None, ("dp", "tensor"), None),
            P(None, ("dp", "tensor")),
            P(None, ("dp", "tensor"), None),
            P(None, ("dp", "tensor")),
            P(("dp", "tensor")),
            P(("dp", "tensor")),
            P(("dp", "tensor"), None),
        ),
        check_vma=False,
    )
```

```python
import jax
import jax.numpy as jnp
from jax import lax
from jax.experimental import pallas as pl
from jax.experimental.pallas import tpu as pltpu
from jax.sharding import PartitionSpec as P

HEAD_DIM = 64
EPS_NORM = 1e-05
HIGH = lax.Precision.HIGHEST
SQRT_HALF = 0.7071067811865476
INV_SQRT_TAU = 0.3989422804014327
BOTH = ("dp", "tensor")
F32 = jnp.float32
BF16 = jnp.bfloat16


def matmul(left, right):
    return jnp.dot(left, right, preferred_element_type=F32)


def matmul_right_t(left, right):
    return lax.dot_general(left, right, (((1,), (1,)), ((), ())), preferred_element_type=F32)


def matmul_left_t(left, right):
    return lax.dot_general(left, right, (((0,), (0,)), ((), ())), preferred_element_type=F32)


def norm_parts(values):
    centered = values - jnp.mean(values, axis=-1, keepdims=True)
    inverse = lax.rsqrt(jnp.mean(centered * centered, axis=-1, keepdims=True) + EPS_NORM)
    return (centered * inverse, inverse)


def norm_back(normed, inverse, grad_scaled):
    return inverse * (
        grad_scaled
        - jnp.mean(grad_scaled, axis=-1, keepdims=True)
        - normed * jnp.mean(grad_scaled * normed, axis=-1, keepdims=True)
    )


def rms_parts(values):
    return lax.rsqrt(jnp.mean(values * values, axis=-1, keepdims=True) + EPS_NORM)


def rms_back(values, inverse, grad_scaled):
    return inverse * grad_scaled - values * inverse**3 * jnp.mean(
        grad_scaled * values, axis=-1, keepdims=True
    )


def rotary_tables(seq_length):
    half_dim = HEAD_DIM // 2
    freqs = 10000.0 ** (-jnp.arange(half_dim, dtype=F32) * 2.0 / HEAD_DIM)
    angles = jnp.arange(seq_length, dtype=F32)[:, None] * freqs[None, :]
    angles = jnp.concatenate([angles, angles], axis=-1)
    return (jnp.cos(angles), jnp.sin(angles))


def swap(values, axis, bit):
    size = lax.axis_size(axis)
    return lax.ppermute(values, axis, [(i, i ^ bit) for i in range(size)])


def lookup_kernel(ids_ref, table_ref, _after, out_ref):
    rows = ids_ref.shape[0]
    height, width = table_ref.shape
    half = height // 2
    ids = ids_ref[...]
    upper = ids >= half
    places = jnp.where(upper, ids - half, ids)
    chosen = places == lax.broadcasted_iota(jnp.int32, (rows, half), 1)
    pairs = jnp.concatenate([table_ref[:half], table_ref[half:]], axis=1)
    found = matmul(jnp.where(chosen, 1.0, 0.0).astype(BF16), pairs)
    out_ref[...] = jnp.where(upper, found[:, width:], found[:, :width]).astype(BF16)


def lookup(ids, table, after):
    count = ids.shape[0]
    height, width = table.shape
    rows = 512
    return pl.pallas_call(
        lookup_kernel,
        grid=(count // rows,),
        in_specs=[
            pl.BlockSpec((rows, 1), lambda i: (i, 0)),
            pl.BlockSpec((height, width), lambda i: (0, 0)),
            pl.BlockSpec(memory_space=pl.ANY),
        ],
        out_specs=pl.BlockSpec((rows, width), lambda i: (i, 0)),
        out_shape=jax.ShapeDtypeStruct((count, width), BF16),
        compiler_params=pltpu.CompilerParams(vmem_limit_bytes=48 << 20),
        cost_estimate=pl.CostEstimate(
            flops=4 * count * height * width, bytes_accessed=4 * count * width, transcendentals=0
        ),
        name="lookup",
    )(ids[:, None], table, after)


def collect_kernel(ids_ref, ids_left, ids_right, left_ref, right_ref, base_ref, out_ref):
    @pl.when(pl.program_id(0) == 0)
    def _():
        out_ref[...] = jnp.zeros_like(out_ref) if base_ref is None else base_ref[...]

    height, width = out_ref.shape
    half = height // 2
    total = None
    for i, (column, rows_ref) in enumerate(((ids_left, left_ref), (ids_right, right_ref))):
        ids = ids_ref[i : i + 1, :]
        ids = jnp.where(ids >= half, ids - half, ids)
        places = lax.broadcasted_iota(jnp.int32, (half, ids.shape[1]), 0)
        chosen = jnp.where(ids == places, 1.0, 0.0).astype(BF16)
        rows = rows_ref[...].astype(F32)
        upper = column[...] >= half
        pairs = [jnp.where(upper, 0.0, rows), jnp.where(upper, rows, 0.0)]
        part = matmul(chosen, jnp.concatenate(pairs, axis=1).astype(BF16))
        total = part if total is None else total + part
    out_ref[:half] += total[:, :width]
    out_ref[half:] += total[:, width:]


def collect(ids, columns, left, right, height, base):
    count, width = left.shape
    rows = 256
    whole = pl.BlockSpec((height, width), lambda i: (0, 0))
    kernel = collect_kernel
    if base is None:
        kernel = lambda *refs: collect_kernel(*refs[:5], None, refs[5])
    return pl.pallas_call(
        kernel,
        grid=(count // rows,),
        in_specs=[pl.BlockSpec((2, rows), lambda i: (0, i))]
        + [pl.BlockSpec((rows, 1), lambda i: (i, 0))] * 2
        + [pl.BlockSpec((rows, width), lambda i: (i, 0))] * 2
        + ([] if base is None else [whole]),
        out_specs=whole,
        out_shape=jax.ShapeDtypeStruct((height, width), F32),
        compiler_params=pltpu.CompilerParams(vmem_limit_bytes=48 << 20),
        cost_estimate=pl.CostEstimate(
            flops=8 * count * height * width, bytes_accessed=8 * count * width, transcendentals=0
        ),
        name="collect",
    )(ids, *columns, left, right, *([] if base is None else [base]))


QUERY_ROWS = 256
ENTRY_LANES = 64
VMEM_LIMIT = 56 << 20


def turn_rows(values):
    half_dim = HEAD_DIM // 2
    return jnp.concatenate([-values[half_dim:], values[:half_dim]], axis=0)


def two_parts(values):
    high = values.astype(BF16)
    return jnp.concatenate([high, (values - high.astype(F32)).astype(BF16)], axis=1)


def entry_table(columns):
    return two_parts(jnp.concatenate([columns, turn_rows(columns)], axis=0))


def spread(table, onehot, trig):
    both = matmul(table, onehot) * trig
    return both[:HEAD_DIM] + both[HEAD_DIM:]


def ahead_mask(rows):
    shape = (rows, rows)
    return lax.broadcasted_iota(jnp.int32, shape, 0) <= lax.broadcasted_iota(jnp.int32, shape, 1)


def attend_kernel(
    place, part0, part1, part2, part3, gain, w_query, w_kv, ids, trig, _after_one, _after_two,
    near, far, context_t, log_total, table_q, table_kv, embeds,
    normed, onehot, keys, values_t,
):
    tokens = ids.shape[1]

    @pl.when(pl.program_id(0) == 0)
    def _():
        own = part0.shape[1]
        for k, part in enumerate((part0, part1, part2, part3)):
            embeds[k * own : (k + 1) * own, :] = part[0]
        wide = embeds[...].astype(F32)
        normed[...] = (wide * rms_parts(wide) * gain[...].astype(F32)).astype(BF16)
        places = lax.broadcasted_iota(jnp.int32, onehot.shape, 0)
        places = jnp.where(places >= ENTRY_LANES, places - ENTRY_LANES, places)
        onehot[...] = jnp.where(places == ids[...], 1.0, 0.0).astype(BF16)
        mixed = matmul(normed[...], w_kv[...]).T
        table_kv[0] = entry_table(mixed[:HEAD_DIM])
        table_kv[1] = entry_table(mixed[HEAD_DIM:])
        keys[...] = spread(table_kv[0], onehot[...], trig[...]).T.astype(BF16)
        values_t[...] = matmul(table_kv[1], onehot[...])[:HEAD_DIM].astype(BF16)

    queries = matmul(normed[...], w_query[...]).T * HEAD_DIM ** (-0.5)
    ahead = ahead_mask(QUERY_ROWS)
    turned = []
    for j in range(2):
        table_q[0, j] = entry_table(queries[j * HEAD_DIM : (j + 1) * HEAD_DIM])
        turned.append(spread(table_q[0, j], onehot[...], trig[...]).astype(BF16))
    odd = place[0] % 2
    rows_out = []
    for block in range(tokens // QUERY_ROWS):
        start, stop = block * QUERY_ROWS, (block + 1) * QUERY_ROWS
        done = []
        for j in range(2):
            scores = matmul(keys[:stop], turned[j][:, start:stop])
            last = jnp.where(ahead, scores[start:], -1e30)
            highest = jnp.max(last, axis=0, keepdims=True)
            if block:
                highest = jnp.maximum(highest, jnp.max(scores[:start], axis=0, keepdims=True))
            last = jnp.exp(last - highest)
            total = jnp.sum(last, axis=0, keepdims=True)
            summed = matmul(values_t[:, start:stop], last.astype(BF16))
            if block:
                first = jnp.exp(scores[:start] - highest)
                total = total + jnp.sum(first, axis=0, keepdims=True)
                summed = summed + matmul(values_t[:, :start], first.astype(BF16))
            done.append(summed / total)
            log_total[0, j : j + 1, start:stop] = highest + jnp.log(total)
        done = jnp.concatenate(done, axis=0)
        context_t[:, start:stop] = done.astype(BF16)
        rows_out.append(done.T.astype(BF16))
        if block % 2:
            even_rows, odd_rows = rows_out[-2:]
            target = (block // 2) ^ (place[0] // 2)
            near[target] = jnp.where(odd == 0, even_rows, odd_rows)
            far[target] = jnp.where(odd == 0, odd_rows, even_rows)


def attend(place, micro, parts, gain, w_query, w_kv, ids, trig, after):
    assert ids.shape[1] == 4 * QUERY_ROWS
    _, own, width = parts[0].shape
    entries = own * len(parts)
    tokens = ids.shape[1]
    pairs = w_query.shape[1] // (2 * HEAD_DIM)
    lanes = 2 * HEAD_DIM
    whole = lambda *shape: pl.BlockSpec(shape, lambda i: (0,) * len(shape))
    return pl.pallas_call(
        attend_kernel,
        grid=(pairs,),
        in_specs=[pl.BlockSpec(memory_space=pltpu.SMEM)]
        + [pl.BlockSpec((1, own, width), lambda i: (micro, 0, 0))] * len(parts)
        + [
            whole(1, width),
            pl.BlockSpec((width, lanes), lambda i: (0, i)),
            whole(width, lanes),
            whole(1, tokens),
            whole(lanes, tokens),
        ]
        + [pl.BlockSpec(memory_space=pl.ANY)] * 2,
        out_specs=[
            pl.BlockSpec((2, QUERY_ROWS, lanes), lambda i: (0, 0, i)),
            pl.BlockSpec((2, QUERY_ROWS, lanes), lambda i: (0, 0, i)),
            pl.BlockSpec((lanes, tokens), lambda i: (i, 0)),
            pl.BlockSpec((1, 2, tokens), lambda i: (i, 0, 0)),
            pl.BlockSpec((1, 2, lanes, lanes), lambda i: (i, 0, 0, 0)),
            whole(2, lanes, lanes),
            whole(entries, width),
        ],
        out_shape=[
            jax.ShapeDtypeStruct((2, QUERY_ROWS, pairs * lanes), BF16),
            jax.ShapeDtypeStruct((2, QUERY_ROWS, pairs * lanes), BF16),
            jax.ShapeDtypeStruct((pairs * lanes, tokens), BF16),
            jax.ShapeDtypeStruct((pairs, 2, tokens), F32),
            jax.ShapeDtypeStruct((pairs, 2, lanes, lanes), BF16),
            jax.ShapeDtypeStruct((2, lanes, lanes), BF16),
            jax.ShapeDtypeStruct((entries, width), BF16),
        ],
        scratch_shapes=[
            pltpu.VMEM((entries, width), BF16),
            pltpu.VMEM((lanes, tokens), BF16),
            pltpu.VMEM((tokens, HEAD_DIM), BF16),
            pltpu.VMEM((HEAD_DIM, tokens), BF16),
        ],
        compiler_params=pltpu.CompilerParams(vmem_limit_bytes=VMEM_LIMIT),
        cost_estimate=pl.CostEstimate(
            flops=12 * 10**9, bytes_accessed=8 * 10**6, transcendentals=5 * 10**6
        ),
        name="attend",
    )(place, *parts, gain, w_query, w_kv, ids, trig, *after)


def attend_back_kernel(
    place, part0, part1, part2, part3, context_t, log_total, table_q, table_kv, ids, ids_share, trig,
    w_query, w_kv, embeds, gain, grad_hidden, _a0, _a1, _a2, _a3, _a4, grads0, grads1, grads2, grads3,
    onehot, columns, keys, keys_t, values, grad_keys, grad_values, total, grad_context,
):
    tokens = ids.shape[1]
    share = part0.shape[0]
    for k, part in enumerate((part0, part1, part2, part3)):
        first = pl.multiple_of((place[0] ^ k) * share, share)
        grad_context[pl.ds(first, share), :] = part[...]
    entries = embeds.shape[0]
    cosine, sine = trig[:HEAD_DIM], trig[HEAD_DIM:]

    @pl.when(pl.program_id(0) == 0)
    def _():
        places = lax.broadcasted_iota(jnp.int32, onehot.shape, 0)
        places = jnp.where(places >= ENTRY_LANES, places - ENTRY_LANES, places)
        chosen = jnp.where(places == ids[...], 1.0, 0.0)
        onehot[...] = chosen.astype(BF16)
        columns[...] = chosen.T.astype(BF16)
        turned = spread(table_kv[0], onehot[...], trig[...])
        keys_t[...] = turned.astype(BF16)
        keys[...] = turned.T.astype(BF16)
        values[...] = matmul(table_kv[1], onehot[...])[:HEAD_DIM].T.astype(BF16)
        grad_keys[...] = jnp.zeros_like(grad_keys)
        grad_values[...] = jnp.zeros_like(grad_values)
        total[...] = jnp.zeros_like(total)

    def to_entries(grads, cos_part, sin_part, rows):
        straight = matmul((grads * cos_part).astype(BF16), rows)
        crossed = matmul((grads * sin_part).astype(BF16), rows)
        return straight, crossed

    def two_stacked(grads):
        high = grads.astype(BF16)
        rest = (grads - high.astype(F32)).astype(BF16)
        lane = lax.broadcasted_iota(jnp.int32, grads.shape, 1)
        return jnp.where(lane < ENTRY_LANES, high.astype(F32), rest.astype(F32)).T.astype(BF16)

    ahead = ahead_mask(QUERY_ROWS)
    grad_t = grad_context[...].astype(F32).T
    products = grad_t * context_t[...].astype(F32)
    grad_t = grad_t.astype(BF16)
    per_head = []
    for j in range(2):
        head = slice(j * HEAD_DIM, (j + 1) * HEAD_DIM)
        turned = spread(table_q[0, j], onehot[...], trig[...])
        queries_t = turned.astype(BF16)
        queries = turned.T.astype(BF16)
        offset = jnp.sum(products[head], axis=0, keepdims=True)
        straight = jnp.zeros((HEAD_DIM, columns.shape[1]), F32)
        crossed = jnp.zeros((HEAD_DIM, columns.shape[1]), F32)
        for block in range(tokens // QUERY_ROWS):
            start, stop = block * QUERY_ROWS, (block + 1) * QUERY_ROWS
            scores = matmul(keys[:stop], queries_t[:, start:stop])
            soft = jnp.exp(scores - log_total[0, j : j + 1, start:stop])
            last = jnp.where(ahead, soft[start:], 0.0)
            soft = jnp.concatenate([soft[:start], last], axis=0) if block else last
            grad_soft = matmul(values[:stop], grad_t[head, start:stop])
            grad_scores = (soft * (grad_soft - offset[:, start:stop])).astype(BF16)
            grad_values[:stop] += matmul(soft.astype(BF16), grad_context[start:stop, head])
            grad_keys[:stop] += matmul(grad_scores, queries[start:stop])
            grad_queries = matmul(keys_t[:, :stop], grad_scores) * HEAD_DIM ** (-0.5)
            parts = to_entries(
                grad_queries, cosine[:, start:stop], sine[:, start:stop], columns[start:stop]
            )
            straight, crossed = straight + parts[0], crossed + parts[1]
        per_head.append(straight - turn_rows(crossed))
    total[...] += matmul_right_t(two_stacked(jnp.concatenate(per_head, axis=0)), w_query[...])

    @pl.when(pl.program_id(0) == pl.num_programs(0) - 1)
    def _():
        grads = jnp.concatenate([grad_keys[...], grad_values[...]], axis=1).T
        straight, crossed = to_entries(grads[:HEAD_DIM], cosine, sine, columns[...])
        summed = matmul(grads[HEAD_DIM:].astype(BF16), columns[...])
        both = jnp.concatenate([straight - turn_rows(crossed), summed], axis=0)
        full = total[...] + matmul_right_t(two_stacked(both), w_kv[...])
        scaled = (full[:entries] + full[entries:]) * gain[...].astype(F32)
        wide = embeds[...].astype(F32)
        places = lax.broadcasted_iota(jnp.int32, (entries, ids_share.shape[1]), 0)
        chosen = jnp.where(places == ids_share[...], 1.0, 0.0).astype(BF16)
        result = rms_back(wide, rms_parts(wide), scaled) + matmul(chosen, grad_hidden[...])
        result = result.astype(BF16)
        own = grads0.shape[0]
        for k, out in enumerate((grads0, grads1, grads2, grads3)):
            out[...] = result[k * own : (k + 1) * own]


def attend_back(
    place, parts, kept, ids, ids_share, trig, w_query, w_kv, gain, grad_hidden, after
):
    context_t, log_total, table_q, table_kv, embeds = kept
    share = parts[0].shape[0]
    entries, width = embeds.shape
    tokens = ids.shape[1]
    pairs = w_query.shape[1] // (2 * HEAD_DIM)
    lanes = 2 * HEAD_DIM
    whole = lambda *shape: pl.BlockSpec(shape, lambda i: (0,) * len(shape))
    return pl.pallas_call(
        attend_back_kernel,
        grid=(pairs,),
        in_specs=[pl.BlockSpec(memory_space=pltpu.SMEM)]
        + [pl.BlockSpec((share, lanes), lambda i: (0, i))] * len(parts)
        + [
            pl.BlockSpec((lanes, tokens), lambda i: (i, 0)),
            pl.BlockSpec((1, 2, tokens), lambda i: (i, 0, 0)),
            pl.BlockSpec((1, 2, lanes, lanes), lambda i: (i, 0, 0, 0)),
            whole(2, lanes, lanes),
            whole(1, tokens),
            whole(*ids_share.shape),
            whole(lanes, tokens),
            pl.BlockSpec((width, lanes), lambda i: (0, i)),
            whole(width, lanes),
            whole(entries, width),
            whole(1, width),
            whole(*grad_hidden.shape),
        ]
        + [pl.BlockSpec(memory_space=pl.ANY)] * 5,
        out_specs=[whole(entries // 4, width)] * 4,
        out_shape=[jax.ShapeDtypeStruct((entries // 4, width), BF16)] * 4,
        scratch_shapes=[
            pltpu.VMEM((lanes, tokens), BF16),
            pltpu.VMEM((tokens, lanes), BF16),
            pltpu.VMEM((tokens, HEAD_DIM), BF16),
            pltpu.VMEM((HEAD_DIM, tokens), BF16),
            pltpu.VMEM((tokens, HEAD_DIM), BF16),
            pltpu.VMEM((tokens, HEAD_DIM), F32),
            pltpu.VMEM((tokens, HEAD_DIM), F32),
            pltpu.VMEM((2 * entries, width), F32),
            pltpu.VMEM((tokens, lanes), BF16),
        ],
        compiler_params=pltpu.CompilerParams(vmem_limit_bytes=VMEM_LIMIT),
        cost_estimate=pl.CostEstimate(
            flops=25 * 10**9, bytes_accessed=8 * 10**6, transcendentals=5 * 10**6
        ),
        name="attend_back",
    )(
        place, *parts, context_t, log_total, table_q, table_kv, ids, ids_share, trig,
        w_query, w_kv, embeds, gain, grad_hidden, *after,
    )


ANY_SPEC = pl.BlockSpec(memory_space=pl.ANY)


def pick_rows(ids, entries):
    places = lax.broadcasted_iota(jnp.int32, (entries, ids.shape[1]), 0)
    return jnp.where(places == ids[...], 1.0, 0.0).astype(BF16)


def load_weights(sources, targets, sems):
    copies = [
        pltpu.make_async_copy(source, target, sems.at[i])
        for i, (source, target) in enumerate(zip(sources, targets))
    ]
    for copy in copies:
        copy.start()
    return copies


def hidden_kernel(
    embeds, ids_own, ids_peer, gain, c0, c1, c2, c3, w0, w1, w2, w3, _after_one, _after_two,
    normed_own, normed_peer, hidden, held, sems,
):
    heads = w0.shape[0]
    copies = load_weights(
        (w0, w1, w2, w3), [held.at[pl.ds(k * heads, heads)] for k in range(4)], sems
    )
    rows = jnp.concatenate([pick_rows(ids_own, embeds.shape[0]), pick_rows(ids_peer, embeds.shape[0])], axis=1)
    total = matmul_left_t(rows, embeds[...])
    for first, (left, right) in ((0, (c0, c1)), (2, (c2, c3))):
        own = first // 2
        sides = [jnp.concatenate([part[own], part[1 - own]], axis=0) for part in (left, right)]
        copies[first].wait()
        copies[first + 1].wait()
        both = jnp.concatenate(sides, axis=1)
        total = total + matmul(both, held[first * heads : (first + 2) * heads])
    low = (total * rms_parts(total) * gain[...].astype(F32)).astype(BF16)
    share = normed_own.shape[0]
    normed_own[...] = low[:share]
    normed_peer[...] = low[share:]
    hidden[...] = total[:share]


def hidden_rows_of(embeds, ids_own, ids_peer, gain, parts, weights, after):
    rows, width = ids_own.shape[1], embeds.shape[1]
    vmem = pl.BlockSpec(memory_space=pltpu.VMEM)
    return pl.pallas_call(
        hidden_kernel,
        in_specs=[vmem] * 8 + [ANY_SPEC] * 6,
        out_specs=[vmem] * 3,
        out_shape=[
            jax.ShapeDtypeStruct((rows, width), BF16),
            jax.ShapeDtypeStruct((rows, width), BF16),
            jax.ShapeDtypeStruct((rows, width), F32),
        ],
        scratch_shapes=[
            pltpu.VMEM((4 * weights[0].shape[0], width), BF16),
            pltpu.SemaphoreType.DMA((4,)),
        ],
        compiler_params=pltpu.CompilerParams(vmem_limit_bytes=VMEM_LIMIT),
        cost_estimate=pl.CostEstimate(
            flops=6 * 10**9, bytes_accessed=18 * 10**6, transcendentals=0
        ),
        name="hidden",
    )(embeds, ids_own, ids_peer, gain, *parts, *weights, *after)


def hidden_back_kernel(
    cotangent, hidden, kept, core_a, core_b, from_chip, gain, w0, w1, w2, w3,
    low, p0, p1, p2, p3, held, sems,
):
    copies = load_weights((w2, w3, w1, w0), [held.at[k] for k in range(4)], sems)
    from_core = jnp.concatenate([core_a[...], core_b[...]], axis=0)
    grads = kept[...].astype(F32) + from_core.astype(F32) + from_chip[...].astype(F32)
    rows = hidden[...]
    scaled = grads * gain[...].astype(F32)
    total = cotangent[0] + rms_back(rows, rms_parts(rows), scaled)
    total = total.astype(BF16)
    low[...] = total
    for k, part in enumerate((p2, p3, p1, p0)):
        copies[k].wait()
        part[...] = matmul_right_t(total, held[k]).astype(BF16)


def hidden_back(micro, cotangent, hidden, kept, from_core, from_chip, gain, weights):
    rows, width = hidden.shape
    heads = weights[0].shape[0]
    whole = lambda *shape: pl.BlockSpec(shape, lambda i: (0,) * len(shape))
    return pl.pallas_call(
        hidden_back_kernel,
        grid=(1,),
        in_specs=[
            pl.BlockSpec((1, rows, width), lambda i: (micro, 0, 0)),
            whole(rows, width),
            whole(rows, width),
            whole(rows // 2, width),
            whole(rows // 2, width),
            whole(rows, width),
            whole(1, width),
        ]
        + [ANY_SPEC] * 4,
        out_specs=[whole(rows, width)] + [whole(rows, heads)] * 4,
        out_shape=[jax.ShapeDtypeStruct((rows, width), BF16)]
        + [jax.ShapeDtypeStruct((rows, heads), BF16)] * 4,
        scratch_shapes=[
            pltpu.VMEM((4, heads, width), BF16),
            pltpu.SemaphoreType.DMA((4,)),
        ],
        compiler_params=pltpu.CompilerParams(vmem_limit_bytes=VMEM_LIMIT),
        cost_estimate=pl.CostEstimate(
            flops=2 * 10**9, bytes_accessed=16 * 10**6, transcendentals=0
        ),
        name="hidden_back",
    )(cotangent, hidden, kept, *from_core, from_chip, gain, *weights)


def mlp_kernel(
    ready, x_mine, x_other, mine_in, other_in, gate_hbm, up_hbm, down_hbm,
    _after_one, _after_two, _after_three,
    out_mine, out_other, grad_mine, grad_a, grad_b,
    w_both, w_down, sems,
):
    units = w_down.shape[0]
    main = units // 256 * 256
    rest = units - main
    cuts = ((0, gate_hbm, 0, main), (main, up_hbm, 0, main), (2 * main, gate_hbm, main, rest),
            (2 * main + rest, up_hbm, main, rest))
    copies = load_weights(
        [source.at[:, pl.ds(at, size)] for _, source, at, size in cuts if size] + [down_hbm],
        [w_both.at[:, pl.ds(to, size)] for to, _, _, size in cuts if size] + [w_down],
        sems,
    )
    for first, (rows, cots, out, grad) in enumerate(
        ((x_other, other_in, out_other, None), (x_mine, mine_in, out_mine, grad_mine))
    ):
        if first == 0:
            copies[0].wait()
        gate = matmul(rows[...], w_both[:, :main])
        if first == 0:
            for copy in copies[1:-1]:
                copy.wait()
        others = matmul(rows[...], w_both[:, main:])
        gate = jnp.concatenate([gate, others[:, main : main + rest]], axis=1)
        upward = jnp.concatenate([others[:, :main], others[:, main + rest :]], axis=1)
        if first == 0:
            copies[-1].wait()
        if ready:
            grad_active = cots[...].astype(F32)
        else:
            grad_active = matmul_right_t(cots[...], w_down[...])
        sigmoid = 1.0 / (1.0 + jnp.exp(-gate))
        silu = gate * sigmoid
        activated = (silu * upward).astype(BF16)
        grad_gate = grad_active * upward * (sigmoid * (1.0 + gate * (1.0 - sigmoid)))
        grad_gate = grad_gate.astype(BF16)
        grad_up = (grad_active * silu).astype(BF16)
        out[...] = matmul(activated, w_down[...]).astype(BF16)
        parts = [grad_gate[:, :main], grad_up[:, :main], grad_gate[:, main:], grad_up[:, main:]]
        total = matmul_right_t(jnp.concatenate(parts, axis=1), w_both[...]).astype(BF16)
        if grad is None:
            half = grad_a.shape[0]
            grad_a[...] = total[:half]
            grad_b[...] = total[half:]
        else:
            grad[...] = total


def mlp(mine, other, mine_in, other_in, w_gate, w_up, w_down, after):
    rows, width = mine.shape
    units = w_gate.shape[1]
    assert units % 256 in (0, 128)
    ready = mine_in.shape[1] == units
    vmem = pl.BlockSpec(memory_space=pltpu.VMEM)
    return pl.pallas_call(
        lambda *refs: mlp_kernel(ready, *refs),
        in_specs=[vmem] * 4 + [ANY_SPEC] * 6,
        out_specs=[vmem] * 5,
        out_shape=[jax.ShapeDtypeStruct((rows, width), BF16)] * 3
        + [jax.ShapeDtypeStruct((rows // 2, width), BF16)] * 2,
        scratch_shapes=[
            pltpu.VMEM((width, 2 * units), BF16),
            pltpu.VMEM((units, width), BF16),
            pltpu.SemaphoreType.DMA((5,)),
        ],
        compiler_params=pltpu.CompilerParams(vmem_limit_bytes=VMEM_LIMIT),
        cost_estimate=pl.CostEstimate(
            flops=24 * rows * width * units, bytes_accessed=26 * 10**6, transcendentals=2 * rows * units
        ),
        name="mlp",
    )(mine, other, mine_in, other_in, w_gate, w_up, w_down, *after)


def cast_kernel(values, _after, out):
    out[...] = values[0].astype(BF16)


def cast_after(micro, values, after):
    _, rows, width = values.shape
    steps = 4
    return pl.pallas_call(
        cast_kernel,
        grid=(steps,),
        in_specs=[pl.BlockSpec((1, rows // steps, width), lambda i: (micro, i, 0)), ANY_SPEC],
        out_specs=pl.BlockSpec((rows // steps, width), lambda i: (i, 0)),
        out_shape=jax.ShapeDtypeStruct((rows, width), BF16),
        name="cast_after",
    )(values, after)


def tie_kernel(_values, _after, _out):
    pass


def tie(values, after):
    return pl.pallas_call(
        tie_kernel,
        in_specs=[ANY_SPEC] * 2,
        out_specs=ANY_SPEC,
        out_shape=jax.ShapeDtypeStruct(values.shape, values.dtype),
        input_output_aliases={0: 0},
        name="tie",
    )(values, after)


def results_kernel(*refs):
    out = refs[9]
    for micro in range(2):
        first, *rest = refs[4 * micro : 4 * micro + 4]
        total = first[...]
        for part in rest:
            total = total + part[...].astype(F32)
        out[micro] = total.astype(BF16)


def add_results(first, second, after):
    rows, width = first[0].shape
    steps = 4
    part = pl.BlockSpec((rows // steps, width), lambda i: (i, 0))
    return pl.pallas_call(
        results_kernel,
        grid=(steps,),
        in_specs=[part] * 8 + [ANY_SPEC],
        out_specs=pl.BlockSpec((2, rows // steps, width), lambda i: (0, i, 0)),
        out_shape=jax.ShapeDtypeStruct((2, rows, width), BF16),
        name="results",
    )(*first, *second, after)


BLOCKS = 32
UNIT = 16
LAYER_UNITS = 12
VECTORS = 8


def square(ref):
    blocks, rows, width = ref.shape
    return ref[...].reshape(blocks * rows, width)


ENTRY_ROWS = 256


def entry_bias(valid, slots):
    shape = (valid.shape[1], valid.shape[1])
    same = lax.broadcasted_iota(jnp.int32, shape, 0) // slots == lax.broadcasted_iota(
        jnp.int32, shape, 1
    ) // slots
    return jnp.where(jnp.logical_and(same, valid > 0.5), 0.0, -1e30)


def entry_soft(queries, keys, bias):
    scores = matmul_right_t(queries, keys) * HEAD_DIM ** (-0.5) + bias
    expon = jnp.exp(scores - jnp.max(scores, axis=1, keepdims=True))
    return expon / jnp.sum(expon, axis=1, keepdims=True)


def bell(values):
    return 0.5 * (1.0 + lax.erf(values * SQRT_HALF))


def lay_out_vectors(small, vectors, inner_bias):
    blocks, rows, lanes = small.shape

    def spread_rows(values, each, width):
        shape = (lanes, width)
        line = lax.broadcasted_iota(jnp.int32, shape, 0)
        column = lax.broadcasted_iota(jnp.int32, shape, 1)
        copies = jnp.where(column % each == line, 1.0, 0.0).astype(BF16)
        wide = matmul(values, copies).reshape(blocks, values.shape[0] // blocks, width)
        block = lax.broadcasted_iota(jnp.int32, wide.shape, 0)
        column = lax.broadcasted_iota(jnp.int32, wide.shape, 2)
        return jnp.sum(jnp.where(column // each == block, wide, 0.0), axis=0)

    count, width = vectors.shape
    layers, inner_width = inner_bias.shape
    values = small[...]
    vectors[...] = spread_rows(values.reshape(blocks * rows, lanes), UNIT, width)[:count]
    line = lax.broadcasted_iota(jnp.int32, values.shape, 1)
    for layer in range(layers):
        chosen = jnp.where(line == count + layer, values.astype(F32), 0.0)
        chosen = jnp.sum(chosen, axis=1).astype(BF16)
        inner_bias[layer : layer + 1, :] = spread_rows(chosen, 4 * UNIT, inner_width)


def hyper_kernel(
    slots, place, _a0, _a1, _a2, _a3, _a4, _a5, _a6, _a7, _a8, _a9, _a10, _a11, part0, part1, part2, part3, valid, small, outer, w_q, w_k, w_v, w_o, in0, in1, in2, in3,
    pr0, pr1, pr2, pr3,
    vectors, inner_bias, below, mixed, context, middle, inner, pooled, pooled_norm, embeds,
    state, joined,
):
    layer = pl.program_id(0)
    layers = pl.num_programs(0)
    rows, width = state.shape

    @pl.when(layer == 0)
    def _():
        columns = part0.shape[1]
        for k, part in enumerate((part0, part1, part2, part3)):
            at = pl.multiple_of((place[0] ^ k) * columns, columns)
            state[:, pl.ds(at, columns)] = part[...].astype(F32)
        lay_out_vectors(small, vectors, inner_bias)

    def vector(index):
        return vectors[pl.ds(index * layers + layer, 1), :]

    hidden = state[...]
    below[0] = hidden
    normed, _ = norm_parts(hidden)
    normed_in = (normed * vector(0) + vector(1)).astype(BF16)
    queries = (matmul(normed_in, square(w_q)) + vector(2)).astype(BF16)
    keys = matmul(normed_in, square(w_k)).astype(BF16)
    values = (matmul(normed_in, square(w_v)) + vector(3)).astype(BF16)
    mixed[0, :, :width] = queries
    mixed[0, :, width : 2 * width] = keys
    mixed[0, :, 2 * width :] = values
    for first in range(0, rows, ENTRY_ROWS):
        lines = slice(first, first + ENTRY_ROWS)
        bias = entry_bias(valid[:, lines], slots)
        for head in range(width // HEAD_DIM):
            at = slice(head * HEAD_DIM, (head + 1) * HEAD_DIM)
            soft = entry_soft(queries[lines, at], keys[lines, at], bias)
            joined[lines, at] = matmul(soft.astype(BF16), values[lines, at])
    context_low = joined[...].astype(BF16)
    context[0] = context_low
    centre = hidden + matmul(context_low, square(w_o)) + vector(4)
    middle[0] = centre
    normed, _ = norm_parts(centre)
    normed_mid = (normed * vector(5) + vector(6)).astype(BF16)
    total = centre + vector(7)
    for j, piece in enumerate((in0, in1, in2, in3)):
        at = slice(j * width, (j + 1) * width)
        part = matmul(normed_mid, square(piece)) + inner_bias[pl.ds(layer, 1), at]
        inner[0, :, at] = part
        activated = (part * bell(part)).astype(BF16)
        blocks = BLOCKS // 4
        total = total + matmul(
            activated, outer[j * blocks : (j + 1) * blocks].reshape(width, width)
        )
    state[...] = total

    @pl.when(layer == layers - 1)
    def _():
        slot = lax.broadcasted_iota(jnp.int32, (rows, width), 0) % slots
        first = jnp.where(slot == 0, total, 0.0).reshape(rows // slots, slots, width)
        first = jnp.sum(first, axis=1)
        pooled[...] = first
        normed, _ = norm_parts(first)
        low = (normed * vectors[VECTORS * layers : VECTORS * layers + 1, :]
               + vectors[VECTORS * layers + 1 : VECTORS * layers + 2, :]).astype(BF16)
        pooled_norm[...] = low
        for j, piece in enumerate((pr0, pr1, pr2, pr3)):
            embeds[:, j * width : (j + 1) * width] = matmul(low, square(piece)).astype(BF16)


def layer_specs(width, which):
    specs = [pl.BlockSpec((BLOCKS, 4 * UNIT, width), lambda i: (0, which(i) * LAYER_UNITS // 4, 0))]
    for j in range(4, LAYER_UNITS):
        specs.append(
            pl.BlockSpec((BLOCKS, UNIT, width), lambda i, j=j: (0, which(i) * LAYER_UNITS + j, 0))
        )
    return specs


def proj_specs(width, layers):
    return [
        pl.BlockSpec((BLOCKS, UNIT, width), lambda i, j=j: (0, layers * LAYER_UNITS + j, 0))
        for j in range(4)
    ]


def whole_spec(*shape):
    return pl.BlockSpec(shape, lambda i: (0,) * len(shape))


def hyper_forward(where, after, parts, valid, packed, slots, layers):
    rows, width = parts[0].shape[0], len(parts) * parts[0].shape[1]
    inner_width = 4 * width
    count = VECTORS * layers + 2
    last_rows = packed.shape[1] // (2 * UNIT) - 1
    entries = rows // slots
    by_layer = lambda *shape: pl.BlockSpec((1,) + shape, lambda i: (i,) + (0,) * len(shape))
    return pl.pallas_call(
        lambda *refs: hyper_kernel(slots, *refs),
        grid=(layers,),
        in_specs=[pl.BlockSpec(memory_space=pltpu.SMEM)]
        + [pl.BlockSpec(memory_space=pl.ANY)] * 12
        + [whole_spec(*part.shape) for part in parts]
        + [
            whole_spec(1, rows),
            pl.BlockSpec((BLOCKS, 2 * UNIT, 128), lambda i: (0, last_rows, 0)),
        ]
        + layer_specs(width, lambda i: i)
        + proj_specs(width, layers),
        out_specs=[
            whole_spec(count, width),
            whole_spec(layers, inner_width),
            by_layer(rows, width),
            by_layer(rows, 3 * width),
            by_layer(rows, width),
            by_layer(rows, width),
            by_layer(rows, inner_width),
            whole_spec(entries, width),
            whole_spec(entries, width),
            whole_spec(entries, 4 * width),
        ],
        out_shape=[
            jax.ShapeDtypeStruct((count, width), F32),
            jax.ShapeDtypeStruct((layers, inner_width), F32),
            jax.ShapeDtypeStruct((layers, rows, width), F32),
            jax.ShapeDtypeStruct((layers, rows, 3 * width), BF16),
            jax.ShapeDtypeStruct((layers, rows, width), BF16),
            jax.ShapeDtypeStruct((layers, rows, width), F32),
            jax.ShapeDtypeStruct((layers, rows, inner_width), F32),
            jax.ShapeDtypeStruct((entries, width), F32),
            jax.ShapeDtypeStruct((entries, width), BF16),
            jax.ShapeDtypeStruct((entries, 4 * width), BF16),
        ],
        scratch_shapes=[pltpu.VMEM((rows, width), F32), pltpu.VMEM((rows, width), F32)],
        compiler_params=pltpu.CompilerParams(vmem_limit_bytes=VMEM_LIMIT),
        cost_estimate=pl.CostEstimate(
            flops=8 * 10**9, bytes_accessed=25 * 10**6, transcendentals=4 * 10**6
        ),
        name="hyper",
    )(where, *after, *parts, valid, *([packed] * (1 + LAYER_UNITS - 3 + 4)))


def hyper_back_kernel(
    slots, layer, layers, last,
    *refs,
):
    place, refs = refs[0], refs[1:]
    if last:
        arrivals, (pooled, pooled_norm, pr0, pr1, pr2, pr3) = refs[:8], refs[8:14]
        refs = refs[14:]
    else:
        grad_start = refs[0]
        refs = refs[1:]
    valid, vectors, below, mixed, context, middle, inner = refs[2:9]
    outer, w_q, w_k, w_v, w_o, in0, in1, in2, in3 = refs[9:18]
    refs = refs[18:]
    if layer == 0:
        small_above, inner_above = refs[:2]
        refs = refs[2:]
    packed = refs[:4]
    grad_below, small, inner_small, grad_mixed = refs[4:8]
    _, rows, width = below.shape
    blocks = BLOCKS // 4
    core, chip, side, line = place[0], place[1], place[2], place[3]
    half = packed[0].shape[3]

    def vector(index):
        at = index * layers + layer
        return vectors[at : at + 1, :]

    def put_rows(lines, at, rows_each, values):
        for i, z in enumerate(lines):
            for x in range(2):
                for y in range(2):
                    left, right = values[i, x, y, 0], values[i, x, y, 1]
                    mine = jnp.where(core == 0, left, right)
                    other = jnp.where(core == 0, right, left)
                    for kind, part in enumerate((mine, other)):
                        if at < half:
                            where = pl.ds(at, rows_each)
                            packed[kind][y ^ chip, x ^ side, (z - line) & 3, where, :] = part
                        else:
                            where = pl.ds(at - half, rows_each)
                            packed[2 + kind][x ^ side, y ^ chip, (z - line) & 3, where, :] = part

    def put(unit, grads):
        grads = grads.astype(BF16).reshape(4, 2, 2, 2, UNIT, width)
        put_rows(range(4), unit * UNIT, UNIT, grads)

    def column_sum(values):
        return jnp.sum(values, axis=0, keepdims=True)

    if last:
        normed, inverse = norm_parts(pooled[...])
        grad_norm = jnp.zeros(normed.shape, F32)
        sums = []
        for group in (arrivals[:4], arrivals[4:]):
            total = group[0][...].astype(F32)
            for part in group[1:]:
                total = total + part[...].astype(F32)
            sums.append(total)
        grad_embeds = jnp.concatenate(sums, axis=0).astype(BF16)
        for j, piece in enumerate((pr0, pr1, pr2, pr3)):
            part = grad_embeds[:, j * width : (j + 1) * width]
            put(LAYER_UNITS + j, matmul_left_t(pooled_norm[...], part))
            grad_norm = grad_norm + matmul_right_t(part, square(piece))
        small[VECTORS : VECTORS + 1, :] = column_sum(grad_norm * normed)
        small[VECTORS + 1 : VECTORS + 2, :] = column_sum(grad_norm)
        final_gain = vectors[VECTORS * layers : VECTORS * layers + 1, :]
        grad_pooled = norm_back(normed, inverse, grad_norm * final_gain)
        slot = lax.broadcasted_iota(jnp.int32, (rows, width), 0) % slots
        grad_rows = jnp.broadcast_to(grad_pooled[:, None, :], (rows // slots, slots, width))
        grad_rows = jnp.where(slot == 0, grad_rows.reshape(rows, width), 0.0)
    else:
        grad_rows = grad_start[...]

    low = grad_rows.astype(BF16)
    small[7:8, :] = column_sum(grad_rows)
    normed_two, inverse_two = norm_parts(middle[0])
    normed_mid = (normed_two * vector(5) + vector(6)).astype(BF16)
    grad_mid = jnp.zeros(grad_rows.shape, F32)
    for j, piece in enumerate((in0, in1, in2, in3)):
        at = slice(j * width, (j + 1) * width)
        part = inner[0, :, at]
        share = bell(part)
        activated = (part * share).astype(BF16)
        slope = share + part * jnp.exp(-0.5 * part * part) * INV_SQRT_TAU
        where = slice(j * blocks, (j + 1) * blocks)
        grad_outer = matmul_left_t(activated, low).astype(BF16)
        put_rows((j,), 0, 4 * UNIT, grad_outer.reshape(1, 2, 2, 2, 4 * UNIT, width))
        grad_part = matmul_right_t(low, outer[where].reshape(width, width)) * slope
        inner_small[:, at] = column_sum(grad_part)
        grad_part = grad_part.astype(BF16)
        put(8 + j, matmul_left_t(normed_mid, grad_part))
        grad_mid = grad_mid + matmul_right_t(grad_part, square(piece))
    small[5:6, :] = column_sum(grad_mid * normed_two)
    small[6:7, :] = column_sum(grad_mid)
    grad_rows = grad_rows + norm_back(normed_two, inverse_two, grad_mid * vector(5))
    small[4:5, :] = column_sum(grad_rows)
    low = grad_rows.astype(BF16)
    put(7, matmul_left_t(context[0], low))
    grad_context = matmul_right_t(low, square(w_o)).astype(BF16)
    for first in range(0, rows, ENTRY_ROWS):
        lines = slice(first, first + ENTRY_ROWS)
        bias = entry_bias(valid[:, lines], slots)
        for head in range(width // HEAD_DIM):
            at, key_at, value_at = (
                slice(i * width + head * HEAD_DIM, i * width + (head + 1) * HEAD_DIM)
                for i in range(3)
            )
            queries, keys, values = (mixed[0, lines, part] for part in (at, key_at, value_at))
            soft = entry_soft(queries, keys, bias)
            grad_head = grad_context[lines, at]
            grad_soft = matmul_right_t(grad_head, values)
            offset = jnp.sum(soft * grad_soft, axis=1, keepdims=True)
            grad_scores = (soft * (grad_soft - offset) * HEAD_DIM ** (-0.5)).astype(BF16)
            grad_mixed[lines, at] = matmul(grad_scores, keys)
            grad_mixed[lines, key_at] = matmul_left_t(grad_scores, queries)
            grad_mixed[lines, value_at] = matmul_left_t(soft.astype(BF16), grad_head)
    normed_one, inverse_one = norm_parts(below[0])
    normed_in = (normed_one * vector(0) + vector(1)).astype(BF16)
    grad_in = jnp.zeros(grad_rows.shape, F32)
    for i, piece in enumerate((w_q, w_k, w_v)):
        part = grad_mixed[:, i * width : (i + 1) * width]
        if i != 1:
            small[2 + i // 2 : 3 + i // 2, :] = column_sum(part)
        part = part.astype(BF16)
        put(4 + i, matmul_left_t(normed_in, part))
        grad_in = grad_in + matmul_right_t(part, square(piece))
    small[0:1, :] = column_sum(grad_in * normed_one)
    small[1:2, :] = column_sum(grad_in)
    grad_rows = grad_rows + norm_back(normed_one, inverse_one, grad_in * vector(0))
    if layer == 0:
        part = grad_rows.astype(BF16)
        columns = grad_below.shape[2]
        for t in range(grad_below.shape[0]):
            grad_below[t ^ (2 * chip + core)] = part[:, t * columns : (t + 1) * columns]
        wide = refs[8]
        wide[...] = jnp.zeros_like(wide)
        own = small[...]
        above = small_above[...]
        for b in range(BLOCKS):
            at = slice(b * UNIT, (b + 1) * UNIT)
            for i in range(layers):
                source = own if i == 0 else above
                wide[b, i * VECTORS : (i + 1) * VECTORS, 0:UNIT] = source[:VECTORS, at]
            wide[b, VECTORS * layers : VECTORS * layers + 2, 0:UNIT] = above[VECTORS:, at]
            at = slice(b * 4 * UNIT, (b + 1) * 4 * UNIT)
            wide[b, VECTORS * layers + 2 : VECTORS * layers + 3, 0 : 4 * UNIT] = inner_small[:, at]
            wide[b, VECTORS * layers + 3 : VECTORS * layers + 4, 0 : 4 * UNIT] = inner_above[:, at]
        base = LAYER_UNITS * UNIT
        spare = jnp.zeros((BLOCKS, 2 * UNIT, width - wide.shape[2]), F32)
        full = jnp.concatenate([wide[...], spare], axis=2).astype(BF16)
        put_rows(range(4), base, 2 * UNIT, full.reshape(4, 2, 2, 2, 2 * UNIT, width))
    else:
        grad_below[...] = grad_rows


def hyper_backward(place, layer, source, valid, vectors, kept, packed, slots, above, columns, after):
    below, mixed, context, middle, inner = kept
    layers, rows, width = below.shape
    inner_width = inner.shape[2]
    last = layer == layers - 1
    at_layer = lambda *shape: pl.BlockSpec((1,) + shape, lambda i: (layer,) + (0,) * len(shape))
    inputs, specs = [place], [pl.BlockSpec(memory_space=pltpu.SMEM)]
    if last:
        arrivals, pooled, pooled_norm = source
        inputs += [*arrivals, pooled, pooled_norm] + [packed] * 4
        specs += [whole_spec(*part.shape) for part in arrivals] + [whole_spec(*pooled.shape)]
        specs += [whole_spec(*pooled_norm.shape)] + proj_specs(width, layers)
    else:
        inputs += [source]
        specs += [whole_spec(rows, width)]
    inputs += [*after, valid, vectors, below, mixed, context, middle, inner]
    specs += [pl.BlockSpec(memory_space=pl.ANY)] * 2
    specs += [whole_spec(1, rows), whole_spec(*vectors.shape), at_layer(rows, width)]
    specs += [at_layer(rows, 3 * width), at_layer(rows, width), at_layer(rows, width)]
    specs += [at_layer(rows, inner_width)]
    inputs += [packed] * (LAYER_UNITS - 3)
    specs += layer_specs(width, lambda i: layer)
    scratch = [pltpu.VMEM((rows, 3 * width), F32)]
    units = LAYER_UNITS + (4 if last else 0) + (2 if layer == 0 else 0)
    below_shape = jax.ShapeDtypeStruct((rows, width), F32)
    if layer == 0:
        inputs += list(above)
        specs += [whole_spec(*part.shape) for part in above]
        below_shape = jax.ShapeDtypeStruct((width // columns, rows, columns), BF16)
        scratch.append(pltpu.VMEM((BLOCKS, 2 * UNIT, 128), F32))
    half = units // 2 * UNIT
    out_shape = [
        jax.ShapeDtypeStruct((2, 2, 4, half, width), BF16),
        jax.ShapeDtypeStruct((2, 2, 4, half, width), BF16),
        jax.ShapeDtypeStruct((2, 2, 4, units * UNIT - half, width), BF16),
        jax.ShapeDtypeStruct((2, 2, 4, units * UNIT - half, width), BF16),
        below_shape,
        jax.ShapeDtypeStruct((VECTORS + (2 if last else 0), width), F32),
        jax.ShapeDtypeStruct((1, inner_width), F32),
    ]
    return pl.pallas_call(
        lambda *refs: hyper_back_kernel(slots, layer, layers, last, *refs),
        grid=(1,),
        in_specs=specs,
        out_specs=[whole_spec(*shape.shape) for shape in out_shape],
        out_shape=out_shape,
        scratch_shapes=scratch,
        compiler_params=pltpu.CompilerParams(vmem_limit_bytes=VMEM_LIMIT),
        cost_estimate=pl.CostEstimate(
            flops=8 * 10**9, bytes_accessed=25 * 10**6, transcendentals=4 * 10**6
        ),
        name="hyper_back",
    )(*inputs)


def pack_kernel(layers, *refs):
    (g1, b1, w_qkv, bq, bv, w_ao, bao, g2, b2, w_in, b_in, w_out, bout, fg, fb, w_proj) = refs[:16]
    packed, wide = refs[16:]
    width = packed.shape[1]
    for layer in range(layers):
        base = layer * LAYER_UNITS * UNIT
        packed[base : base + 4 * UNIT] = w_out[layer]
        for j in range(3):
            at = base + (4 + j) * UNIT
            packed[at : at + UNIT] = w_qkv[layer, :, j * width : (j + 1) * width]
        packed[base + 7 * UNIT : base + 8 * UNIT] = w_ao[layer]
        for j in range(4):
            at = base + (8 + j) * UNIT
            packed[at : at + UNIT] = w_in[layer, :, j * width : (j + 1) * width]
    base = layers * LAYER_UNITS * UNIT
    for j in range(4):
        packed[base + j * UNIT : base + (j + 1) * UNIT] = w_proj[:, j * width : (j + 1) * width]
    wide[...] = jnp.zeros_like(wide)
    for j, ref in enumerate((g1, b1, bq, bv, bao, g2, b2, bout)):
        wide[j * layers : (j + 1) * layers, 0:UNIT] = ref[...].astype(F32)
    at = VECTORS * layers
    wide[at : at + 1, 0:UNIT] = fg[...].astype(F32)
    wide[at + 1 : at + 2, 0:UNIT] = fb[...].astype(F32)
    wide[at + 2 : at + 2 + layers, 0 : 4 * UNIT] = b_in[...].astype(F32)
    base = base + 4 * UNIT
    packed[base:] = jnp.zeros((2 * UNIT, width), BF16)
    packed[base:, : wide.shape[1]] = wide[...].astype(BF16)


def pack_shards(shards):
    (g1, b1, w_qkv, bq, bv, w_ao, bao, g2, b2, w_in, b_in, w_out, bout, fg, fb, w_proj) = shards
    layers, own, _ = w_qkv.shape
    width = w_ao.shape[2]
    if own == UNIT:
        inputs = list(shards)
        inputs[13], inputs[14] = fg[None], fb[None]
        return pl.pallas_call(
            lambda *refs: pack_kernel(layers, *refs),
            out_shape=jax.ShapeDtypeStruct(((layers * LAYER_UNITS + 6) * UNIT, width), BF16),
            scratch_shapes=[pltpu.VMEM((2 * UNIT, 128), F32)],
            name="pack",
        )(*inputs)
    pieces = []
    for layer in range(layers):
        pieces += [w_out[layer]]
        pieces += [w_qkv[layer, :, i * width : (i + 1) * width] for i in range(3)]
        pieces += [w_ao[layer]]
        pieces += [w_in[layer, :, i * width : (i + 1) * width] for i in range(4)]
    pieces += [w_proj[:, i * width : (i + 1) * width] for i in range(4)]
    small = [jnp.concatenate([g1, b1, bq, bv, bao, g2, b2, bout, fg[None], fb[None]]), b_in]
    small = [jnp.pad(part, ((0, 0), (0, width - part.shape[1]))) for part in small]
    small = jnp.concatenate(small)
    small = jnp.pad(small, ((0, 2 * UNIT - small.shape[0]), (0, 0)))
    return jnp.concatenate(pieces + [small])


def piece_rows(layers, own, first_layer=0, last_layer=None):
    return [4 * own] + [own] * (LAYER_UNITS - 4)


def canonical(gathered, own, layers):
    if own == UNIT:
        return gathered
    devices, _, width = gathered.shape
    count = VECTORS * layers + 2
    pieces, at = [], 0
    for rows in piece_rows(layers, own) * layers + [own] * 4:
        pieces.append(gathered[:, at : at + rows].reshape(BLOCKS, -1, width))
        at += rows
    small = []
    for first, rows, each in ((at, count, own), (at + count, layers, 4 * own)):
        part = gathered[:, first : first + rows, :each].reshape(BLOCKS, -1, rows, each)
        part = part.transpose(0, 2, 1, 3).reshape(BLOCKS, rows, -1)
        small.append(jnp.pad(part, ((0, 0), (0, 0), (0, width - part.shape[2]))))
    small = jnp.concatenate(small, axis=1)
    pieces.append(jnp.pad(small, ((0, 0), (0, 2 * UNIT - small.shape[1]), (0, 0))))
    return jnp.concatenate(pieces, axis=1)


def to_devices(packed, devices, rows_list, vector_rows):
    if devices == BLOCKS:
        return packed
    width = packed.shape[2]
    split = devices // BLOCKS
    pieces, at = [], 0
    for rows in rows_list:
        pieces.append(packed[:, at : at + rows].reshape(devices, rows // split, width))
        at += rows
    if vector_rows:
        small = packed[:, at : at + vector_rows]
        narrow = small[:, : vector_rows - 14, :UNIT].reshape(BLOCKS, -1, split, UNIT // split)
        broad = small[:, vector_rows - 14 : vector_rows - 12, : 4 * UNIT]
        broad = broad.reshape(BLOCKS, -1, split, 4 * UNIT // split)
        parts = []
        for part in (narrow, broad):
            part = part.transpose(0, 2, 1, 3).reshape(devices, part.shape[1], part.shape[3])
            parts.append(jnp.pad(part, ((0, 0), (0, 0), (0, width - part.shape[2]))))
        small = jnp.concatenate(parts, axis=1)
        pieces.append(jnp.pad(small, ((0, 0), (0, vector_rows - small.shape[1]), (0, 0))))
    return jnp.concatenate(pieces, axis=1)


def unpack_kernel(layers, above_kept, above_got, below_kept, below_got, g_qkv, g_ao, g_in, g_out, g_proj, *vectors):
    width = above_kept.shape[2]
    above = above_kept[0].astype(F32) + above_got[...].astype(F32)
    below = below_kept[0].astype(F32) + below_got[...].astype(F32)
    for layer, ref in ((0, below), (1, above)):
        g_out[layer] = ref[: 4 * UNIT]
        for j in range(3):
            at = (4 + j) * UNIT
            g_qkv[layer, :, j * width : (j + 1) * width] = ref[at : at + UNIT]
        g_ao[layer] = ref[7 * UNIT : 8 * UNIT]
        for j in range(4):
            at = (8 + j) * UNIT
            g_in[layer, :, j * width : (j + 1) * width] = ref[at : at + UNIT]
    base = LAYER_UNITS * UNIT
    for j in range(4):
        at = base + j * UNIT
        g_proj[:, j * width : (j + 1) * width] = above[at : at + UNIT]
    small = below[base : base + 2 * UNIT, :128]
    for j in range(VECTORS):
        for i in range(layers):
            vectors[j][i : i + 1, :] = small[i * VECTORS + j : i * VECTORS + j + 1, :UNIT]
    count = VECTORS * layers
    vectors[VECTORS][...] = small[count : count + 1, :UNIT]
    vectors[VECTORS + 1][...] = small[count + 1 : count + 2, :UNIT]
    vectors[VECTORS + 2][...] = small[count + 2 : count + 2 + layers, : 4 * UNIT]


def unpack_grads(above, below, own, layers):
    width = above[0].shape[-1]
    count = VECTORS * layers
    if own == UNIT:
        shapes = [
            (layers, own, 3 * width),
            (layers, own, width),
            (layers, own, 4 * width),
            (layers, 4 * own, width),
            (own, 4 * width),
        ]
        shapes += [(layers, own)] * VECTORS + [(1, own), (1, own), (layers, 4 * own)]
        outs = pl.pallas_call(
            lambda *refs: unpack_kernel(layers, *refs),
            out_shape=[jax.ShapeDtypeStruct(shape, F32) for shape in shapes],
            name="unpack",
        )(*above, *below)
        return outs[:5], outs[5:13], outs[13][0], outs[14][0], outs[15]
    parts = []
    for ref in (below, above):
        cuts, at = [], 0
        for rows in piece_rows(layers, own):
            cuts.append(ref[at : at + rows].astype(F32))
            at += rows
        parts.append(cuts)
    mats = [
        jnp.stack([jnp.concatenate(cuts[1:4], axis=1) for cuts in parts]),
        jnp.stack([cuts[4] for cuts in parts]),
        jnp.stack([jnp.concatenate(cuts[5:9], axis=1) for cuts in parts]),
        jnp.stack([cuts[0] for cuts in parts]),
        jnp.concatenate(
            [above[at + i * own : at + (i + 1) * own].astype(F32) for i in range(4)], axis=1
        ),
    ]
    small = below[at : at + 2 * UNIT, :128].astype(F32)
    vectors = [
        jnp.stack([small[i * VECTORS + j, :own] for i in range(layers)]) for j in range(VECTORS)
    ]
    inner_bias = small[count + 2 : count + 2 + layers, : 4 * own]
    return mats, vectors, small[count, :own], small[count + 1, :own], inner_bias


def pair_swap(values, bit):
    return swap(values, "tensor", bit)


def halve_kernel(mine_a, got_a, mine_b, got_b, _after_one, _after_two, keep_a, send_a, keep_b, send_b):
    for mine, got, keep, send in ((mine_a, got_a, keep_a, send_a), (mine_b, got_b, keep_b, send_b)):
        for i, out in enumerate((keep, send)):
            out[...] = (mine[i].astype(F32) + got[i].astype(F32)).astype(BF16)


def halve_after(mine_a, got_a, mine_b, got_b, *after):
    width = mine_a.shape[-1]
    count = mine_a[0].size // (mine_a.shape[-2] * width)
    together = 2
    inputs, specs, outs, out_specs = [], [], [], []
    for mine, got in ((mine_a, got_a), (mine_b, got_b)):
        rows = mine.shape[-2]
        inputs += [part.reshape(2, count, rows, width) for part in (mine, got)]
        specs += [pl.BlockSpec((2, together, rows, width), lambda i: (0, i, 0, 0))] * 2
        outs += [jax.ShapeDtypeStruct((count, rows, width), BF16)] * 2
        out_specs += [pl.BlockSpec((together, rows, width), lambda i: (i, 0, 0))] * 2
    halves = pl.pallas_call(
        halve_kernel,
        grid=(count // together,),
        in_specs=specs + [pl.BlockSpec(memory_space=pl.ANY)] * 2,
        out_specs=out_specs,
        out_shape=outs,
        name="halve_after",
    )(*inputs, after[0], after[-1])
    shapes = [part.shape[1:] for part in (mine_a, mine_a, mine_b, mine_b)]
    return [half.reshape(shape) for half, shape in zip(halves, shapes)]


def join_kernel(kept_a, got_a, kept_b, got_b, _after_one, _after_two, rest, last):
    rows = kept_a.shape[1]
    for at, kept, got in ((slice(0, rows), kept_a, got_a), (slice(rows, None), kept_b, got_b)):
        total = (kept[...].astype(F32) + got[...].astype(F32)).astype(BF16)
        rest[:, at, :] = total[:-1]
        last[at, :] = total[-1]


def join_after(kept_a, got_a, kept_b, got_b, *after):
    line, rows_a, width = kept_a.shape
    rows = rows_a + kept_b.shape[1]
    vmem = pl.BlockSpec(memory_space=pltpu.VMEM)
    return pl.pallas_call(
        join_kernel,
        in_specs=[vmem] * 4 + [pl.BlockSpec(memory_space=pl.ANY)] * 2,
        out_specs=[vmem] * 2,
        out_shape=[
            jax.ShapeDtypeStruct((line - 1, rows, width), BF16),
            jax.ShapeDtypeStruct((rows, width), BF16),
        ],
        name="join_after",
    )(kept_a, got_a, kept_b, got_b, after[0], after[-1])


def stack_kernel(p0, p1, p2, p3, _after_one, _after_two, out):
    for k, part in enumerate((p0, p1, p2, p3)):
        out[k] = part[...]


def stack_after(parts, *after):
    vmem = pl.BlockSpec(memory_space=pltpu.VMEM)
    return pl.pallas_call(
        stack_kernel,
        in_specs=[vmem] * 4 + [pl.BlockSpec(memory_space=pl.ANY)] * 2,
        out_specs=vmem,
        out_shape=jax.ShapeDtypeStruct((4,) + parts[0].shape, parts[0].dtype),
        name="stack_after",
    )(*parts, *after)


def next_on_line(values):
    size = lax.axis_size("dp")
    return lax.ppermute(values, "dp", [(i, (i + 2) % size) for i in range(size)])


def scatter_line(rest, last):
    totals = [last]
    for ahead in (2, 1):
        got = next_on_line(totals[-1])
        totals.append((rest[ahead].astype(F32) + got.astype(F32)).astype(BF16))
    return totals[1], totals[2], next_on_line(totals[2])


def gather_line(values, *after):
    parts = [values]
    for step in range(lax.axis_size("dp") // 2 - 1):
        sent = parts[-1] if step >= len(after) else tie(parts[-1], after[step])
        parts.append(next_on_line(sent))
    return parts


def sum_grads(packed, rows_list, vector_rows):
    packed_a = jnp.stack(packed[:2]).transpose(3, 2, 1, 0, 4, 5)
    packed_b = jnp.stack(packed[2:]).transpose(3, 1, 2, 0, 4, 5)
    packed = jnp.concatenate([packed_a, packed_b], axis=4)
    packed = packed.reshape((BLOCKS,) + packed.shape[4:])
    packed = to_devices(packed, 4 * lax.axis_size("dp"), rows_list, vector_rows)
    return lax.psum_scatter(packed, BOTH, scatter_dimension=0, tiled=True)[0]


def dp_bits():
    size = lax.axis_size("dp")
    return [1 << i for i in range(size.bit_length() - 1)]


def dp_places():
    bits = dp_bits()
    return [
        sum(bit for i, bit in enumerate(reversed(bits)) if (place >> i) & 1)
        for place in range(lax.axis_size("dp"))
    ]


def gather_relative(values, first, last):
    for bit in list(reversed(dp_bits()))[first:last]:
        values = jnp.concatenate([values, swap(values, "dp", bit)])
    return values


def reduce_relative(keep, send):
    bits = dp_bits()
    first = keep = keep + swap(send, "dp", bits[0])
    for bit in bits[1:]:
        half = keep.shape[0] // 2
        keep = keep[:half] + swap(keep[half:], "dp", bit)
    return keep[0], first


def exchange_relative(first, second, third):
    return [pair_swap(first, 1), pair_swap(second, 2), pair_swap(third, 3)]


def local(
    piece_table,
    piece_ids,
    piece_counts,
    text_ids,
    cotangent,
    rms_gain_one,
    w_query,
    w_key,
    w_value,
    w_output,
    rms_gain_two,
    w_gate,
    w_up,
    w_down,
    *shard_params,
):
    tensor_index = lax.axis_index("tensor")
    dp_index = lax.axis_index("dp")
    tensor_size = lax.axis_size("tensor")
    dp_size = lax.axis_size("dp")
    devices = tensor_size * dp_size
    micro_count, group_entries, slot_count = piece_ids.shape
    own_entries = group_entries // tensor_size
    seq_length = text_ids.shape[1]
    share = cotangent.shape[1]
    layer_count, own, _ = shard_params[2].shape
    width = shard_params[5].shape[2]
    lm_width = cotangent.shape[2]
    table_rows, table_cols = piece_table.shape
    gain_first = rms_gain_one[None, :]
    gain_second = rms_gain_two[None, :]
    cosine, sine = rotary_tables(seq_length)
    trig = jnp.concatenate([cosine.T, sine.T], axis=0)
    w_kv = jnp.concatenate([w_key, w_value], axis=1)

    where = tensor_index.astype(jnp.int32)[None]

    gathered = lax.all_gather(pack_shards(shard_params), BOTH, axis=0)

    stages = len(dp_bits())
    ids_rel = gather_relative(piece_ids[None], 0, stages)
    ids_rel = ids_rel.reshape(dp_size, micro_count, tensor_size, own_entries, slot_count)
    ids_rel = jnp.take(ids_rel, tensor_index ^ jnp.arange(tensor_size), axis=2)
    ids_rel = ids_rel.transpose(0, 2, 1, 3, 4) - dp_index * table_rows
    places = jnp.asarray(dp_places())
    ids_back = jnp.zeros_like(ids_rel).at[dp_index ^ places].set(ids_rel)
    if dp_size == 8:
        behind = (dp_index + dp_size - 2 * jnp.arange(dp_size // 2)) % dp_size
        ids_back = jnp.take(ids_back, jnp.stack([behind, behind ^ 1], axis=1).reshape(-1), axis=0)
    ids_back = ids_back.reshape(4, -1)
    ids_columns = [ids[:, None] for ids in ids_back]
    ids_rel = ids_rel.reshape(2, -1)
    own_rows = micro_count * own_entries * slot_count
    looked = []
    for i in (1, 0):
        rows = lookup(ids_rel[i], piece_table, looked[0] if looked else ids_rel)
        looked.append(rows.reshape(dp_size // 2, tensor_size, own_rows, table_cols))
    near_looked = looked[1]
    looked, _ = reduce_relative(looked[1], looked[0])
    pieces = [looked[0], *exchange_relative(*looked[1:])]

    text_rel = text_ids ^ (tensor_index * own_entries)
    micros = range(micro_count)
    ids_row, ids_own, ids_peer = [], [], []
    for micro in micros:
        row = text_rel[micro][None, :]
        ids_row.append(row)
        ids_own.append(lax.dynamic_slice_in_dim(row, tensor_index * share, share, 1))
        ids_peer.append(lax.dynamic_slice_in_dim(row, (tensor_index ^ 2) * share, share, 1))
    ids_small = jnp.stack(ids_own + ids_peer)

    packed = canonical(gathered, own, layer_count)
    counts_own = lax.dynamic_slice_in_dim(piece_counts, tensor_index * own_entries, own_entries, 1)
    valid = jnp.arange(slot_count)[None, :] < counts_own.reshape(-1)[:, None]
    valid = valid.astype(F32).reshape(1, own_rows)
    w_out = [w_output, pair_swap(w_output, 1), pair_swap(w_output, 2)]
    cots = [cast_after(micro, cotangent, near_looked) for micro in range(micro_count)]
    grads_near = [
        [matmul_right_t(part, w_down).astype(BF16) for part in (cot, pair_swap(cot, 1))]
        for cot in cots
    ]
    vectors, _, *kept_hyper, pooled, pooled_norm, embeds = hyper_forward(
        where, (w_out[2], *grads_near[0], *grads_near[1], trig, ids_small, *ids_columns, ids_back), pieces, valid, packed, slot_count, layer_count
    )

    w_out.append(pair_swap(w_out[2], 1))
    embeds = embeds.reshape(micro_count, own_entries, lm_width)
    embeds = [embeds] + [pair_swap(embeds, k) for k in (1, 2, 3)]

    def peer_cot(micro, after):
        cot = pair_swap(tie(cots[micro], after), 2)
        return cot, pair_swap(cot, 1)

    cots_peer = [peer_cot(0, embeds[3])]
    kept_attn, contexts = [], []
    after = (embeds[0], embeds[0])
    for micro in micros:
        near, far, *kept = attend(
            where, micro, embeds, gain_first, w_query, w_kv, ids_row[micro], trig, after
        )
        kept_attn.append(kept)
        contexts.append([near, *exchange_relative(far, near, far)])
        after = (near, cots_peer[0][0])

    def after_attention(micro, after):
        own, peer, rows = hidden_rows_of(
            kept_attn[micro][-1], ids_own[micro], ids_peer[micro], gain_second,
            contexts[micro], w_out, after,
        )
        return (own, pair_swap(own, 1)), (peer, pair_swap(peer, 1)), rows

    def feed_forward(normed, grads_in, *after):
        after = (after + after[:1] * 2)[:3]
        return mlp(*normed, *grads_in, w_gate, w_up, w_down, after)

    def travel(part):
        from_core = jnp.concatenate([pair_swap(half, 1) for half in part[3:]])
        away = (part[2].astype(F32) + from_core.astype(F32)).astype(BF16)
        return away, pair_swap(away, 2)

    def back_of(micro, rows, near, arrived):
        low, *parts = hidden_back(
            micro, cotangent, rows, near[2], [pair_swap(half, 1) for half in near[3:]], arrived,
            gain_second, w_out,
        )
        return low, [parts[0], *exchange_relative(*parts[1:])]

    def send_result(peer, after):
        total = (peer[0].astype(F32) + pair_swap(peer[1], 1).astype(F32)).astype(BF16)
        return pair_swap(tie(total, after), 2)

    near_in, peer_in, rows_a = after_attention(0, (contexts[1][0], contexts[1][0]))
    near_a = feed_forward(near_in, grads_near[0], rows_a)
    cots_peer.append(peer_cot(1, near_a[2]))
    peer_a = feed_forward(peer_in, cots_peer[0], near_a[2], contexts[1][2], contexts[1][3])
    away_a, arrived_a = travel(peer_a)
    near_in, peer_in, rows_b = after_attention(1, (away_a, cots_peer[1][0]))
    peer_b = feed_forward(peer_in, cots_peer[1], rows_b)
    away_b, arrived_b = travel(peer_b)
    low_a, parts_a = back_of(0, rows_a, near_a, arrived_a)
    near_b = feed_forward(near_in, grads_near[1], low_a, away_b)
    result_a = send_result(peer_a, near_b[2])
    low_b, parts_b = back_of(1, rows_b, near_b, arrived_b)

    place = jnp.stack([tensor_index % 2, tensor_index // 2, dp_index % 2, dp_index // 2])
    place = place.astype(jnp.int32)
    grad_embeds = []
    after = (low_b,) * 5
    near_swapped = [pair_swap(near[1], 1) for near in (near_a, near_b)]
    for micro, parts, low in ((0, parts_a, low_a), (1, parts_b, low_b)):
        grads = attend_back(
            where, parts, kept_attn[micro], ids_row[micro], ids_own[micro], trig,
            w_query, w_kv, gain_first, low, after,
        )
        after = (grads[0], result_a, parts_b[2], *near_swapped)
        if micro == 0:
            result_b = send_result(peer_b, grads[0])
        grad_embeds += [grads[0], *exchange_relative(*grads[1:])]

    if dp_size != 8:
        place = place * 0
    source = (grad_embeds, pooled, pooled_norm)
    packs, above, after = [None] * layer_count, (), (result_b, result_b)
    near_side, near_chip = ("dp", 1), ("tensor", 2)
    for layer in range(layer_count - 1, -1, -1):
        *parts, source, small, inner_small = hyper_backward(
            place, layer, source, valid, vectors, kept_hyper, packed, slot_count, above,
            table_cols, after,
        )
        above = (small, inner_small)
        packs[layer] = parts
        if dp_size == 8 and layer == layer_count - 1:
            upper = halve_after(
                parts[0], pair_swap(parts[1], 1), parts[2], pair_swap(parts[3], 1), small
            )
            after = (upper[1], upper[3])
    if dp_size == 8:
        parts = packs[0]
        from_chip = pair_swap(source[2:], 2)
        results = add_results(
            (rows_a, near_a[0], near_swapped[0], result_a),
            (rows_b, near_b[0], near_swapped[1], result_b),
            parts[0],
        )
        upper = halve_after(
            upper[0], swap(upper[1], *near_chip), upper[2], swap(upper[3], *near_side), results
        )
        upper_got = swap(upper[3], *near_chip)
        other_a, other_b = tie(parts[1], upper[1]), tie(parts[3], upper[1])
        from_chip = pair_swap(source[2:], 2)
        lower = halve_after(
            parts[0], pair_swap(other_a, 1), parts[2], pair_swap(other_b, 1), upper[1]
        )
        near_piece, forward = tie(source[1], lower[1]), tie(from_chip[1], lower[1])
        pieces = [source[0], pair_swap(near_piece, 1), from_chip[0], pair_swap(forward, 1)]
        pieces = stack_after(pieces, upper_got, lower[1])
        upper_rest, last = join_after(
            upper[0], swap(upper[1], *near_side), upper[2], upper_got, pieces
        )
        sent = [tie(lower[1], last), tie(lower[3], last)]
        pieces = gather_line(jnp.stack([pieces, swap(pieces, "dp", 1)]), last)
        pieces = [part.reshape(-1, table_cols) for part in pieces]
        step_one, step_two, upper_got = scatter_line(upper_rest, last)
        table_grad = collect(ids_back[:2], ids_columns[:2], pieces[0], pieces[1], table_rows, None)
        lower = halve_after(
            lower[0], swap(sent[0], *near_chip), lower[2], swap(sent[1], *near_side), last
        )
        lower_rest, last = join_after(
            lower[0], swap(lower[1], *near_side), lower[2], swap(lower[3], *near_chip), table_grad, step_two
        )
        *_, lower_got = scatter_line(lower_rest, last)
        reduced = [(lower_rest, lower_got), (upper_rest, upper_got)]
    else:
        pieces = jnp.take(source, tensor_index ^ jnp.arange(tensor_size), axis=0)
        pieces = jnp.stack([pieces[0], *exchange_relative(*pieces[1:])])
        pieces = lax.all_gather(pieces, "dp", axis=0).reshape(4, -1, table_cols)
        rows_list = piece_rows(layer_count, UNIT)
        reduced = [
            sum_grads(packs[0], rows_list, 2 * UNIT),
            sum_grads(packs[1], rows_list + [UNIT] * 4, 0),
        ]
        table_grad = collect(ids_back[:2], ids_columns[:2], pieces[0], pieces[1], table_rows, None)
        results = add_results(
            (rows_a, near_a[0], near_swapped[0], result_a),
            (rows_b, near_b[0], near_swapped[1], result_b),
            table_grad,
        )
    table_grad = collect(ids_back[2:], ids_columns[2:], pieces[2], pieces[3], table_rows, table_grad)

    mats, vecs, out_final_gain, out_final_bias, out_inner_bias = unpack_grads(
        reduced[1], reduced[0], own, layer_count
    )
    return (
        results,
        table_grad,
        vecs[0],
        vecs[1],
        mats[0],
        vecs[2],
        vecs[3],
        mats[1],
        vecs[4],
        vecs[5],
        vecs[6],
        mats[2],
        out_inner_bias,
        mats[3],
        vecs[7],
        out_final_gain,
        out_final_bias,
        mats[4],
    )


def solution(mesh):
    return jax.shard_map(
        local,
        mesh=mesh,
        in_specs=(
            P("dp", "tensor"),
            P(None, "dp", None),
            P(None, "dp"),
            P(None, "dp"),
            P(None, ("dp", "tensor"), None),
            P(),
            P(None, "tensor"),
            P(None, "tensor"),
            P(None, "tensor"),
            P("tensor", None),
            P(),
            P(None, "tensor"),
            P(None, "tensor"),
            P("tensor", None),
            P(None, ("dp", "tensor")),
            P(None, ("dp", "tensor")),
            P(None, ("dp", "tensor"), None),
            P(None, ("dp", "tensor")),
            P(None, ("dp", "tensor")),
            P(None, ("dp", "tensor"), None),
            P(None, ("dp", "tensor")),
            P(None, ("dp", "tensor")),
            P(None, ("dp", "tensor")),
            P(None, ("dp", "tensor"), None),
            P(None, ("dp", "tensor")),
            P(None, ("dp", "tensor"), None),
            P(None, ("dp", "tensor")),
            P(("dp", "tensor")),
            P(("dp", "tensor")),
            P(("dp", "tensor"), None),
        ),
        out_specs=(
            P(None, ("dp", "tensor"), None),
            P("dp", "tensor"),
            P(None, ("dp", "tensor")),
            P(None, ("dp", "tensor")),
            P(None, ("dp", "tensor"), None),
            P(None, ("dp", "tensor")),
            P(None, ("dp", "tensor")),
            P(None, ("dp", "tensor"), None),
            P(None, ("dp", "tensor")),
            P(None, ("dp", "tensor")),
            P(None, ("dp", "tensor")),
            P(None, ("dp", "tensor"), None),
            P(None, ("dp", "tensor")),
            P(None, ("dp", "tensor"), None),
            P(None, ("dp", "tensor")),
            P(("dp", "tensor")),
            P(("dp", "tensor")),
            P(("dp", "tensor"), None),
        ),
        check_vma=False,
    )
```

```python
import jax
import jax.numpy as jnp
from jax import lax
from jax.experimental import pallas as pl
from jax.experimental.pallas import tpu as pltpu
from jax.sharding import PartitionSpec as P

HEAD_DIM = 64
EPS_NORM = 1e-05
HIGH = lax.Precision.HIGHEST
SQRT_HALF = 0.7071067811865476
INV_SQRT_TAU = 0.3989422804014327
BOTH = ("dp", "tensor")
F32 = jnp.float32
BF16 = jnp.bfloat16


def matmul(left, right):
    return jnp.dot(left, right, preferred_element_type=F32)


def matmul_right_t(left, right):
    return lax.dot_general(left, right, (((1,), (1,)), ((), ())), preferred_element_type=F32)


def matmul_left_t(left, right):
    return lax.dot_general(left, right, (((0,), (0,)), ((), ())), preferred_element_type=F32)


def norm_parts(values):
    centered = values - jnp.mean(values, axis=-1, keepdims=True)
    inverse = lax.rsqrt(jnp.mean(centered * centered, axis=-1, keepdims=True) + EPS_NORM)
    return (centered * inverse, inverse)


def norm_back(normed, inverse, grad_scaled):
    return inverse * (
        grad_scaled
        - jnp.mean(grad_scaled, axis=-1, keepdims=True)
        - normed * jnp.mean(grad_scaled * normed, axis=-1, keepdims=True)
    )


def rms_parts(values):
    return lax.rsqrt(jnp.mean(values * values, axis=-1, keepdims=True) + EPS_NORM)


def rms_back(values, inverse, grad_scaled):
    return inverse * grad_scaled - values * inverse**3 * jnp.mean(
        grad_scaled * values, axis=-1, keepdims=True
    )


def rotary_tables(seq_length):
    half_dim = HEAD_DIM // 2
    freqs = 10000.0 ** (-jnp.arange(half_dim, dtype=F32) * 2.0 / HEAD_DIM)
    angles = jnp.arange(seq_length, dtype=F32)[:, None] * freqs[None, :]
    angles = jnp.concatenate([angles, angles], axis=-1)
    return (jnp.cos(angles), jnp.sin(angles))


def swap(values, axis, bit):
    size = lax.axis_size(axis)
    return lax.ppermute(values, axis, [(i, i ^ bit) for i in range(size)])


def lookup_kernel(ids_ref, table_ref, _after, out_ref):
    rows = ids_ref.shape[0]
    height, width = table_ref.shape
    half = height // 2
    ids = ids_ref[...]
    upper = ids >= half
    places = jnp.where(upper, ids - half, ids)
    chosen = places == lax.broadcasted_iota(jnp.int32, (rows, half), 1)
    pairs = jnp.concatenate([table_ref[:half], table_ref[half:]], axis=1)
    found = matmul(jnp.where(chosen, 1.0, 0.0).astype(BF16), pairs)
    out_ref[...] = jnp.where(upper, found[:, width:], found[:, :width]).astype(BF16)


def lookup(ids, table, after):
    count = ids.shape[0]
    height, width = table.shape
    rows = 512
    return pl.pallas_call(
        lookup_kernel,
        grid=(count // rows,),
        in_specs=[
            pl.BlockSpec((rows, 1), lambda i: (i, 0)),
            pl.BlockSpec((height, width), lambda i: (0, 0)),
            pl.BlockSpec(memory_space=pl.ANY),
        ],
        out_specs=pl.BlockSpec((rows, width), lambda i: (i, 0)),
        out_shape=jax.ShapeDtypeStruct((count, width), BF16),
        compiler_params=pltpu.CompilerParams(vmem_limit_bytes=48 << 20),
        cost_estimate=pl.CostEstimate(
            flops=4 * count * height * width, bytes_accessed=4 * count * width, transcendentals=0
        ),
        name="lookup",
    )(ids[:, None], table, after)


def collect_kernel(ids_ref, ids_left, ids_right, left_ref, right_ref, base_ref, out_ref):
    @pl.when(pl.program_id(0) == 0)
    def _():
        out_ref[...] = jnp.zeros_like(out_ref) if base_ref is None else base_ref[...]

    height, width = out_ref.shape
    half = height // 2
    total = None
    for i, (column, rows_ref) in enumerate(((ids_left, left_ref), (ids_right, right_ref))):
        ids = ids_ref[i : i + 1, :]
        ids = jnp.where(ids >= half, ids - half, ids)
        places = lax.broadcasted_iota(jnp.int32, (half, ids.shape[1]), 0)
        chosen = jnp.where(ids == places, 1.0, 0.0).astype(BF16)
        rows = rows_ref[...].astype(F32)
        upper = column[...] >= half
        pairs = [jnp.where(upper, 0.0, rows), jnp.where(upper, rows, 0.0)]
        part = matmul(chosen, jnp.concatenate(pairs, axis=1).astype(BF16))
        total = part if total is None else total + part
    out_ref[:half] += total[:, :width]
    out_ref[half:] += total[:, width:]


def collect(ids, columns, left, right, height, base):
    count, width = left.shape
    rows = 256
    whole = pl.BlockSpec((height, width), lambda i: (0, 0))
    kernel = collect_kernel
    if base is None:
        kernel = lambda *refs: collect_kernel(*refs[:5], None, refs[5])
    return pl.pallas_call(
        kernel,
        grid=(count // rows,),
        in_specs=[pl.BlockSpec((2, rows), lambda i: (0, i))]
        + [pl.BlockSpec((rows, 1), lambda i: (i, 0))] * 2
        + [pl.BlockSpec((rows, width), lambda i: (i, 0))] * 2
        + ([] if base is None else [whole]),
        out_specs=whole,
        out_shape=jax.ShapeDtypeStruct((height, width), F32),
        compiler_params=pltpu.CompilerParams(vmem_limit_bytes=48 << 20),
        cost_estimate=pl.CostEstimate(
            flops=8 * count * height * width, bytes_accessed=8 * count * width, transcendentals=0
        ),
        name="collect",
    )(ids, *columns, left, right, *([] if base is None else [base]))


QUERY_ROWS = 256
ENTRY_LANES = 64
VMEM_LIMIT = 56 << 20


def turn_rows(values):
    half_dim = HEAD_DIM // 2
    return jnp.concatenate([-values[half_dim:], values[:half_dim]], axis=0)


def two_parts(values):
    high = values.astype(BF16)
    return jnp.concatenate([high, (values - high.astype(F32)).astype(BF16)], axis=1)


def entry_table(columns):
    return two_parts(jnp.concatenate([columns, turn_rows(columns)], axis=0))


def spread(table, onehot, trig):
    both = matmul(table, onehot) * trig
    return both[:HEAD_DIM] + both[HEAD_DIM:]


def ahead_mask(rows):
    shape = (rows, rows)
    return lax.broadcasted_iota(jnp.int32, shape, 0) <= lax.broadcasted_iota(jnp.int32, shape, 1)


def attend_kernel(
    place, part0, part1, part2, part3, gain, w_query, w_kv, ids, trig, _after_one, _after_two,
    near, far, context_t, log_total, table_q, table_kv, embeds,
    normed, onehot, keys, values_t,
):
    tokens = ids.shape[1]

    @pl.when(pl.program_id(0) == 0)
    def _():
        own = part0.shape[1]
        for k, part in enumerate((part0, part1, part2, part3)):
            embeds[k * own : (k + 1) * own, :] = part[0]
        wide = embeds[...].astype(F32)
        normed[...] = (wide * rms_parts(wide) * gain[...].astype(F32)).astype(BF16)
        places = lax.broadcasted_iota(jnp.int32, onehot.shape, 0)
        places = jnp.where(places >= ENTRY_LANES, places - ENTRY_LANES, places)
        onehot[...] = jnp.where(places == ids[...], 1.0, 0.0).astype(BF16)
        mixed = matmul(normed[...], w_kv[...]).T
        table_kv[0] = entry_table(mixed[:HEAD_DIM])
        table_kv[1] = entry_table(mixed[HEAD_DIM:])
        keys[...] = spread(table_kv[0], onehot[...], trig[...]).T.astype(BF16)
        values_t[...] = matmul(table_kv[1], onehot[...])[:HEAD_DIM].astype(BF16)

    queries = matmul(normed[...], w_query[...]).T * HEAD_DIM ** (-0.5)
    ahead = ahead_mask(QUERY_ROWS)
    turned = []
    for j in range(2):
        table_q[0, j] = entry_table(queries[j * HEAD_DIM : (j + 1) * HEAD_DIM])
        turned.append(spread(table_q[0, j], onehot[...], trig[...]).astype(BF16))
    odd = place[0] % 2
    rows_out = []

    def score(block):
        start, stop = block * QUERY_ROWS, (block + 1) * QUERY_ROWS
        return [matmul(keys[:stop], turned[j][:, start:stop]) for j in range(2)]

    blocks = tokens // QUERY_ROWS
    scores = score(0)
    for block in range(blocks):
        start, stop = block * QUERY_ROWS, (block + 1) * QUERY_ROWS
        following = score(block + 1) if block + 1 < blocks else None
        done = []
        for j in range(2):
            last = jnp.where(ahead, scores[j][start:], -1e30)
            highest = jnp.max(last, axis=0, keepdims=True)
            if block:
                highest = jnp.maximum(highest, jnp.max(scores[j][:start], axis=0, keepdims=True))
            last = jnp.exp(last - highest)
            total = jnp.sum(last, axis=0, keepdims=True)
            soft = last.astype(BF16)
            if block:
                first = jnp.exp(scores[j][:start] - highest)
                total = total + jnp.sum(first, axis=0, keepdims=True)
                soft = jnp.concatenate([first.astype(BF16), soft], axis=0)
            done.append(matmul(values_t[:, :stop], soft) / total)
            log_total[0, j : j + 1, start:stop] = highest + jnp.log(total)
        scores = following
        done = jnp.concatenate(done, axis=0)
        context_t[:, start:stop] = done.astype(BF16)
        rows_out.append(done.T.astype(BF16))
        if block % 2:
            even_rows, odd_rows = rows_out[-2:]
            target = (block // 2) ^ (place[0] // 2)
            near[target] = jnp.where(odd == 0, even_rows, odd_rows)
            far[target] = jnp.where(odd == 0, odd_rows, even_rows)


def attend(place, micro, parts, gain, w_query, w_kv, ids, trig, after):
    assert ids.shape[1] == 4 * QUERY_ROWS
    _, own, width = parts[0].shape
    entries = own * len(parts)
    tokens = ids.shape[1]
    pairs = w_query.shape[1] // (2 * HEAD_DIM)
    lanes = 2 * HEAD_DIM
    whole = lambda *shape: pl.BlockSpec(shape, lambda i: (0,) * len(shape))
    return pl.pallas_call(
        attend_kernel,
        grid=(pairs,),
        in_specs=[pl.BlockSpec(memory_space=pltpu.SMEM)]
        + [pl.BlockSpec((1, own, width), lambda i: (micro, 0, 0))] * len(parts)
        + [
            whole(1, width),
            pl.BlockSpec((width, lanes), lambda i: (0, i)),
            whole(width, lanes),
            whole(1, tokens),
            whole(lanes, tokens),
        ]
        + [pl.BlockSpec(memory_space=pl.ANY)] * 2,
        out_specs=[
            pl.BlockSpec((2, QUERY_ROWS, lanes), lambda i: (0, 0, i)),
            pl.BlockSpec((2, QUERY_ROWS, lanes), lambda i: (0, 0, i)),
            pl.BlockSpec((lanes, tokens), lambda i: (i, 0)),
            pl.BlockSpec((1, 2, tokens), lambda i: (i, 0, 0)),
            pl.BlockSpec((1, 2, lanes, lanes), lambda i: (i, 0, 0, 0)),
            whole(2, lanes, lanes),
            whole(entries, width),
        ],
        out_shape=[
            jax.ShapeDtypeStruct((2, QUERY_ROWS, pairs * lanes), BF16),
            jax.ShapeDtypeStruct((2, QUERY_ROWS, pairs * lanes), BF16),
            jax.ShapeDtypeStruct((pairs * lanes, tokens), BF16),
            jax.ShapeDtypeStruct((pairs, 2, tokens), F32),
            jax.ShapeDtypeStruct((pairs, 2, lanes, lanes), BF16),
            jax.ShapeDtypeStruct((2, lanes, lanes), BF16),
            jax.ShapeDtypeStruct((entries, width), BF16),
        ],
        scratch_shapes=[
            pltpu.VMEM((entries, width), BF16),
            pltpu.VMEM((lanes, tokens), BF16),
            pltpu.VMEM((tokens, HEAD_DIM), BF16),
            pltpu.VMEM((HEAD_DIM, tokens), BF16),
        ],
        compiler_params=pltpu.CompilerParams(vmem_limit_bytes=VMEM_LIMIT),
        cost_estimate=pl.CostEstimate(
            flops=12 * 10**9, bytes_accessed=8 * 10**6, transcendentals=5 * 10**6
        ),
        name="attend",
    )(place, *parts, gain, w_query, w_kv, ids, trig, *after)


def attend_back_kernel(
    place, part0, part1, part2, part3, context_t, log_total, table_q, table_kv, ids, ids_share, trig,
    w_query, w_kv, embeds, gain, grad_hidden, _a0, _a1, _a2, _a3, _a4, grads0, grads1, grads2, grads3,
    onehot, columns, keys, keys_t, values, grad_keys, grad_values, total, grad_context,
):
    tokens = ids.shape[1]
    share = part0.shape[0]
    for k, part in enumerate((part0, part1, part2, part3)):
        first = pl.multiple_of((place[0] ^ k) * share, share)
        grad_context[pl.ds(first, share), :] = part[...]
    entries = embeds.shape[0]
    cosine, sine = trig[:HEAD_DIM], trig[HEAD_DIM:]

    @pl.when(pl.program_id(0) == 0)
    def _():
        places = lax.broadcasted_iota(jnp.int32, onehot.shape, 0)
        places = jnp.where(places >= ENTRY_LANES, places - ENTRY_LANES, places)
        chosen = jnp.where(places == ids[...], 1.0, 0.0)
        onehot[...] = chosen.astype(BF16)
        columns[...] = chosen.T.astype(BF16)
        turned = spread(table_kv[0], onehot[...], trig[...])
        keys_t[...] = turned.astype(BF16)
        keys[...] = turned.T.astype(BF16)
        values[...] = matmul(table_kv[1], onehot[...])[:HEAD_DIM].T.astype(BF16)
        grad_keys[...] = jnp.zeros_like(grad_keys)
        grad_values[...] = jnp.zeros_like(grad_values)
        total[...] = jnp.zeros_like(total)

    def to_entries(grads, cos_part, sin_part, rows):
        straight = matmul((grads * cos_part).astype(BF16), rows)
        crossed = matmul((grads * sin_part).astype(BF16), rows)
        return straight, crossed

    def two_stacked(grads):
        high = grads.astype(BF16)
        rest = (grads - high.astype(F32)).astype(BF16)
        lane = lax.broadcasted_iota(jnp.int32, grads.shape, 1)
        return jnp.where(lane < ENTRY_LANES, high.astype(F32), rest.astype(F32)).T.astype(BF16)

    ahead = ahead_mask(QUERY_ROWS)
    grad_t = grad_context[...].astype(F32).T
    products = grad_t * context_t[...].astype(F32)
    grad_t = grad_t.astype(BF16)
    heads = [slice(j * HEAD_DIM, (j + 1) * HEAD_DIM) for j in range(2)]
    turned = [spread(table_q[0, j], onehot[...], trig[...]) for j in range(2)]
    queries_t = [part.astype(BF16) for part in turned]
    queries = [part.T.astype(BF16) for part in turned]
    offset = [jnp.sum(products[head], axis=0, keepdims=True) for head in heads]
    turned_back = [[], []]

    def score(block, j):
        start, stop = block * QUERY_ROWS, (block + 1) * QUERY_ROWS
        return (
            matmul(keys[:stop], queries_t[j][:, start:stop]),
            matmul(values[:stop], grad_t[heads[j], start:stop]),
        )

    order = [(block, j) for block in range(tokens // QUERY_ROWS) for j in range(2)]
    sums = [[None, None] for _ in range(tokens // QUERY_ROWS)]

    def weigh(block, j, scores, grad_soft):
        start, stop = block * QUERY_ROWS, (block + 1) * QUERY_ROWS
        soft = jnp.exp(scores - log_total[0, j : j + 1, start:stop])
        last = jnp.where(ahead, soft[start:], 0.0)
        soft = jnp.concatenate([soft[:start], last], axis=0) if block else last
        grad_scores = (soft * (grad_soft - offset[j][:, start:stop])).astype(BF16)
        return soft.astype(BF16), grad_scores

    def gather_up(block, j, soft, grad_scores):
        start, stop = block * QUERY_ROWS, (block + 1) * QUERY_ROWS
        for kind, part in enumerate(
            (
                matmul(soft, grad_context[start:stop, heads[j]]),
                matmul(grad_scores, queries[j][start:stop]),
            )
        ):
            for i in range(block + 1):
                piece = part[i * QUERY_ROWS : (i + 1) * QUERY_ROWS]
                held = sums[i][kind]
                sums[i][kind] = piece if held is None else held + piece
        grad_queries = matmul(keys_t[:, :stop], grad_scores) * HEAD_DIM ** (-0.5)
        turned_back[j].append(
            jnp.concatenate(
                [grad_queries * cosine[:, start:stop], grad_queries * sine[:, start:stop]], axis=0
            ).astype(BF16)
        )

    ready = score(*order[0])
    waiting = None
    for i, item in enumerate(order):
        current = ready
        ready = score(*order[i + 1]) if i + 1 < len(order) else None
        if waiting is not None:
            gather_up(*waiting)
        waiting = (*item, *weigh(*item, *current))
    gather_up(*waiting)
    for i, (value_sum, key_sum) in enumerate(sums):
        lines = slice(i * QUERY_ROWS, (i + 1) * QUERY_ROWS)
        grad_values[lines] += value_sum
        grad_keys[lines] += key_sum
    both = jnp.concatenate([jnp.concatenate(parts, axis=1) for parts in turned_back], axis=0)
    both = matmul(both, columns[...])
    per_head = []
    for j in range(2):
        at = 2 * HEAD_DIM * j
        straight, crossed = both[at : at + HEAD_DIM], both[at + HEAD_DIM : at + 2 * HEAD_DIM]
        per_head.append(straight - turn_rows(crossed))
    total[...] += matmul_right_t(two_stacked(jnp.concatenate(per_head, axis=0)), w_query[...])

    @pl.when(pl.program_id(0) == pl.num_programs(0) - 1)
    def _():
        grads = jnp.concatenate([grad_keys[...], grad_values[...]], axis=1).T
        straight, crossed = to_entries(grads[:HEAD_DIM], cosine, sine, columns[...])
        summed = matmul(grads[HEAD_DIM:].astype(BF16), columns[...])
        both = jnp.concatenate([straight - turn_rows(crossed), summed], axis=0)
        full = total[...] + matmul_right_t(two_stacked(both), w_kv[...])
        scaled = (full[:entries] + full[entries:]) * gain[...].astype(F32)
        wide = embeds[...].astype(F32)
        places = lax.broadcasted_iota(jnp.int32, (entries, ids_share.shape[1]), 0)
        chosen = jnp.where(places == ids_share[...], 1.0, 0.0).astype(BF16)
        result = rms_back(wide, rms_parts(wide), scaled) + matmul(chosen, grad_hidden[...])
        result = result.astype(BF16)
        own = grads0.shape[0]
        for k, out in enumerate((grads0, grads1, grads2, grads3)):
            out[...] = result[k * own : (k + 1) * own]


def attend_back(
    place, parts, kept, ids, ids_share, trig, w_query, w_kv, gain, grad_hidden, after
):
    context_t, log_total, table_q, table_kv, embeds = kept
    share = parts[0].shape[0]
    entries, width = embeds.shape
    tokens = ids.shape[1]
    pairs = w_query.shape[1] // (2 * HEAD_DIM)
    lanes = 2 * HEAD_DIM
    whole = lambda *shape: pl.BlockSpec(shape, lambda i: (0,) * len(shape))
    return pl.pallas_call(
        attend_back_kernel,
        grid=(pairs,),
        in_specs=[pl.BlockSpec(memory_space=pltpu.SMEM)]
        + [pl.BlockSpec((share, lanes), lambda i: (0, i))] * len(parts)
        + [
            pl.BlockSpec((lanes, tokens), lambda i: (i, 0)),
            pl.BlockSpec((1, 2, tokens), lambda i: (i, 0, 0)),
            pl.BlockSpec((1, 2, lanes, lanes), lambda i: (i, 0, 0, 0)),
            whole(2, lanes, lanes),
            whole(1, tokens),
            whole(*ids_share.shape),
            whole(lanes, tokens),
            pl.BlockSpec((width, lanes), lambda i: (0, i)),
            whole(width, lanes),
            whole(entries, width),
            whole(1, width),
            whole(*grad_hidden.shape),
        ]
        + [pl.BlockSpec(memory_space=pl.ANY)] * 5,
        out_specs=[whole(entries // 4, width)] * 4,
        out_shape=[jax.ShapeDtypeStruct((entries // 4, width), BF16)] * 4,
        scratch_shapes=[
            pltpu.VMEM((lanes, tokens), BF16),
            pltpu.VMEM((tokens, lanes), BF16),
            pltpu.VMEM((tokens, HEAD_DIM), BF16),
            pltpu.VMEM((HEAD_DIM, tokens), BF16),
            pltpu.VMEM((tokens, HEAD_DIM), BF16),
            pltpu.VMEM((tokens, HEAD_DIM), F32),
            pltpu.VMEM((tokens, HEAD_DIM), F32),
            pltpu.VMEM((2 * entries, width), F32),
            pltpu.VMEM((tokens, lanes), BF16),
        ],
        compiler_params=pltpu.CompilerParams(vmem_limit_bytes=VMEM_LIMIT),
        cost_estimate=pl.CostEstimate(
            flops=25 * 10**9, bytes_accessed=8 * 10**6, transcendentals=5 * 10**6
        ),
        name="attend_back",
    )(
        place, *parts, context_t, log_total, table_q, table_kv, ids, ids_share, trig,
        w_query, w_kv, embeds, gain, grad_hidden, *after,
    )


ANY_SPEC = pl.BlockSpec(memory_space=pl.ANY)


def pick_rows(ids, entries):
    places = lax.broadcasted_iota(jnp.int32, (entries, ids.shape[1]), 0)
    return jnp.where(places == ids[...], 1.0, 0.0).astype(BF16)


def load_weights(sources, targets, sems):
    copies = [
        pltpu.make_async_copy(source, target, sems.at[i])
        for i, (source, target) in enumerate(zip(sources, targets))
    ]
    for copy in copies:
        copy.start()
    return copies


def hidden_kernel(
    embeds, ids_own, ids_peer, gain, c0, c1, c2, c3, w0, w1, w2, w3, _after_one, _after_two,
    normed_own, normed_peer, hidden, held, sems,
):
    heads = w0.shape[0]
    copies = load_weights(
        (w0, w1, w2, w3), [held.at[pl.ds(k * heads, heads)] for k in range(4)], sems
    )
    rows = jnp.concatenate([pick_rows(ids_own, embeds.shape[0]), pick_rows(ids_peer, embeds.shape[0])], axis=1)
    total = matmul_left_t(rows, embeds[...])
    for first, (left, right) in ((0, (c0, c1)), (2, (c2, c3))):
        own = first // 2
        sides = [jnp.concatenate([part[own], part[1 - own]], axis=0) for part in (left, right)]
        copies[first].wait()
        copies[first + 1].wait()
        both = jnp.concatenate(sides, axis=1)
        total = total + matmul(both, held[first * heads : (first + 2) * heads])
    low = (total * rms_parts(total) * gain[...].astype(F32)).astype(BF16)
    share = normed_own.shape[0]
    normed_own[...] = low[:share]
    normed_peer[...] = low[share:]
    hidden[...] = total[:share]


def hidden_rows_of(embeds, ids_own, ids_peer, gain, parts, weights, after):
    rows, width = ids_own.shape[1], embeds.shape[1]
    vmem = pl.BlockSpec(memory_space=pltpu.VMEM)
    return pl.pallas_call(
        hidden_kernel,
        in_specs=[vmem] * 8 + [ANY_SPEC] * 6,
        out_specs=[vmem] * 3,
        out_shape=[
            jax.ShapeDtypeStruct((rows, width), BF16),
            jax.ShapeDtypeStruct((rows, width), BF16),
            jax.ShapeDtypeStruct((rows, width), F32),
        ],
        scratch_shapes=[
            pltpu.VMEM((4 * weights[0].shape[0], width), BF16),
            pltpu.SemaphoreType.DMA((4,)),
        ],
        compiler_params=pltpu.CompilerParams(vmem_limit_bytes=VMEM_LIMIT),
        cost_estimate=pl.CostEstimate(
            flops=6 * 10**9, bytes_accessed=18 * 10**6, transcendentals=0
        ),
        name="hidden",
    )(embeds, ids_own, ids_peer, gain, *parts, *weights, *after)


def hidden_back_kernel(
    cotangent, hidden, kept, core_a, core_b, from_chip, gain, w0, w1, w2, w3,
    low, p0, p1, p2, p3, held, sems,
):
    copies = load_weights((w2, w3, w1, w0), [held.at[k] for k in range(4)], sems)
    from_core = jnp.concatenate([core_a[...], core_b[...]], axis=0)
    grads = kept[...].astype(F32) + from_core.astype(F32) + from_chip[...].astype(F32)
    rows = hidden[...]
    scaled = grads * gain[...].astype(F32)
    total = cotangent[0] + rms_back(rows, rms_parts(rows), scaled)
    total = total.astype(BF16)
    low[...] = total
    for k, part in enumerate((p2, p3, p1, p0)):
        copies[k].wait()
        part[...] = matmul_right_t(total, held[k]).astype(BF16)


def hidden_back(micro, cotangent, hidden, kept, from_core, from_chip, gain, weights):
    rows, width = hidden.shape
    heads = weights[0].shape[0]
    whole = lambda *shape: pl.BlockSpec(shape, lambda i: (0,) * len(shape))
    return pl.pallas_call(
        hidden_back_kernel,
        grid=(1,),
        in_specs=[
            pl.BlockSpec((1, rows, width), lambda i: (micro, 0, 0)),
            whole(rows, width),
            whole(rows, width),
            whole(rows // 2, width),
            whole(rows // 2, width),
            whole(rows, width),
            whole(1, width),
        ]
        + [ANY_SPEC] * 4,
        out_specs=[whole(rows, width)] + [whole(rows, heads)] * 4,
        out_shape=[jax.ShapeDtypeStruct((rows, width), BF16)]
        + [jax.ShapeDtypeStruct((rows, heads), BF16)] * 4,
        scratch_shapes=[
            pltpu.VMEM((4, heads, width), BF16),
            pltpu.SemaphoreType.DMA((4,)),
        ],
        compiler_params=pltpu.CompilerParams(vmem_limit_bytes=VMEM_LIMIT),
        cost_estimate=pl.CostEstimate(
            flops=2 * 10**9, bytes_accessed=16 * 10**6, transcendentals=0
        ),
        name="hidden_back",
    )(cotangent, hidden, kept, *from_core, from_chip, gain, *weights)


def mlp_kernel(
    ready, x_mine, x_other, mine_in, other_in, gate_hbm, up_hbm, down_hbm,
    _after_one, _after_two, _after_three,
    out_mine, out_other, grad_mine, grad_a, grad_b,
    w_both, w_down, sems,
):
    units = w_down.shape[0]
    main = units // 256 * 256
    rest = units - main
    cuts = ((0, gate_hbm, 0, main), (main, up_hbm, 0, main), (2 * main, gate_hbm, main, rest),
            (2 * main + rest, up_hbm, main, rest))
    copies = load_weights(
        [source.at[:, pl.ds(at, size)] for _, source, at, size in cuts if size] + [down_hbm],
        [w_both.at[:, pl.ds(to, size)] for to, _, _, size in cuts if size] + [w_down],
        sems,
    )
    halves = ((x_other, other_in), (x_mine, mine_in))
    copies[0].wait()
    gates = [matmul(rows[...], w_both[:, :main]) for rows, _ in halves]
    for copy in copies[1:-1]:
        copy.wait()
    others = [matmul(rows[...], w_both[:, main:]) for rows, _ in halves]
    copies[-1].wait()
    if ready:
        grads_active = [cots[...].astype(F32) for _, cots in halves]
    else:
        grads_active = [matmul_right_t(cots[...], w_down[...]) for _, cots in halves]
    middle = []
    for gate, other, grad_active in zip(gates, others, grads_active):
        gate = jnp.concatenate([gate, other[:, main : main + rest]], axis=1)
        upward = jnp.concatenate([other[:, :main], other[:, main + rest :]], axis=1)
        sigmoid = 1.0 / (1.0 + jnp.exp(-gate))
        silu = gate * sigmoid
        activated = (silu * upward).astype(BF16)
        grad_gate = grad_active * upward * (sigmoid * (1.0 + gate * (1.0 - sigmoid)))
        grad_gate = grad_gate.astype(BF16)
        grad_up = (grad_active * silu).astype(BF16)
        parts = [grad_gate[:, :main], grad_up[:, :main], grad_gate[:, main:], grad_up[:, main:]]
        middle.append((activated, jnp.concatenate(parts, axis=1)))
    for (activated, grads), out, grad in zip(middle, (out_other, out_mine), (None, grad_mine)):
        total = matmul_right_t(grads, w_both[...]).astype(BF16)
        if grad is None:
            half = grad_a.shape[0]
            grad_a[...] = total[:half]
            grad_b[...] = total[half:]
        else:
            grad[...] = total
        out[...] = matmul(activated, w_down[...]).astype(BF16)


def mlp(mine, other, mine_in, other_in, w_gate, w_up, w_down, after):
    rows, width = mine.shape
    units = w_gate.shape[1]
    assert units % 256 in (0, 128)
    ready = mine_in.shape[1] == units
    vmem = pl.BlockSpec(memory_space=pltpu.VMEM)
    return pl.pallas_call(
        lambda *refs: mlp_kernel(ready, *refs),
        in_specs=[vmem] * 4 + [ANY_SPEC] * 6,
        out_specs=[vmem] * 5,
        out_shape=[jax.ShapeDtypeStruct((rows, width), BF16)] * 3
        + [jax.ShapeDtypeStruct((rows // 2, width), BF16)] * 2,
        scratch_shapes=[
            pltpu.VMEM((width, 2 * units), BF16),
            pltpu.VMEM((units, width), BF16),
            pltpu.SemaphoreType.DMA((5,)),
        ],
        compiler_params=pltpu.CompilerParams(vmem_limit_bytes=VMEM_LIMIT),
        cost_estimate=pl.CostEstimate(
            flops=24 * rows * width * units, bytes_accessed=26 * 10**6, transcendentals=2 * rows * units
        ),
        name="mlp",
    )(mine, other, mine_in, other_in, w_gate, w_up, w_down, *after)


def cast_kernel(values, _after, out):
    out[...] = values[0].astype(BF16)


def cast_after(micro, values, after):
    _, rows, width = values.shape
    steps = 4
    return pl.pallas_call(
        cast_kernel,
        grid=(steps,),
        in_specs=[pl.BlockSpec((1, rows // steps, width), lambda i: (micro, i, 0)), ANY_SPEC],
        out_specs=pl.BlockSpec((rows // steps, width), lambda i: (i, 0)),
        out_shape=jax.ShapeDtypeStruct((rows, width), BF16),
        name="cast_after",
    )(values, after)


def tie_kernel(_values, _after, _out):
    pass


def tie(values, after):
    return pl.pallas_call(
        tie_kernel,
        in_specs=[ANY_SPEC] * 2,
        out_specs=ANY_SPEC,
        out_shape=jax.ShapeDtypeStruct(values.shape, values.dtype),
        input_output_aliases={0: 0},
        name="tie",
    )(values, after)


def results_kernel(*refs):
    out = refs[9]
    for micro in range(2):
        first, *rest = refs[4 * micro : 4 * micro + 4]
        total = first[...]
        for part in rest:
            total = total + part[...].astype(F32)
        out[micro] = total.astype(BF16)


def add_results(first, second, after):
    rows, width = first[0].shape
    steps = 4
    part = pl.BlockSpec((rows // steps, width), lambda i: (i, 0))
    return pl.pallas_call(
        results_kernel,
        grid=(steps,),
        in_specs=[part] * 8 + [ANY_SPEC],
        out_specs=pl.BlockSpec((2, rows // steps, width), lambda i: (0, i, 0)),
        out_shape=jax.ShapeDtypeStruct((2, rows, width), BF16),
        name="results",
    )(*first, *second, after)


BLOCKS = 32
UNIT = 16
LAYER_UNITS = 12
VECTORS = 8


def square(ref):
    blocks, rows, width = ref.shape
    return ref[...].reshape(blocks * rows, width)


def entry_bias(valid, slots):
    shape = (valid.shape[1], valid.shape[1])
    same = lax.broadcasted_iota(jnp.int32, shape, 0) // slots == lax.broadcasted_iota(
        jnp.int32, shape, 1
    ) // slots
    return jnp.where(jnp.logical_and(same, valid > 0.5), 0.0, -1e30)


def entry_scores(queries, keys, bias):
    return matmul_right_t(queries, keys) * HEAD_DIM ** (-0.5) + bias


def entry_soft(scores):
    expon = jnp.exp(scores - jnp.max(scores, axis=1, keepdims=True))
    return expon / jnp.sum(expon, axis=1, keepdims=True)


def bell(values):
    return 0.5 * (1.0 + lax.erf(values * SQRT_HALF))


def lay_out_vectors(small, vectors, inner_bias):
    blocks, rows, lanes = small.shape

    def spread_rows(values, each, width):
        shape = (lanes, width)
        line = lax.broadcasted_iota(jnp.int32, shape, 0)
        column = lax.broadcasted_iota(jnp.int32, shape, 1)
        copies = jnp.where(column % each == line, 1.0, 0.0).astype(BF16)
        wide = matmul(values, copies).reshape(blocks, values.shape[0] // blocks, width)
        block = lax.broadcasted_iota(jnp.int32, wide.shape, 0)
        column = lax.broadcasted_iota(jnp.int32, wide.shape, 2)
        return jnp.sum(jnp.where(column // each == block, wide, 0.0), axis=0)

    count, width = vectors.shape
    layers, inner_width = inner_bias.shape
    values = small[...]
    vectors[...] = spread_rows(values.reshape(blocks * rows, lanes), UNIT, width)[:count]
    line = lax.broadcasted_iota(jnp.int32, values.shape, 1)
    for layer in range(layers):
        chosen = jnp.where(line == count + layer, values.astype(F32), 0.0)
        chosen = jnp.sum(chosen, axis=1).astype(BF16)
        inner_bias[layer : layer + 1, :] = spread_rows(chosen, 4 * UNIT, inner_width)


def hyper_kernel(
    slots, place, _a0, _a1, _a2, _a3, _a4, _a5, _a6, _a7, _a8, _a9, _a10, _a11, part0, part1, part2, part3, valid, small, outer, w_q, w_k, w_v, w_o, in0, in1, in2, in3,
    pr0, pr1, pr2, pr3,
    vectors, inner_bias, below, mixed, context, middle, inner, pooled, pooled_norm, embeds,
    state, joined,
):
    layer = pl.program_id(0)
    layers = pl.num_programs(0)
    rows, width = state.shape

    @pl.when(layer == 0)
    def _():
        columns = part0.shape[1]
        for k, part in enumerate((part0, part1, part2, part3)):
            at = pl.multiple_of((place[0] ^ k) * columns, columns)
            state[:, pl.ds(at, columns)] = part[...].astype(F32)
        lay_out_vectors(small, vectors, inner_bias)

    def vector(index):
        return vectors[pl.ds(index * layers + layer, 1), :]

    hidden = state[...]
    below[0] = hidden
    normed, _ = norm_parts(hidden)
    normed_in = (normed * vector(0) + vector(1)).astype(BF16)
    queries = (matmul(normed_in, square(w_q)) + vector(2)).astype(BF16)
    keys = matmul(normed_in, square(w_k)).astype(BF16)
    values = (matmul(normed_in, square(w_v)) + vector(3)).astype(BF16)
    mixed[0, :, :width] = queries
    mixed[0, :, width : 2 * width] = keys
    mixed[0, :, 2 * width :] = values
    bias = entry_bias(valid[...], slots)
    heads = [slice(i, i + HEAD_DIM) for i in range(0, width, HEAD_DIM)]
    scores = [entry_scores(queries[:, at], keys[:, at], bias) for at in heads]
    soft = [entry_soft(part).astype(BF16) for part in scores]
    parts = [matmul(part, values[:, at]) for part, at in zip(soft, heads)]
    joined[...] = jnp.concatenate(parts, axis=1)
    context_low = joined[...].astype(BF16)
    context[0] = context_low
    centre = hidden + matmul(context_low, square(w_o)) + vector(4)
    middle[0] = centre
    normed, _ = norm_parts(centre)
    normed_mid = (normed * vector(5) + vector(6)).astype(BF16)
    total = centre + vector(7)
    for j, piece in enumerate((in0, in1, in2, in3)):
        at = slice(j * width, (j + 1) * width)
        part = matmul(normed_mid, square(piece)) + inner_bias[pl.ds(layer, 1), at]
        inner[0, :, at] = part
        activated = (part * bell(part)).astype(BF16)
        blocks = BLOCKS // 4
        total = total + matmul(
            activated, outer[j * blocks : (j + 1) * blocks].reshape(width, width)
        )
    state[...] = total

    @pl.when(layer == layers - 1)
    def _():
        slot = lax.broadcasted_iota(jnp.int32, (rows, width), 0) % slots
        first = jnp.where(slot == 0, total, 0.0).reshape(rows // slots, slots, width)
        first = jnp.sum(first, axis=1)
        pooled[...] = first
        normed, _ = norm_parts(first)
        low = (normed * vectors[VECTORS * layers : VECTORS * layers + 1, :]
               + vectors[VECTORS * layers + 1 : VECTORS * layers + 2, :]).astype(BF16)
        pooled_norm[...] = low
        for j, piece in enumerate((pr0, pr1, pr2, pr3)):
            embeds[:, j * width : (j + 1) * width] = matmul(low, square(piece)).astype(BF16)


def layer_specs(width, which):
    specs = [pl.BlockSpec((BLOCKS, 4 * UNIT, width), lambda i: (0, which(i) * LAYER_UNITS // 4, 0))]
    for j in range(4, LAYER_UNITS):
        specs.append(
            pl.BlockSpec((BLOCKS, UNIT, width), lambda i, j=j: (0, which(i) * LAYER_UNITS + j, 0))
        )
    return specs


def proj_specs(width, layers):
    return [
        pl.BlockSpec((BLOCKS, UNIT, width), lambda i, j=j: (0, layers * LAYER_UNITS + j, 0))
        for j in range(4)
    ]


def whole_spec(*shape):
    return pl.BlockSpec(shape, lambda i: (0,) * len(shape))


def hyper_forward(where, after, parts, valid, packed, slots, layers):
    rows, width = parts[0].shape[0], len(parts) * parts[0].shape[1]
    inner_width = 4 * width
    count = VECTORS * layers + 2
    last_rows = packed.shape[1] // (2 * UNIT) - 1
    entries = rows // slots
    by_layer = lambda *shape: pl.BlockSpec((1,) + shape, lambda i: (i,) + (0,) * len(shape))
    return pl.pallas_call(
        lambda *refs: hyper_kernel(slots, *refs),
        grid=(layers,),
        in_specs=[pl.BlockSpec(memory_space=pltpu.SMEM)]
        + [pl.BlockSpec(memory_space=pl.ANY)] * 12
        + [whole_spec(*part.shape) for part in parts]
        + [
            whole_spec(1, rows),
            pl.BlockSpec((BLOCKS, 2 * UNIT, 128), lambda i: (0, last_rows, 0)),
        ]
        + layer_specs(width, lambda i: i)
        + proj_specs(width, layers),
        out_specs=[
            whole_spec(count, width),
            whole_spec(layers, inner_width),
            by_layer(rows, width),
            by_layer(rows, 3 * width),
            by_layer(rows, width),
            by_layer(rows, width),
            by_layer(rows, inner_width),
            whole_spec(entries, width),
            whole_spec(entries, width),
            whole_spec(entries, 4 * width),
        ],
        out_shape=[
            jax.ShapeDtypeStruct((count, width), F32),
            jax.ShapeDtypeStruct((layers, inner_width), F32),
            jax.ShapeDtypeStruct((layers, rows, width), F32),
            jax.ShapeDtypeStruct((layers, rows, 3 * width), BF16),
            jax.ShapeDtypeStruct((layers, rows, width), BF16),
            jax.ShapeDtypeStruct((layers, rows, width), F32),
            jax.ShapeDtypeStruct((layers, rows, inner_width), F32),
            jax.ShapeDtypeStruct((entries, width), F32),
            jax.ShapeDtypeStruct((entries, width), BF16),
            jax.ShapeDtypeStruct((entries, 4 * width), BF16),
        ],
        scratch_shapes=[pltpu.VMEM((rows, width), F32), pltpu.VMEM((rows, width), F32)],
        compiler_params=pltpu.CompilerParams(vmem_limit_bytes=VMEM_LIMIT),
        cost_estimate=pl.CostEstimate(
            flops=8 * 10**9, bytes_accessed=25 * 10**6, transcendentals=4 * 10**6
        ),
        name="hyper",
    )(where, *after, *parts, valid, *([packed] * (1 + LAYER_UNITS - 3 + 4)))


def hyper_back_kernel(
    slots, layer, layers, last,
    *refs,
):
    place, refs = refs[0], refs[1:]
    if last:
        arrivals, (pooled, pooled_norm, pr0, pr1, pr2, pr3) = refs[:8], refs[8:14]
        refs = refs[14:]
    else:
        grad_start = refs[0]
        refs = refs[1:]
    valid, vectors, below, mixed, context, middle, inner = refs[2:9]
    outer, w_q, w_k, w_v, w_o, in0, in1, in2, in3 = refs[9:18]
    refs = refs[18:]
    if layer == 0:
        small_above, inner_above = refs[:2]
        refs = refs[2:]
    packed = refs[:4]
    grad_below, small, inner_small, grad_mixed = refs[4:8]
    _, rows, width = below.shape
    blocks = BLOCKS // 4
    core, chip, side, line = place[0], place[1], place[2], place[3]
    half = packed[0].shape[3]

    def vector(index):
        at = index * layers + layer
        return vectors[at : at + 1, :]

    def put_rows(lines, at, rows_each, values):
        for i, z in enumerate(lines):
            for x in range(2):
                for y in range(2):
                    left, right = values[i, x, y, 0], values[i, x, y, 1]
                    mine = jnp.where(core == 0, left, right)
                    other = jnp.where(core == 0, right, left)
                    for kind, part in enumerate((mine, other)):
                        if at < half:
                            where = pl.ds(at, rows_each)
                            packed[kind][y ^ chip, x ^ side, (z - line) & 3, where, :] = part
                        else:
                            where = pl.ds(at - half, rows_each)
                            packed[2 + kind][x ^ side, y ^ chip, (z - line) & 3, where, :] = part

    def put(unit, grads):
        grads = grads.astype(BF16).reshape(4, 2, 2, 2, UNIT, width)
        put_rows(range(4), unit * UNIT, UNIT, grads)

    def column_sum(values):
        return jnp.sum(values, axis=0, keepdims=True)

    if last:
        normed, inverse = norm_parts(pooled[...])
        grad_norm = jnp.zeros(normed.shape, F32)
        sums = []
        for group in (arrivals[:4], arrivals[4:]):
            total = group[0][...].astype(F32)
            for part in group[1:]:
                total = total + part[...].astype(F32)
            sums.append(total)
        grad_embeds = jnp.concatenate(sums, axis=0).astype(BF16)
        for j, piece in enumerate((pr0, pr1, pr2, pr3)):
            part = grad_embeds[:, j * width : (j + 1) * width]
            put(LAYER_UNITS + j, matmul_left_t(pooled_norm[...], part))
            grad_norm = grad_norm + matmul_right_t(part, square(piece))
        small[VECTORS : VECTORS + 1, :] = column_sum(grad_norm * normed)
        small[VECTORS + 1 : VECTORS + 2, :] = column_sum(grad_norm)
        final_gain = vectors[VECTORS * layers : VECTORS * layers + 1, :]
        grad_pooled = norm_back(normed, inverse, grad_norm * final_gain)
        slot = lax.broadcasted_iota(jnp.int32, (rows, width), 0) % slots
        grad_rows = jnp.broadcast_to(grad_pooled[:, None, :], (rows // slots, slots, width))
        grad_rows = jnp.where(slot == 0, grad_rows.reshape(rows, width), 0.0)
    else:
        grad_rows = grad_start[...]

    low = grad_rows.astype(BF16)
    small[7:8, :] = column_sum(grad_rows)
    normed_two, inverse_two = norm_parts(middle[0])
    normed_mid = (normed_two * vector(5) + vector(6)).astype(BF16)
    grad_mid = jnp.zeros(grad_rows.shape, F32)
    for j, piece in enumerate((in0, in1, in2, in3)):
        at = slice(j * width, (j + 1) * width)
        part = inner[0, :, at]
        share = bell(part)
        activated = (part * share).astype(BF16)
        slope = share + part * jnp.exp(-0.5 * part * part) * INV_SQRT_TAU
        where = slice(j * blocks, (j + 1) * blocks)
        grad_outer = matmul_left_t(activated, low).astype(BF16)
        put_rows((j,), 0, 4 * UNIT, grad_outer.reshape(1, 2, 2, 2, 4 * UNIT, width))
        grad_part = matmul_right_t(low, outer[where].reshape(width, width)) * slope
        inner_small[:, at] = column_sum(grad_part)
        grad_part = grad_part.astype(BF16)
        put(8 + j, matmul_left_t(normed_mid, grad_part))
        grad_mid = grad_mid + matmul_right_t(grad_part, square(piece))
    small[5:6, :] = column_sum(grad_mid * normed_two)
    small[6:7, :] = column_sum(grad_mid)
    grad_rows = grad_rows + norm_back(normed_two, inverse_two, grad_mid * vector(5))
    small[4:5, :] = column_sum(grad_rows)
    low = grad_rows.astype(BF16)
    put(7, matmul_left_t(context[0], low))
    grad_context = matmul_right_t(low, square(w_o)).astype(BF16)
    bias = entry_bias(valid[...], slots)
    heads = [slice(i, i + HEAD_DIM) for i in range(0, width, HEAD_DIM)]
    queries, keys, values = (
        [mixed[0, :, i * width + at.start : i * width + at.stop] for at in heads] for i in range(3)
    )
    grads = [grad_context[:, at] for at in heads]
    scores = [entry_scores(q, k, bias) for q, k in zip(queries, keys)]
    grad_soft = [matmul_right_t(g, v) for g, v in zip(grads, values)]
    soft = [entry_soft(part) for part in scores]
    grad_scores = []
    for part, grad in zip(soft, grad_soft):
        offset = jnp.sum(part * grad, axis=1, keepdims=True)
        grad_scores.append((part * (grad - offset) * HEAD_DIM ** (-0.5)).astype(BF16))
    soft = [part.astype(BF16) for part in soft]
    grad_mixed[:, :width] = jnp.concatenate(
        [matmul(g, k) for g, k in zip(grad_scores, keys)], axis=1
    )
    grad_mixed[:, width : 2 * width] = jnp.concatenate(
        [matmul_left_t(g, q) for g, q in zip(grad_scores, queries)], axis=1
    )
    grad_mixed[:, 2 * width :] = jnp.concatenate(
        [matmul_left_t(p, g) for p, g in zip(soft, grads)], axis=1
    )
    normed_one, inverse_one = norm_parts(below[0])
    normed_in = (normed_one * vector(0) + vector(1)).astype(BF16)
    grad_in = jnp.zeros(grad_rows.shape, F32)
    for i, piece in enumerate((w_q, w_k, w_v)):
        part = grad_mixed[:, i * width : (i + 1) * width]
        if i != 1:
            small[2 + i // 2 : 3 + i // 2, :] = column_sum(part)
        part = part.astype(BF16)
        put(4 + i, matmul_left_t(normed_in, part))
        grad_in = grad_in + matmul_right_t(part, square(piece))
    small[0:1, :] = column_sum(grad_in * normed_one)
    small[1:2, :] = column_sum(grad_in)
    grad_rows = grad_rows + norm_back(normed_one, inverse_one, grad_in * vector(0))
    if layer == 0:
        part = grad_rows.astype(BF16)
        columns = grad_below.shape[2]
        for t in range(grad_below.shape[0]):
            grad_below[t ^ (2 * chip + core)] = part[:, t * columns : (t + 1) * columns]
        wide = refs[8]
        wide[...] = jnp.zeros_like(wide)
        own = small[...]
        above = small_above[...]
        for b in range(BLOCKS):
            at = slice(b * UNIT, (b + 1) * UNIT)
            for i in range(layers):
                source = own if i == 0 else above
                wide[b, i * VECTORS : (i + 1) * VECTORS, 0:UNIT] = source[:VECTORS, at]
            wide[b, VECTORS * layers : VECTORS * layers + 2, 0:UNIT] = above[VECTORS:, at]
            at = slice(b * 4 * UNIT, (b + 1) * 4 * UNIT)
            wide[b, VECTORS * layers + 2 : VECTORS * layers + 3, 0 : 4 * UNIT] = inner_small[:, at]
            wide[b, VECTORS * layers + 3 : VECTORS * layers + 4, 0 : 4 * UNIT] = inner_above[:, at]
        base = LAYER_UNITS * UNIT
        spare = jnp.zeros((BLOCKS, 2 * UNIT, width - wide.shape[2]), F32)
        full = jnp.concatenate([wide[...], spare], axis=2).astype(BF16)
        put_rows(range(4), base, 2 * UNIT, full.reshape(4, 2, 2, 2, 2 * UNIT, width))
    else:
        grad_below[...] = grad_rows


def hyper_backward(place, layer, source, valid, vectors, kept, packed, slots, above, columns, after):
    below, mixed, context, middle, inner = kept
    layers, rows, width = below.shape
    inner_width = inner.shape[2]
    last = layer == layers - 1
    at_layer = lambda *shape: pl.BlockSpec((1,) + shape, lambda i: (layer,) + (0,) * len(shape))
    inputs, specs = [place], [pl.BlockSpec(memory_space=pltpu.SMEM)]
    if last:
        arrivals, pooled, pooled_norm = source
        inputs += [*arrivals, pooled, pooled_norm] + [packed] * 4
        specs += [whole_spec(*part.shape) for part in arrivals] + [whole_spec(*pooled.shape)]
        specs += [whole_spec(*pooled_norm.shape)] + proj_specs(width, layers)
    else:
        inputs += [source]
        specs += [whole_spec(rows, width)]
    inputs += [*after, valid, vectors, below, mixed, context, middle, inner]
    specs += [pl.BlockSpec(memory_space=pl.ANY)] * 2
    specs += [whole_spec(1, rows), whole_spec(*vectors.shape), at_layer(rows, width)]
    specs += [at_layer(rows, 3 * width), at_layer(rows, width), at_layer(rows, width)]
    specs += [at_layer(rows, inner_width)]
    inputs += [packed] * (LAYER_UNITS - 3)
    specs += layer_specs(width, lambda i: layer)
    scratch = [pltpu.VMEM((rows, 3 * width), F32)]
    units = LAYER_UNITS + (4 if last else 0) + (2 if layer == 0 else 0)
    below_shape = jax.ShapeDtypeStruct((rows, width), F32)
    if layer == 0:
        inputs += list(above)
        specs += [whole_spec(*part.shape) for part in above]
        below_shape = jax.ShapeDtypeStruct((width // columns, rows, columns), BF16)
        scratch.append(pltpu.VMEM((BLOCKS, 2 * UNIT, 128), F32))
    half = units // 2 * UNIT
    out_shape = [
        jax.ShapeDtypeStruct((2, 2, 4, half, width), BF16),
        jax.ShapeDtypeStruct((2, 2, 4, half, width), BF16),
        jax.ShapeDtypeStruct((2, 2, 4, units * UNIT - half, width), BF16),
        jax.ShapeDtypeStruct((2, 2, 4, units * UNIT - half, width), BF16),
        below_shape,
        jax.ShapeDtypeStruct((VECTORS + (2 if last else 0), width), F32),
        jax.ShapeDtypeStruct((1, inner_width), F32),
    ]
    return pl.pallas_call(
        lambda *refs: hyper_back_kernel(slots, layer, layers, last, *refs),
        grid=(1,),
        in_specs=specs,
        out_specs=[whole_spec(*shape.shape) for shape in out_shape],
        out_shape=out_shape,
        scratch_shapes=scratch,
        compiler_params=pltpu.CompilerParams(vmem_limit_bytes=VMEM_LIMIT),
        cost_estimate=pl.CostEstimate(
            flops=8 * 10**9, bytes_accessed=25 * 10**6, transcendentals=4 * 10**6
        ),
        name="hyper_back",
    )(*inputs)


def pack_kernel(layers, *refs):
    (g1, b1, w_qkv, bq, bv, w_ao, bao, g2, b2, w_in, b_in, w_out, bout, fg, fb, w_proj) = refs[:16]
    packed, wide = refs[16:]
    width = packed.shape[1]
    for layer in range(layers):
        base = layer * LAYER_UNITS * UNIT
        packed[base : base + 4 * UNIT] = w_out[layer]
        for j in range(3):
            at = base + (4 + j) * UNIT
            packed[at : at + UNIT] = w_qkv[layer, :, j * width : (j + 1) * width]
        packed[base + 7 * UNIT : base + 8 * UNIT] = w_ao[layer]
        for j in range(4):
            at = base + (8 + j) * UNIT
            packed[at : at + UNIT] = w_in[layer, :, j * width : (j + 1) * width]
    base = layers * LAYER_UNITS * UNIT
    for j in range(4):
        packed[base + j * UNIT : base + (j + 1) * UNIT] = w_proj[:, j * width : (j + 1) * width]
    wide[...] = jnp.zeros_like(wide)
    for j, ref in enumerate((g1, b1, bq, bv, bao, g2, b2, bout)):
        wide[j * layers : (j + 1) * layers, 0:UNIT] = ref[...].astype(F32)
    at = VECTORS * layers
    wide[at : at + 1, 0:UNIT] = fg[...].astype(F32)
    wide[at + 1 : at + 2, 0:UNIT] = fb[...].astype(F32)
    wide[at + 2 : at + 2 + layers, 0 : 4 * UNIT] = b_in[...].astype(F32)
    base = base + 4 * UNIT
    packed[base:] = jnp.zeros((2 * UNIT, width), BF16)
    packed[base:, : wide.shape[1]] = wide[...].astype(BF16)


def pack_shards(shards):
    (g1, b1, w_qkv, bq, bv, w_ao, bao, g2, b2, w_in, b_in, w_out, bout, fg, fb, w_proj) = shards
    layers, own, _ = w_qkv.shape
    width = w_ao.shape[2]
    if own == UNIT:
        inputs = list(shards)
        inputs[13], inputs[14] = fg[None], fb[None]
        return pl.pallas_call(
            lambda *refs: pack_kernel(layers, *refs),
            out_shape=jax.ShapeDtypeStruct(((layers * LAYER_UNITS + 6) * UNIT, width), BF16),
            scratch_shapes=[pltpu.VMEM((2 * UNIT, 128), F32)],
            name="pack",
        )(*inputs)
    pieces = []
    for layer in range(layers):
        pieces += [w_out[layer]]
        pieces += [w_qkv[layer, :, i * width : (i + 1) * width] for i in range(3)]
        pieces += [w_ao[layer]]
        pieces += [w_in[layer, :, i * width : (i + 1) * width] for i in range(4)]
    pieces += [w_proj[:, i * width : (i + 1) * width] for i in range(4)]
    small = [jnp.concatenate([g1, b1, bq, bv, bao, g2, b2, bout, fg[None], fb[None]]), b_in]
    small = [jnp.pad(part, ((0, 0), (0, width - part.shape[1]))) for part in small]
    small = jnp.concatenate(small)
    small = jnp.pad(small, ((0, 2 * UNIT - small.shape[0]), (0, 0)))
    return jnp.concatenate(pieces + [small])


def piece_rows(layers, own, first_layer=0, last_layer=None):
    return [4 * own] + [own] * (LAYER_UNITS - 4)


def canonical(gathered, own, layers):
    if own == UNIT:
        return gathered
    devices, _, width = gathered.shape
    count = VECTORS * layers + 2
    pieces, at = [], 0
    for rows in piece_rows(layers, own) * layers + [own] * 4:
        pieces.append(gathered[:, at : at + rows].reshape(BLOCKS, -1, width))
        at += rows
    small = []
    for first, rows, each in ((at, count, own), (at + count, layers, 4 * own)):
        part = gathered[:, first : first + rows, :each].reshape(BLOCKS, -1, rows, each)
        part = part.transpose(0, 2, 1, 3).reshape(BLOCKS, rows, -1)
        small.append(jnp.pad(part, ((0, 0), (0, 0), (0, width - part.shape[2]))))
    small = jnp.concatenate(small, axis=1)
    pieces.append(jnp.pad(small, ((0, 0), (0, 2 * UNIT - small.shape[1]), (0, 0))))
    return jnp.concatenate(pieces, axis=1)


def to_devices(packed, devices, rows_list, vector_rows):
    if devices == BLOCKS:
        return packed
    width = packed.shape[2]
    split = devices // BLOCKS
    pieces, at = [], 0
    for rows in rows_list:
        pieces.append(packed[:, at : at + rows].reshape(devices, rows // split, width))
        at += rows
    if vector_rows:
        small = packed[:, at : at + vector_rows]
        narrow = small[:, : vector_rows - 14, :UNIT].reshape(BLOCKS, -1, split, UNIT // split)
        broad = small[:, vector_rows - 14 : vector_rows - 12, : 4 * UNIT]
        broad = broad.reshape(BLOCKS, -1, split, 4 * UNIT // split)
        parts = []
        for part in (narrow, broad):
            part = part.transpose(0, 2, 1, 3).reshape(devices, part.shape[1], part.shape[3])
            parts.append(jnp.pad(part, ((0, 0), (0, 0), (0, width - part.shape[2]))))
        small = jnp.concatenate(parts, axis=1)
        pieces.append(jnp.pad(small, ((0, 0), (0, vector_rows - small.shape[1]), (0, 0))))
    return jnp.concatenate(pieces, axis=1)


def unpack_kernel(layers, above_kept, above_got, below_kept, below_got, g_qkv, g_ao, g_in, g_out, g_proj, *vectors):
    width = above_kept.shape[2]
    above = above_kept[0].astype(F32) + above_got[...].astype(F32)
    below = below_kept[0].astype(F32) + below_got[...].astype(F32)
    for layer, ref in ((0, below), (1, above)):
        g_out[layer] = ref[: 4 * UNIT]
        for j in range(3):
            at = (4 + j) * UNIT
            g_qkv[layer, :, j * width : (j + 1) * width] = ref[at : at + UNIT]
        g_ao[layer] = ref[7 * UNIT : 8 * UNIT]
        for j in range(4):
            at = (8 + j) * UNIT
            g_in[layer, :, j * width : (j + 1) * width] = ref[at : at + UNIT]
    base = LAYER_UNITS * UNIT
    for j in range(4):
        at = base + j * UNIT
        g_proj[:, j * width : (j + 1) * width] = above[at : at + UNIT]
    small = below[base : base + 2 * UNIT, :128]
    for j in range(VECTORS):
        for i in range(layers):
            vectors[j][i : i + 1, :] = small[i * VECTORS + j : i * VECTORS + j + 1, :UNIT]
    count = VECTORS * layers
    vectors[VECTORS][...] = small[count : count + 1, :UNIT]
    vectors[VECTORS + 1][...] = small[count + 1 : count + 2, :UNIT]
    vectors[VECTORS + 2][...] = small[count + 2 : count + 2 + layers, : 4 * UNIT]


def unpack_grads(above, below, own, layers):
    width = above[0].shape[-1]
    count = VECTORS * layers
    if own == UNIT:
        shapes = [
            (layers, own, 3 * width),
            (layers, own, width),
            (layers, own, 4 * width),
            (layers, 4 * own, width),
            (own, 4 * width),
        ]
        shapes += [(layers, own)] * VECTORS + [(1, own), (1, own), (layers, 4 * own)]
        outs = pl.pallas_call(
            lambda *refs: unpack_kernel(layers, *refs),
            out_shape=[jax.ShapeDtypeStruct(shape, F32) for shape in shapes],
            name="unpack",
        )(*above, *below)
        return outs[:5], outs[5:13], outs[13][0], outs[14][0], outs[15]
    parts = []
    for ref in (below, above):
        cuts, at = [], 0
        for rows in piece_rows(layers, own):
            cuts.append(ref[at : at + rows].astype(F32))
            at += rows
        parts.append(cuts)
    mats = [
        jnp.stack([jnp.concatenate(cuts[1:4], axis=1) for cuts in parts]),
        jnp.stack([cuts[4] for cuts in parts]),
        jnp.stack([jnp.concatenate(cuts[5:9], axis=1) for cuts in parts]),
        jnp.stack([cuts[0] for cuts in parts]),
        jnp.concatenate(
            [above[at + i * own : at + (i + 1) * own].astype(F32) for i in range(4)], axis=1
        ),
    ]
    small = below[at : at + 2 * UNIT, :128].astype(F32)
    vectors = [
        jnp.stack([small[i * VECTORS + j, :own] for i in range(layers)]) for j in range(VECTORS)
    ]
    inner_bias = small[count + 2 : count + 2 + layers, : 4 * own]
    return mats, vectors, small[count, :own], small[count + 1, :own], inner_bias


def pair_swap(values, bit):
    return swap(values, "tensor", bit)


def halve_kernel(mine_a, got_a, mine_b, got_b, _after_one, _after_two, keep_a, send_a, keep_b, send_b):
    for mine, got, keep, send in ((mine_a, got_a, keep_a, send_a), (mine_b, got_b, keep_b, send_b)):
        for i, out in enumerate((keep, send)):
            out[...] = (mine[i].astype(F32) + got[i].astype(F32)).astype(BF16)


def halve_after(mine_a, got_a, mine_b, got_b, *after):
    width = mine_a.shape[-1]
    count = mine_a[0].size // (mine_a.shape[-2] * width)
    together = 2
    inputs, specs, outs, out_specs = [], [], [], []
    for mine, got in ((mine_a, got_a), (mine_b, got_b)):
        rows = mine.shape[-2]
        inputs += [part.reshape(2, count, rows, width) for part in (mine, got)]
        specs += [pl.BlockSpec((2, together, rows, width), lambda i: (0, i, 0, 0))] * 2
        outs += [jax.ShapeDtypeStruct((count, rows, width), BF16)] * 2
        out_specs += [pl.BlockSpec((together, rows, width), lambda i: (i, 0, 0))] * 2
    halves = pl.pallas_call(
        halve_kernel,
        grid=(count // together,),
        in_specs=specs + [pl.BlockSpec(memory_space=pl.ANY)] * 2,
        out_specs=out_specs,
        out_shape=outs,
        name="halve_after",
    )(*inputs, after[0], after[-1])
    shapes = [part.shape[1:] for part in (mine_a, mine_a, mine_b, mine_b)]
    return [half.reshape(shape) for half, shape in zip(halves, shapes)]


def join_kernel(kept_a, got_a, kept_b, got_b, _after_one, _after_two, rest, last):
    rows = kept_a.shape[1]
    for at, kept, got in ((slice(0, rows), kept_a, got_a), (slice(rows, None), kept_b, got_b)):
        total = (kept[...].astype(F32) + got[...].astype(F32)).astype(BF16)
        rest[:, at, :] = total[:-1]
        last[at, :] = total[-1]


def join_after(kept_a, got_a, kept_b, got_b, *after):
    line, rows_a, width = kept_a.shape
    rows = rows_a + kept_b.shape[1]
    vmem = pl.BlockSpec(memory_space=pltpu.VMEM)
    return pl.pallas_call(
        join_kernel,
        in_specs=[vmem] * 4 + [pl.BlockSpec(memory_space=pl.ANY)] * 2,
        out_specs=[vmem] * 2,
        out_shape=[
            jax.ShapeDtypeStruct((line - 1, rows, width), BF16),
            jax.ShapeDtypeStruct((rows, width), BF16),
        ],
        name="join_after",
    )(kept_a, got_a, kept_b, got_b, after[0], after[-1])


def stack_kernel(p0, p1, p2, p3, _after_one, _after_two, out):
    for k, part in enumerate((p0, p1, p2, p3)):
        out[k] = part[...]


def stack_after(parts, *after):
    vmem = pl.BlockSpec(memory_space=pltpu.VMEM)
    return pl.pallas_call(
        stack_kernel,
        in_specs=[vmem] * 4 + [pl.BlockSpec(memory_space=pl.ANY)] * 2,
        out_specs=vmem,
        out_shape=jax.ShapeDtypeStruct((4,) + parts[0].shape, parts[0].dtype),
        name="stack_after",
    )(*parts, *after)


def next_on_line(values):
    size = lax.axis_size("dp")
    return lax.ppermute(values, "dp", [(i, (i + 2) % size) for i in range(size)])


def scatter_line(rest, last):
    totals = [last]
    for ahead in (2, 1):
        got = next_on_line(totals[-1])
        totals.append((rest[ahead].astype(F32) + got.astype(F32)).astype(BF16))
    return totals[1], totals[2], next_on_line(totals[2])


def gather_line(values, *after):
    parts = [values]
    for step in range(lax.axis_size("dp") // 2 - 1):
        sent = parts[-1] if step >= len(after) else tie(parts[-1], after[step])
        parts.append(next_on_line(sent))
    return parts


def sum_grads(packed, rows_list, vector_rows):
    packed_a = jnp.stack(packed[:2]).transpose(3, 2, 1, 0, 4, 5)
    packed_b = jnp.stack(packed[2:]).transpose(3, 1, 2, 0, 4, 5)
    packed = jnp.concatenate([packed_a, packed_b], axis=4)
    packed = packed.reshape((BLOCKS,) + packed.shape[4:])
    packed = to_devices(packed, 4 * lax.axis_size("dp"), rows_list, vector_rows)
    return lax.psum_scatter(packed, BOTH, scatter_dimension=0, tiled=True)[0]


def dp_bits():
    size = lax.axis_size("dp")
    return [1 << i for i in range(size.bit_length() - 1)]


def dp_places():
    bits = dp_bits()
    return [
        sum(bit for i, bit in enumerate(reversed(bits)) if (place >> i) & 1)
        for place in range(lax.axis_size("dp"))
    ]


def gather_relative(values, first, last):
    for bit in list(reversed(dp_bits()))[first:last]:
        values = jnp.concatenate([values, swap(values, "dp", bit)])
    return values


def reduce_relative(keep, send):
    bits = dp_bits()
    first = keep = keep + swap(send, "dp", bits[0])
    for bit in bits[1:]:
        half = keep.shape[0] // 2
        keep = keep[:half] + swap(keep[half:], "dp", bit)
    return keep[0], first


def exchange_relative(first, second, third):
    return [pair_swap(first, 1), pair_swap(second, 2), pair_swap(third, 3)]


def local(
    piece_table,
    piece_ids,
    piece_counts,
    text_ids,
    cotangent,
    rms_gain_one,
    w_query,
    w_key,
    w_value,
    w_output,
    rms_gain_two,
    w_gate,
    w_up,
    w_down,
    *shard_params,
):
    tensor_index = lax.axis_index("tensor")
    dp_index = lax.axis_index("dp")
    tensor_size = lax.axis_size("tensor")
    dp_size = lax.axis_size("dp")
    devices = tensor_size * dp_size
    micro_count, group_entries, slot_count = piece_ids.shape
    own_entries = group_entries // tensor_size
    seq_length = text_ids.shape[1]
    share = cotangent.shape[1]
    layer_count, own, _ = shard_params[2].shape
    width = shard_params[5].shape[2]
    lm_width = cotangent.shape[2]
    table_rows, table_cols = piece_table.shape
    gain_first = rms_gain_one[None, :]
    gain_second = rms_gain_two[None, :]
    cosine, sine = rotary_tables(seq_length)
    trig = jnp.concatenate([cosine.T, sine.T], axis=0)
    w_kv = jnp.concatenate([w_key, w_value], axis=1)

    where = tensor_index.astype(jnp.int32)[None]

    gathered = lax.all_gather(pack_shards(shard_params), BOTH, axis=0)

    stages = len(dp_bits())
    ids_rel = gather_relative(piece_ids[None], 0, stages)
    ids_rel = ids_rel.reshape(dp_size, micro_count, tensor_size, own_entries, slot_count)
    ids_rel = jnp.take(ids_rel, tensor_index ^ jnp.arange(tensor_size), axis=2)
    ids_rel = ids_rel.transpose(0, 2, 1, 3, 4) - dp_index * table_rows
    places = jnp.asarray(dp_places())
    ids_back = jnp.zeros_like(ids_rel).at[dp_index ^ places].set(ids_rel)
    if dp_size == 8:
        behind = (dp_index + dp_size - 2 * jnp.arange(dp_size // 2)) % dp_size
        ids_back = jnp.take(ids_back, jnp.stack([behind, behind ^ 1], axis=1).reshape(-1), axis=0)
    ids_back = ids_back.reshape(4, -1)
    ids_columns = [ids[:, None] for ids in ids_back]
    ids_rel = ids_rel.reshape(2, -1)
    own_rows = micro_count * own_entries * slot_count
    looked = []
    for i in (1, 0):
        rows = lookup(ids_rel[i], piece_table, looked[0] if looked else ids_rel)
        looked.append(rows.reshape(dp_size // 2, tensor_size, own_rows, table_cols))
    near_looked = looked[1]
    looked, _ = reduce_relative(looked[1], looked[0])
    pieces = [looked[0], *exchange_relative(*looked[1:])]

    text_rel = text_ids ^ (tensor_index * own_entries)
    micros = range(micro_count)
    ids_row, ids_own, ids_peer = [], [], []
    for micro in micros:
        row = text_rel[micro][None, :]
        ids_row.append(row)
        ids_own.append(lax.dynamic_slice_in_dim(row, tensor_index * share, share, 1))
        ids_peer.append(lax.dynamic_slice_in_dim(row, (tensor_index ^ 2) * share, share, 1))
    ids_small = jnp.stack(ids_own + ids_peer)

    packed = canonical(gathered, own, layer_count)
    counts_own = lax.dynamic_slice_in_dim(piece_counts, tensor_index * own_entries, own_entries, 1)
    valid = jnp.arange(slot_count)[None, :] < counts_own.reshape(-1)[:, None]
    valid = valid.astype(F32).reshape(1, own_rows)
    w_out = [w_output, pair_swap(w_output, 1), pair_swap(w_output, 2)]
    cots = [cast_after(micro, cotangent, near_looked) for micro in range(micro_count)]
    grads_near = [
        [matmul_right_t(part, w_down).astype(BF16) for part in (cot, pair_swap(cot, 1))]
        for cot in cots
    ]
    vectors, _, *kept_hyper, pooled, pooled_norm, embeds = hyper_forward(
        where, (w_out[2], *grads_near[0], *grads_near[1], trig, ids_small, *ids_columns, ids_back), pieces, valid, packed, slot_count, layer_count
    )

    w_out.append(pair_swap(w_out[2], 1))
    embeds = embeds.reshape(micro_count, own_entries, lm_width)
    embeds = [embeds] + [pair_swap(embeds, k) for k in (1, 2, 3)]

    def peer_cot(micro, after):
        cot = pair_swap(tie(cots[micro], after), 2)
        return cot, pair_swap(cot, 1)

    cots_peer = [peer_cot(0, embeds[3])]
    kept_attn, contexts = [], []
    after = (embeds[0], embeds[0])
    for micro in micros:
        near, far, *kept = attend(
            where, micro, embeds, gain_first, w_query, w_kv, ids_row[micro], trig, after
        )
        kept_attn.append(kept)
        contexts.append([near, *exchange_relative(far, near, far)])
        after = (near, cots_peer[0][0])

    def after_attention(micro, after):
        own, peer, rows = hidden_rows_of(
            kept_attn[micro][-1], ids_own[micro], ids_peer[micro], gain_second,
            contexts[micro], w_out, after,
        )
        return (own, pair_swap(own, 1)), (peer, pair_swap(peer, 1)), rows

    def feed_forward(normed, grads_in, *after):
        after = (after + after[:1] * 2)[:3]
        return mlp(*normed, *grads_in, w_gate, w_up, w_down, after)

    def travel(part):
        from_core = jnp.concatenate([pair_swap(half, 1) for half in part[3:]])
        away = (part[2].astype(F32) + from_core.astype(F32)).astype(BF16)
        return away, pair_swap(away, 2)

    def back_of(micro, rows, near, arrived):
        low, *parts = hidden_back(
            micro, cotangent, rows, near[2], [pair_swap(half, 1) for half in near[3:]], arrived,
            gain_second, w_out,
        )
        return low, [parts[0], *exchange_relative(*parts[1:])]

    def send_result(peer, after):
        total = (peer[0].astype(F32) + pair_swap(peer[1], 1).astype(F32)).astype(BF16)
        return pair_swap(tie(total, after), 2)

    near_in, peer_in, rows_a = after_attention(0, (contexts[1][0], contexts[1][0]))
    near_a = feed_forward(near_in, grads_near[0], rows_a)
    cots_peer.append(peer_cot(1, near_a[2]))
    peer_a = feed_forward(peer_in, cots_peer[0], near_a[2], contexts[1][2], contexts[1][3])
    away_a, arrived_a = travel(peer_a)
    near_in, peer_in, rows_b = after_attention(1, (away_a, cots_peer[1][0]))
    peer_b = feed_forward(peer_in, cots_peer[1], rows_b)
    away_b, arrived_b = travel(peer_b)
    low_a, parts_a = back_of(0, rows_a, near_a, arrived_a)
    near_b = feed_forward(near_in, grads_near[1], low_a, away_b)
    result_a = send_result(peer_a, near_b[2])
    low_b, parts_b = back_of(1, rows_b, near_b, arrived_b)

    place = jnp.stack([tensor_index % 2, tensor_index // 2, dp_index % 2, dp_index // 2])
    place = place.astype(jnp.int32)
    grad_embeds = []
    after = (low_b,) * 5
    near_swapped = [pair_swap(near[1], 1) for near in (near_a, near_b)]
    for micro, parts, low in ((0, parts_a, low_a), (1, parts_b, low_b)):
        grads = attend_back(
            where, parts, kept_attn[micro], ids_row[micro], ids_own[micro], trig,
            w_query, w_kv, gain_first, low, after,
        )
        after = (grads[0], result_a, parts_b[2], *near_swapped)
        if micro == 0:
            result_b = send_result(peer_b, grads[0])
        grad_embeds += [grads[0], *exchange_relative(*grads[1:])]

    if dp_size != 8:
        place = place * 0
    source = (grad_embeds, pooled, pooled_norm)
    packs, above, after = [None] * layer_count, (), (result_b, result_b)
    near_side, near_chip = ("dp", 1), ("tensor", 2)
    for layer in range(layer_count - 1, -1, -1):
        *parts, source, small, inner_small = hyper_backward(
            place, layer, source, valid, vectors, kept_hyper, packed, slot_count, above,
            table_cols, after,
        )
        above = (small, inner_small)
        packs[layer] = parts
        if dp_size == 8 and layer == layer_count - 1:
            upper = halve_after(
                parts[0], pair_swap(parts[1], 1), parts[2], pair_swap(parts[3], 1), small
            )
            after = (upper[1], upper[3])
    if dp_size == 8:
        parts = packs[0]
        from_chip = pair_swap(source[2:], 2)
        results = add_results(
            (rows_a, near_a[0], near_swapped[0], result_a),
            (rows_b, near_b[0], near_swapped[1], result_b),
            parts[0],
        )
        upper = halve_after(
            upper[0], swap(upper[1], *near_chip), upper[2], swap(upper[3], *near_side), results
        )
        upper_got = swap(upper[3], *near_chip)
        other_a, other_b = tie(parts[1], upper[1]), tie(parts[3], upper[1])
        from_chip = pair_swap(source[2:], 2)
        lower = halve_after(
            parts[0], pair_swap(other_a, 1), parts[2], pair_swap(other_b, 1), upper[1]
        )
        near_piece, forward = tie(source[1], lower[1]), tie(from_chip[1], lower[1])
        pieces = [source[0], pair_swap(near_piece, 1), from_chip[0], pair_swap(forward, 1)]
        pieces = stack_after(pieces, upper_got, lower[1])
        upper_rest, last = join_after(
            upper[0], swap(upper[1], *near_side), upper[2], upper_got, pieces
        )
        sent = [tie(lower[1], last), tie(lower[3], last)]
        pieces = gather_line(jnp.stack([pieces, swap(pieces, "dp", 1)]), last)
        pieces = [part.reshape(-1, table_cols) for part in pieces]
        step_one, step_two, upper_got = scatter_line(upper_rest, last)
        table_grad = collect(ids_back[:2], ids_columns[:2], pieces[0], pieces[1], table_rows, None)
        lower = halve_after(
            lower[0], swap(sent[0], *near_chip), lower[2], swap(sent[1], *near_side), last
        )
        lower_rest, last = join_after(
            lower[0], swap(lower[1], *near_side), lower[2], swap(lower[3], *near_chip), table_grad, step_two
        )
        *_, lower_got = scatter_line(lower_rest, last)
        reduced = [(lower_rest, lower_got), (upper_rest, upper_got)]
    else:
        pieces = jnp.take(source, tensor_index ^ jnp.arange(tensor_size), axis=0)
        pieces = jnp.stack([pieces[0], *exchange_relative(*pieces[1:])])
        pieces = lax.all_gather(pieces, "dp", axis=0).reshape(4, -1, table_cols)
        rows_list = piece_rows(layer_count, UNIT)
        reduced = [
            sum_grads(packs[0], rows_list, 2 * UNIT),
            sum_grads(packs[1], rows_list + [UNIT] * 4, 0),
        ]
        table_grad = collect(ids_back[:2], ids_columns[:2], pieces[0], pieces[1], table_rows, None)
        results = add_results(
            (rows_a, near_a[0], near_swapped[0], result_a),
            (rows_b, near_b[0], near_swapped[1], result_b),
            table_grad,
        )
    table_grad = collect(ids_back[2:], ids_columns[2:], pieces[2], pieces[3], table_rows, table_grad)

    mats, vecs, out_final_gain, out_final_bias, out_inner_bias = unpack_grads(
        reduced[1], reduced[0], own, layer_count
    )
    return (
        results,
        table_grad,
        vecs[0],
        vecs[1],
        mats[0],
        vecs[2],
        vecs[3],
        mats[1],
        vecs[4],
        vecs[5],
        vecs[6],
        mats[2],
        out_inner_bias,
        mats[3],
        vecs[7],
        out_final_gain,
        out_final_bias,
        mats[4],
    )


def solution(mesh):
    return jax.shard_map(
        local,
        mesh=mesh,
        in_specs=(
            P("dp", "tensor"),
            P(None, "dp", None),
            P(None, "dp"),
            P(None, "dp"),
            P(None, ("dp", "tensor"), None),
            P(),
            P(None, "tensor"),
            P(None, "tensor"),
            P(None, "tensor"),
            P("tensor", None),
            P(),
            P(None, "tensor"),
            P(None, "tensor"),
            P("tensor", None),
            P(None, ("dp", "tensor")),
            P(None, ("dp", "tensor")),
            P(None, ("dp", "tensor"), None),
            P(None, ("dp", "tensor")),
            P(None, ("dp", "tensor")),
            P(None, ("dp", "tensor"), None),
            P(None, ("dp", "tensor")),
            P(None, ("dp", "tensor")),
            P(None, ("dp", "tensor")),
            P(None, ("dp", "tensor"), None),
            P(None, ("dp", "tensor")),
            P(None, ("dp", "tensor"), None),
            P(None, ("dp", "tensor")),
            P(("dp", "tensor")),
            P(("dp", "tensor")),
            P(("dp", "tensor"), None),
        ),
        out_specs=(
            P(None, ("dp", "tensor"), None),
            P("dp", "tensor"),
            P(None, ("dp", "tensor")),
            P(None, ("dp", "tensor")),
            P(None, ("dp", "tensor"), None),
            P(None, ("dp", "tensor")),
            P(None, ("dp", "tensor")),
            P(None, ("dp", "tensor"), None),
            P(None, ("dp", "tensor")),
            P(None, ("dp", "tensor")),
            P(None, ("dp", "tensor")),
            P(None, ("dp", "tensor"), None),
            P(None, ("dp", "tensor")),
            P(None, ("dp", "tensor"), None),
            P(None, ("dp", "tensor")),
            P(("dp", "tensor")),
            P(("dp", "tensor")),
            P(("dp", "tensor"), None),
        ),
        check_vma=False,
    )
```

```python
import jax
import jax.numpy as jnp
from jax import lax
from jax.experimental import pallas as pl
from jax.experimental.pallas import tpu as pltpu
from jax.sharding import PartitionSpec as P

HEAD_DIM = 64
EPS_NORM = 1e-05
HIGH = lax.Precision.HIGHEST
SQRT_HALF = 0.7071067811865476
INV_SQRT_TAU = 0.3989422804014327
BOTH = ("dp", "tensor")
F32 = jnp.float32
BF16 = jnp.bfloat16


def matmul(left, right):
    return jnp.dot(left, right, preferred_element_type=F32)


def matmul_right_t(left, right):
    return lax.dot_general(left, right, (((1,), (1,)), ((), ())), preferred_element_type=F32)


def matmul_left_t(left, right):
    return lax.dot_general(left, right, (((0,), (0,)), ((), ())), preferred_element_type=F32)


def norm_parts(values):
    centered = values - jnp.mean(values, axis=-1, keepdims=True)
    inverse = lax.rsqrt(jnp.mean(centered * centered, axis=-1, keepdims=True) + EPS_NORM)
    return (centered * inverse, inverse)


def norm_back(normed, inverse, grad_scaled):
    return inverse * (
        grad_scaled
        - jnp.mean(grad_scaled, axis=-1, keepdims=True)
        - normed * jnp.mean(grad_scaled * normed, axis=-1, keepdims=True)
    )


def rms_parts(values):
    return lax.rsqrt(jnp.mean(values * values, axis=-1, keepdims=True) + EPS_NORM)


def rms_back(values, inverse, grad_scaled):
    return inverse * grad_scaled - values * inverse**3 * jnp.mean(
        grad_scaled * values, axis=-1, keepdims=True
    )


def rotary_tables(seq_length):
    half_dim = HEAD_DIM // 2
    freqs = 10000.0 ** (-jnp.arange(half_dim, dtype=F32) * 2.0 / HEAD_DIM)
    angles = jnp.arange(seq_length, dtype=F32)[:, None] * freqs[None, :]
    angles = jnp.concatenate([angles, angles], axis=-1)
    return (jnp.cos(angles), jnp.sin(angles))


def swap(values, axis, bit):
    size = lax.axis_size(axis)
    return lax.ppermute(values, axis, [(i, i ^ bit) for i in range(size)])


def lookup_kernel(ids_ref, table_ref, _after, out_ref):
    rows = ids_ref.shape[0]
    height, width = table_ref.shape
    half = height // 2
    ids = ids_ref[...]
    upper = ids >= half
    places = jnp.where(upper, ids - half, ids)
    chosen = places == lax.broadcasted_iota(jnp.int32, (rows, half), 1)
    pairs = jnp.concatenate([table_ref[:half], table_ref[half:]], axis=1)
    found = matmul(jnp.where(chosen, 1.0, 0.0).astype(BF16), pairs)
    out_ref[...] = jnp.where(upper, found[:, width:], found[:, :width]).astype(BF16)


def lookup(ids, table, after):
    count = ids.shape[0]
    height, width = table.shape
    rows = 512
    return pl.pallas_call(
        lookup_kernel,
        grid=(count // rows,),
        in_specs=[
            pl.BlockSpec((rows, 1), lambda i: (i, 0)),
            pl.BlockSpec((height, width), lambda i: (0, 0)),
            pl.BlockSpec(memory_space=pl.ANY),
        ],
        out_specs=pl.BlockSpec((rows, width), lambda i: (i, 0)),
        out_shape=jax.ShapeDtypeStruct((count, width), BF16),
        compiler_params=pltpu.CompilerParams(vmem_limit_bytes=48 << 20),
        cost_estimate=pl.CostEstimate(
            flops=4 * count * height * width, bytes_accessed=4 * count * width, transcendentals=0
        ),
        name="lookup",
    )(ids[:, None], table, after)


def collect_kernel(ids_ref, ids_left, ids_right, left_ref, right_ref, base_ref, out_ref):
    @pl.when(pl.program_id(0) == 0)
    def _():
        out_ref[...] = jnp.zeros_like(out_ref) if base_ref is None else base_ref[...]

    height, width = out_ref.shape
    half = height // 2
    total = None
    for i, (column, rows_ref) in enumerate(((ids_left, left_ref), (ids_right, right_ref))):
        ids = ids_ref[i : i + 1, :]
        ids = jnp.where(ids >= half, ids - half, ids)
        places = lax.broadcasted_iota(jnp.int32, (half, ids.shape[1]), 0)
        chosen = jnp.where(ids == places, 1.0, 0.0).astype(BF16)
        rows = rows_ref[...].astype(F32)
        upper = column[...] >= half
        pairs = [jnp.where(upper, 0.0, rows), jnp.where(upper, rows, 0.0)]
        part = matmul(chosen, jnp.concatenate(pairs, axis=1).astype(BF16))
        total = part if total is None else total + part
    out_ref[:half] += total[:, :width]
    out_ref[half:] += total[:, width:]


def collect(ids, columns, left, right, height, base):
    count, width = left.shape
    rows = 256
    whole = pl.BlockSpec((height, width), lambda i: (0, 0))
    kernel = collect_kernel
    if base is None:
        kernel = lambda *refs: collect_kernel(*refs[:5], None, refs[5])
    return pl.pallas_call(
        kernel,
        grid=(count // rows,),
        in_specs=[pl.BlockSpec((2, rows), lambda i: (0, i))]
        + [pl.BlockSpec((rows, 1), lambda i: (i, 0))] * 2
        + [pl.BlockSpec((rows, width), lambda i: (i, 0))] * 2
        + ([] if base is None else [whole]),
        out_specs=whole,
        out_shape=jax.ShapeDtypeStruct((height, width), F32),
        compiler_params=pltpu.CompilerParams(vmem_limit_bytes=48 << 20),
        cost_estimate=pl.CostEstimate(
            flops=8 * count * height * width, bytes_accessed=8 * count * width, transcendentals=0
        ),
        name="collect",
    )(ids, *columns, left, right, *([] if base is None else [base]))


QUERY_ROWS = 256
ENTRY_LANES = 64
VMEM_LIMIT = 56 << 20


def turn_rows(values):
    half_dim = HEAD_DIM // 2
    return jnp.concatenate([-values[half_dim:], values[:half_dim]], axis=0)


def two_parts(values):
    high = values.astype(BF16)
    return jnp.concatenate([high, (values - high.astype(F32)).astype(BF16)], axis=1)


def entry_table(columns):
    return two_parts(jnp.concatenate([columns, turn_rows(columns)], axis=0))


def spread(table, onehot, trig):
    both = matmul(table, onehot) * trig
    return both[:HEAD_DIM] + both[HEAD_DIM:]


def ahead_mask(rows):
    shape = (rows, rows)
    return lax.broadcasted_iota(jnp.int32, shape, 0) <= lax.broadcasted_iota(jnp.int32, shape, 1)


def attend_kernel(
    place, part0, part1, part2, part3, gain, w_query, w_kv, ids, trig, _after_one, _after_two,
    near, far, context_t, log_total, table_q, table_kv, embeds,
    normed, onehot, keys, values_t,
):
    tokens = ids.shape[1]

    @pl.when(pl.program_id(0) == 0)
    def _():
        own = part0.shape[1]
        for k, part in enumerate((part0, part1, part2, part3)):
            embeds[k * own : (k + 1) * own, :] = part[0]
        wide = embeds[...].astype(F32)
        normed[...] = (wide * rms_parts(wide) * gain[...].astype(F32)).astype(BF16)
        places = lax.broadcasted_iota(jnp.int32, onehot.shape, 0)
        places = jnp.where(places >= ENTRY_LANES, places - ENTRY_LANES, places)
        onehot[...] = jnp.where(places == ids[...], 1.0, 0.0).astype(BF16)
        mixed = matmul(normed[...], w_kv[...]).T
        table_kv[0] = entry_table(mixed[:HEAD_DIM])
        table_kv[1] = entry_table(mixed[HEAD_DIM:])
        keys[...] = spread(table_kv[0], onehot[...], trig[...]).T.astype(BF16)
        values_t[...] = matmul(table_kv[1], onehot[...])[:HEAD_DIM].astype(BF16)

    queries = matmul(normed[...], w_query[...]).T * HEAD_DIM ** (-0.5)
    ahead = ahead_mask(QUERY_ROWS)
    turned = []
    for j in range(2):
        table_q[0, j] = entry_table(queries[j * HEAD_DIM : (j + 1) * HEAD_DIM])
        turned.append(spread(table_q[0, j], onehot[...], trig[...]).astype(BF16))
    odd = place[0] % 2
    rows_out = []

    def score(block):
        start, stop = block * QUERY_ROWS, (block + 1) * QUERY_ROWS
        return [matmul(keys[:stop], turned[j][:, start:stop]) for j in range(2)]

    blocks = tokens // QUERY_ROWS
    scores = score(0)
    for block in range(blocks):
        start, stop = block * QUERY_ROWS, (block + 1) * QUERY_ROWS
        following = score(block + 1) if block + 1 < blocks else None
        done = []
        for j in range(2):
            last = jnp.where(ahead, scores[j][start:], -1e30)
            highest = jnp.max(last, axis=0, keepdims=True)
            if block:
                highest = jnp.maximum(highest, jnp.max(scores[j][:start], axis=0, keepdims=True))
            last = jnp.exp(last - highest)
            total = jnp.sum(last, axis=0, keepdims=True)
            soft = last.astype(BF16)
            if block:
                first = jnp.exp(scores[j][:start] - highest)
                total = total + jnp.sum(first, axis=0, keepdims=True)
                soft = jnp.concatenate([first.astype(BF16), soft], axis=0)
            done.append(matmul(values_t[:, :stop], soft) / total)
            log_total[0, j : j + 1, start:stop] = highest + jnp.log(total)
        scores = following
        done = jnp.concatenate(done, axis=0)
        context_t[:, start:stop] = done.astype(BF16)
        rows_out.append(done.T.astype(BF16))
        if block % 2:
            even_rows, odd_rows = rows_out[-2:]
            target = (block // 2) ^ (place[0] // 2)
            near[target] = jnp.where(odd == 0, even_rows, odd_rows)
            far[target] = jnp.where(odd == 0, odd_rows, even_rows)


def attend(place, micro, parts, gain, w_query, w_kv, ids, trig, after):
    assert ids.shape[1] == 4 * QUERY_ROWS
    _, own, width = parts[0].shape
    entries = own * len(parts)
    tokens = ids.shape[1]
    pairs = w_query.shape[1] // (2 * HEAD_DIM)
    lanes = 2 * HEAD_DIM
    whole = lambda *shape: pl.BlockSpec(shape, lambda i: (0,) * len(shape))
    return pl.pallas_call(
        attend_kernel,
        grid=(pairs,),
        in_specs=[pl.BlockSpec(memory_space=pltpu.SMEM)]
        + [pl.BlockSpec((1, own, width), lambda i: (micro, 0, 0))] * len(parts)
        + [
            whole(1, width),
            pl.BlockSpec((width, lanes), lambda i: (0, i)),
            whole(width, lanes),
            whole(1, tokens),
            whole(lanes, tokens),
        ]
        + [pl.BlockSpec(memory_space=pl.ANY)] * 2,
        out_specs=[
            pl.BlockSpec((2, QUERY_ROWS, lanes), lambda i: (0, 0, i)),
            pl.BlockSpec((2, QUERY_ROWS, lanes), lambda i: (0, 0, i)),
            pl.BlockSpec((lanes, tokens), lambda i: (i, 0)),
            pl.BlockSpec((1, 2, tokens), lambda i: (i, 0, 0)),
            pl.BlockSpec((1, 2, lanes, lanes), lambda i: (i, 0, 0, 0)),
            whole(2, lanes, lanes),
            whole(entries, width),
        ],
        out_shape=[
            jax.ShapeDtypeStruct((2, QUERY_ROWS, pairs * lanes), BF16),
            jax.ShapeDtypeStruct((2, QUERY_ROWS, pairs * lanes), BF16),
            jax.ShapeDtypeStruct((pairs * lanes, tokens), BF16),
            jax.ShapeDtypeStruct((pairs, 2, tokens), F32),
            jax.ShapeDtypeStruct((pairs, 2, lanes, lanes), BF16),
            jax.ShapeDtypeStruct((2, lanes, lanes), BF16),
            jax.ShapeDtypeStruct((entries, width), BF16),
        ],
        scratch_shapes=[
            pltpu.VMEM((entries, width), BF16),
            pltpu.VMEM((lanes, tokens), BF16),
            pltpu.VMEM((tokens, HEAD_DIM), BF16),
            pltpu.VMEM((HEAD_DIM, tokens), BF16),
        ],
        compiler_params=pltpu.CompilerParams(vmem_limit_bytes=VMEM_LIMIT),
        cost_estimate=pl.CostEstimate(
            flops=12 * 10**9, bytes_accessed=8 * 10**6, transcendentals=5 * 10**6
        ),
        name="attend",
    )(place, *parts, gain, w_query, w_kv, ids, trig, *after)


def attend_back_kernel(
    place, part0, part1, part2, part3, context_t, log_total, table_q, table_kv, ids, ids_share, trig,
    w_query, w_kv, embeds, gain, grad_hidden, _a0, _a1, _a2, _a3, _a4, grads0, grads1, grads2, grads3,
    onehot, columns, keys, keys_t, values, grad_keys, grad_values, total, grad_context,
):
    tokens = ids.shape[1]
    share = part0.shape[0]
    for k, part in enumerate((part0, part1, part2, part3)):
        first = pl.multiple_of((place[0] ^ k) * share, share)
        grad_context[pl.ds(first, share), :] = part[...]
    entries = embeds.shape[0]
    cosine, sine = trig[:HEAD_DIM], trig[HEAD_DIM:]

    @pl.when(pl.program_id(0) == 0)
    def _():
        places = lax.broadcasted_iota(jnp.int32, onehot.shape, 0)
        places = jnp.where(places >= ENTRY_LANES, places - ENTRY_LANES, places)
        chosen = jnp.where(places == ids[...], 1.0, 0.0)
        onehot[...] = chosen.astype(BF16)
        columns[...] = chosen.T.astype(BF16)
        turned = spread(table_kv[0], onehot[...], trig[...])
        keys_t[...] = turned.astype(BF16)
        keys[...] = turned.T.astype(BF16)
        values[...] = matmul(table_kv[1], onehot[...])[:HEAD_DIM].T.astype(BF16)
        grad_keys[...] = jnp.zeros_like(grad_keys)
        grad_values[...] = jnp.zeros_like(grad_values)
        total[...] = jnp.zeros_like(total)

    def to_entries(grads, cos_part, sin_part, rows):
        straight = matmul((grads * cos_part).astype(BF16), rows)
        crossed = matmul((grads * sin_part).astype(BF16), rows)
        return straight, crossed

    def two_stacked(grads):
        high = grads.astype(BF16)
        rest = (grads - high.astype(F32)).astype(BF16)
        lane = lax.broadcasted_iota(jnp.int32, grads.shape, 1)
        return jnp.where(lane < ENTRY_LANES, high.astype(F32), rest.astype(F32)).T.astype(BF16)

    ahead = ahead_mask(QUERY_ROWS)
    grad_t = grad_context[...].astype(F32).T
    products = grad_t * context_t[...].astype(F32)
    grad_t = grad_t.astype(BF16)
    heads = [slice(j * HEAD_DIM, (j + 1) * HEAD_DIM) for j in range(2)]
    turned = [spread(table_q[0, j], onehot[...], trig[...]) for j in range(2)]
    queries_t = [part.astype(BF16) for part in turned]
    queries = [part.T.astype(BF16) for part in turned]
    offset = [jnp.sum(products[head], axis=0, keepdims=True) for head in heads]
    turned_back = [[], []]

    def score(block, j):
        start, stop = block * QUERY_ROWS, (block + 1) * QUERY_ROWS
        return (
            matmul(keys[:stop], queries_t[j][:, start:stop]),
            matmul(values[:stop], grad_t[heads[j], start:stop]),
        )

    order = [(block, j) for block in range(tokens // QUERY_ROWS) for j in range(2)]
    sums = [[None, None] for _ in range(tokens // QUERY_ROWS)]

    def weigh(block, j, scores, grad_soft):
        start, stop = block * QUERY_ROWS, (block + 1) * QUERY_ROWS
        soft = jnp.exp(scores - log_total[0, j : j + 1, start:stop])
        last = jnp.where(ahead, soft[start:], 0.0)
        soft = jnp.concatenate([soft[:start], last], axis=0) if block else last
        grad_scores = (soft * (grad_soft - offset[j][:, start:stop])).astype(BF16)
        return soft.astype(BF16), grad_scores

    def gather_up(block, j, soft, grad_scores):
        start, stop = block * QUERY_ROWS, (block + 1) * QUERY_ROWS
        for kind, part in enumerate(
            (
                matmul(soft, grad_context[start:stop, heads[j]]),
                matmul(grad_scores, queries[j][start:stop]),
            )
        ):
            for i in range(block + 1):
                piece = part[i * QUERY_ROWS : (i + 1) * QUERY_ROWS]
                held = sums[i][kind]
                sums[i][kind] = piece if held is None else held + piece
        grad_queries = matmul(keys_t[:, :stop], grad_scores) * HEAD_DIM ** (-0.5)
        turned_back[j].append(
            jnp.concatenate(
                [grad_queries * cosine[:, start:stop], grad_queries * sine[:, start:stop]], axis=0
            ).astype(BF16)
        )

    ready = score(*order[0])
    waiting = None
    for i, item in enumerate(order):
        current = ready
        ready = score(*order[i + 1]) if i + 1 < len(order) else None
        if waiting is not None:
            gather_up(*waiting)
        waiting = (*item, *weigh(*item, *current))
    gather_up(*waiting)
    for i, (value_sum, key_sum) in enumerate(sums):
        lines = slice(i * QUERY_ROWS, (i + 1) * QUERY_ROWS)
        grad_values[lines] += value_sum
        grad_keys[lines] += key_sum
    both = jnp.concatenate([jnp.concatenate(parts, axis=1) for parts in turned_back], axis=0)
    both = matmul(both, columns[...])
    per_head = []
    for j in range(2):
        at = 2 * HEAD_DIM * j
        straight, crossed = both[at : at + HEAD_DIM], both[at + HEAD_DIM : at + 2 * HEAD_DIM]
        per_head.append(straight - turn_rows(crossed))
    total[...] += matmul_right_t(two_stacked(jnp.concatenate(per_head, axis=0)), w_query[...])

    @pl.when(pl.program_id(0) == pl.num_programs(0) - 1)
    def _():
        grads = jnp.concatenate([grad_keys[...], grad_values[...]], axis=1).T
        straight, crossed = to_entries(grads[:HEAD_DIM], cosine, sine, columns[...])
        summed = matmul(grads[HEAD_DIM:].astype(BF16), columns[...])
        both = jnp.concatenate([straight - turn_rows(crossed), summed], axis=0)
        full = total[...] + matmul_right_t(two_stacked(both), w_kv[...])
        scaled = (full[:entries] + full[entries:]) * gain[...].astype(F32)
        wide = embeds[...].astype(F32)
        places = lax.broadcasted_iota(jnp.int32, (entries, ids_share.shape[1]), 0)
        chosen = jnp.where(places == ids_share[...], 1.0, 0.0).astype(BF16)
        result = rms_back(wide, rms_parts(wide), scaled) + matmul(chosen, grad_hidden[...])
        result = result.astype(BF16)
        own = grads0.shape[0]
        for k, out in enumerate((grads0, grads1, grads2, grads3)):
            out[...] = result[k * own : (k + 1) * own]


def attend_back(
    place, parts, kept, ids, ids_share, trig, w_query, w_kv, gain, grad_hidden, after
):
    context_t, log_total, table_q, table_kv, embeds = kept
    share = parts[0].shape[0]
    entries, width = embeds.shape
    tokens = ids.shape[1]
    pairs = w_query.shape[1] // (2 * HEAD_DIM)
    lanes = 2 * HEAD_DIM
    whole = lambda *shape: pl.BlockSpec(shape, lambda i: (0,) * len(shape))
    return pl.pallas_call(
        attend_back_kernel,
        grid=(pairs,),
        in_specs=[pl.BlockSpec(memory_space=pltpu.SMEM)]
        + [pl.BlockSpec((share, lanes), lambda i: (0, i))] * len(parts)
        + [
            pl.BlockSpec((lanes, tokens), lambda i: (i, 0)),
            pl.BlockSpec((1, 2, tokens), lambda i: (i, 0, 0)),
            pl.BlockSpec((1, 2, lanes, lanes), lambda i: (i, 0, 0, 0)),
            whole(2, lanes, lanes),
            whole(1, tokens),
            whole(*ids_share.shape),
            whole(lanes, tokens),
            pl.BlockSpec((width, lanes), lambda i: (0, i)),
            whole(width, lanes),
            whole(entries, width),
            whole(1, width),
            whole(*grad_hidden.shape),
        ]
        + [pl.BlockSpec(memory_space=pl.ANY)] * 5,
        out_specs=[whole(entries // 4, width)] * 4,
        out_shape=[jax.ShapeDtypeStruct((entries // 4, width), BF16)] * 4,
        scratch_shapes=[
            pltpu.VMEM((lanes, tokens), BF16),
            pltpu.VMEM((tokens, lanes), BF16),
            pltpu.VMEM((tokens, HEAD_DIM), BF16),
            pltpu.VMEM((HEAD_DIM, tokens), BF16),
            pltpu.VMEM((tokens, HEAD_DIM), BF16),
            pltpu.VMEM((tokens, HEAD_DIM), F32),
            pltpu.VMEM((tokens, HEAD_DIM), F32),
            pltpu.VMEM((2 * entries, width), F32),
            pltpu.VMEM((tokens, lanes), BF16),
        ],
        compiler_params=pltpu.CompilerParams(vmem_limit_bytes=VMEM_LIMIT),
        cost_estimate=pl.CostEstimate(
            flops=25 * 10**9, bytes_accessed=8 * 10**6, transcendentals=5 * 10**6
        ),
        name="attend_back",
    )(
        place, *parts, context_t, log_total, table_q, table_kv, ids, ids_share, trig,
        w_query, w_kv, embeds, gain, grad_hidden, *after,
    )


ANY_SPEC = pl.BlockSpec(memory_space=pl.ANY)


def pick_rows(ids, entries):
    places = lax.broadcasted_iota(jnp.int32, (entries, ids.shape[1]), 0)
    return jnp.where(places == ids[...], 1.0, 0.0).astype(BF16)


def load_weights(sources, targets, sems):
    copies = [
        pltpu.make_async_copy(source, target, sems.at[i])
        for i, (source, target) in enumerate(zip(sources, targets))
    ]
    for copy in copies:
        copy.start()
    return copies


def hidden_kernel(
    embeds, ids_own, ids_peer, gain, c0, c1, c2, c3, w0, w1, w2, w3, _after_one, _after_two,
    normed_own, normed_peer, hidden, held, sems,
):
    heads = w0.shape[0]
    copies = load_weights(
        (w0, w1, w2, w3), [held.at[pl.ds(k * heads, heads)] for k in range(4)], sems
    )
    rows = jnp.concatenate([pick_rows(ids_own, embeds.shape[0]), pick_rows(ids_peer, embeds.shape[0])], axis=1)
    total = matmul_left_t(rows, embeds[...])
    for first, (left, right) in ((0, (c0, c1)), (2, (c2, c3))):
        own = first // 2
        sides = [jnp.concatenate([part[own], part[1 - own]], axis=0) for part in (left, right)]
        copies[first].wait()
        copies[first + 1].wait()
        both = jnp.concatenate(sides, axis=1)
        total = total + matmul(both, held[first * heads : (first + 2) * heads])
    low = (total * rms_parts(total) * gain[...].astype(F32)).astype(BF16)
    share = normed_own.shape[0]
    normed_own[...] = low[:share]
    normed_peer[...] = low[share:]
    hidden[...] = total[:share]


def hidden_rows_of(embeds, ids_own, ids_peer, gain, parts, weights, after):
    rows, width = ids_own.shape[1], embeds.shape[1]
    vmem = pl.BlockSpec(memory_space=pltpu.VMEM)
    return pl.pallas_call(
        hidden_kernel,
        in_specs=[vmem] * 8 + [ANY_SPEC] * 6,
        out_specs=[vmem] * 3,
        out_shape=[
            jax.ShapeDtypeStruct((rows, width), BF16),
            jax.ShapeDtypeStruct((rows, width), BF16),
            jax.ShapeDtypeStruct((rows, width), F32),
        ],
        scratch_shapes=[
            pltpu.VMEM((4 * weights[0].shape[0], width), BF16),
            pltpu.SemaphoreType.DMA((4,)),
        ],
        compiler_params=pltpu.CompilerParams(vmem_limit_bytes=VMEM_LIMIT),
        cost_estimate=pl.CostEstimate(
            flops=6 * 10**9, bytes_accessed=18 * 10**6, transcendentals=0
        ),
        name="hidden",
    )(embeds, ids_own, ids_peer, gain, *parts, *weights, *after)


def hidden_back_kernel(
    cotangent, hidden, kept, core_a, core_b, from_chip, gain, w0, w1, w2, w3,
    low, p0, p1, p2, p3, held, sems,
):
    copies = load_weights((w2, w3, w1, w0), [held.at[k] for k in range(4)], sems)
    from_core = jnp.concatenate([core_a[...], core_b[...]], axis=0)
    grads = kept[...].astype(F32) + from_core.astype(F32) + from_chip[...].astype(F32)
    rows = hidden[...]
    scaled = grads * gain[...].astype(F32)
    total = cotangent[0] + rms_back(rows, rms_parts(rows), scaled)
    total = total.astype(BF16)
    low[...] = total
    for k, part in enumerate((p2, p3, p1, p0)):
        copies[k].wait()
        part[...] = matmul_right_t(total, held[k]).astype(BF16)


def hidden_back(micro, cotangent, hidden, kept, from_core, from_chip, gain, weights):
    rows, width = hidden.shape
    heads = weights[0].shape[0]
    whole = lambda *shape: pl.BlockSpec(shape, lambda i: (0,) * len(shape))
    return pl.pallas_call(
        hidden_back_kernel,
        grid=(1,),
        in_specs=[
            pl.BlockSpec((1, rows, width), lambda i: (micro, 0, 0)),
            whole(rows, width),
            whole(rows, width),
            whole(rows // 2, width),
            whole(rows // 2, width),
            whole(rows, width),
            whole(1, width),
        ]
        + [ANY_SPEC] * 4,
        out_specs=[whole(rows, width)] + [whole(rows, heads)] * 4,
        out_shape=[jax.ShapeDtypeStruct((rows, width), BF16)]
        + [jax.ShapeDtypeStruct((rows, heads), BF16)] * 4,
        scratch_shapes=[
            pltpu.VMEM((4, heads, width), BF16),
            pltpu.SemaphoreType.DMA((4,)),
        ],
        compiler_params=pltpu.CompilerParams(vmem_limit_bytes=VMEM_LIMIT),
        cost_estimate=pl.CostEstimate(
            flops=2 * 10**9, bytes_accessed=16 * 10**6, transcendentals=0
        ),
        name="hidden_back",
    )(cotangent, hidden, kept, *from_core, from_chip, gain, *weights)


def mlp_kernel(
    ready, x_mine, x_other, mine_in, other_in, gate_hbm, up_hbm, down_hbm,
    _after_one, _after_two, _after_three,
    out_mine, out_other, grad_mine, grad_a, grad_b,
    w_both, w_down, sems,
):
    units = w_down.shape[0]
    main = units // 256 * 256
    rest = units - main
    cuts = ((0, gate_hbm, 0, main), (main, up_hbm, 0, main), (2 * main, gate_hbm, main, rest),
            (2 * main + rest, up_hbm, main, rest))
    copies = load_weights(
        [source.at[:, pl.ds(at, size)] for _, source, at, size in cuts if size] + [down_hbm],
        [w_both.at[:, pl.ds(to, size)] for to, _, _, size in cuts if size] + [w_down],
        sems,
    )
    halves = ((x_other, other_in), (x_mine, mine_in))
    copies[0].wait()
    gates = [matmul(rows[...], w_both[:, :main]) for rows, _ in halves]
    for copy in copies[1:-1]:
        copy.wait()
    others = [matmul(rows[...], w_both[:, main:]) for rows, _ in halves]
    copies[-1].wait()
    if ready:
        grads_active = [cots[...].astype(F32) for _, cots in halves]
    else:
        grads_active = [matmul_right_t(cots[...], w_down[...]) for _, cots in halves]
    middle = []
    for gate, other, grad_active in zip(gates, others, grads_active):
        gate = jnp.concatenate([gate, other[:, main : main + rest]], axis=1)
        upward = jnp.concatenate([other[:, :main], other[:, main + rest :]], axis=1)
        sigmoid = 1.0 / (1.0 + jnp.exp(-gate))
        silu = gate * sigmoid
        activated = (silu * upward).astype(BF16)
        grad_gate = grad_active * upward * (sigmoid * (1.0 + gate * (1.0 - sigmoid)))
        grad_gate = grad_gate.astype(BF16)
        grad_up = (grad_active * silu).astype(BF16)
        parts = [grad_gate[:, :main], grad_up[:, :main], grad_gate[:, main:], grad_up[:, main:]]
        middle.append((activated, jnp.concatenate(parts, axis=1)))
    for (activated, grads), out, grad in zip(middle, (out_other, out_mine), (None, grad_mine)):
        total = matmul_right_t(grads, w_both[...]).astype(BF16)
        if grad is None:
            half = grad_a.shape[0]
            grad_a[...] = total[:half]
            grad_b[...] = total[half:]
        else:
            grad[...] = total
        out[...] = matmul(activated, w_down[...]).astype(BF16)


def mlp(mine, other, mine_in, other_in, w_gate, w_up, w_down, after):
    rows, width = mine.shape
    units = w_gate.shape[1]
    assert units % 256 in (0, 128)
    ready = mine_in.shape[1] == units
    vmem = pl.BlockSpec(memory_space=pltpu.VMEM)
    return pl.pallas_call(
        lambda *refs: mlp_kernel(ready, *refs),
        in_specs=[vmem] * 4 + [ANY_SPEC] * 6,
        out_specs=[vmem] * 5,
        out_shape=[jax.ShapeDtypeStruct((rows, width), BF16)] * 3
        + [jax.ShapeDtypeStruct((rows // 2, width), BF16)] * 2,
        scratch_shapes=[
            pltpu.VMEM((width, 2 * units), BF16),
            pltpu.VMEM((units, width), BF16),
            pltpu.SemaphoreType.DMA((5,)),
        ],
        compiler_params=pltpu.CompilerParams(vmem_limit_bytes=VMEM_LIMIT),
        cost_estimate=pl.CostEstimate(
            flops=24 * rows * width * units, bytes_accessed=26 * 10**6, transcendentals=2 * rows * units
        ),
        name="mlp",
    )(mine, other, mine_in, other_in, w_gate, w_up, w_down, *after)


def cast_kernel(values, _after, out):
    out[...] = values[0].astype(BF16)


def cast_after(micro, values, after):
    _, rows, width = values.shape
    steps = 4
    return pl.pallas_call(
        cast_kernel,
        grid=(steps,),
        in_specs=[pl.BlockSpec((1, rows // steps, width), lambda i: (micro, i, 0)), ANY_SPEC],
        out_specs=pl.BlockSpec((rows // steps, width), lambda i: (i, 0)),
        out_shape=jax.ShapeDtypeStruct((rows, width), BF16),
        name="cast_after",
    )(values, after)


def tie_kernel(_values, _after, _out):
    pass


def tie(values, after):
    return pl.pallas_call(
        tie_kernel,
        in_specs=[ANY_SPEC] * 2,
        out_specs=ANY_SPEC,
        out_shape=jax.ShapeDtypeStruct(values.shape, values.dtype),
        input_output_aliases={0: 0},
        name="tie",
    )(values, after)


def results_kernel(*refs):
    out = refs[9]
    for micro in range(2):
        first, *rest = refs[4 * micro : 4 * micro + 4]
        total = first[...]
        for part in rest:
            total = total + part[...].astype(F32)
        out[micro] = total.astype(BF16)


def add_results(first, second, after):
    rows, width = first[0].shape
    steps = 4
    part = pl.BlockSpec((rows // steps, width), lambda i: (i, 0))
    return pl.pallas_call(
        results_kernel,
        grid=(steps,),
        in_specs=[part] * 8 + [ANY_SPEC],
        out_specs=pl.BlockSpec((2, rows // steps, width), lambda i: (0, i, 0)),
        out_shape=jax.ShapeDtypeStruct((2, rows, width), BF16),
        name="results",
    )(*first, *second, after)


BLOCKS = 32
UNIT = 16
LAYER_UNITS = 12
VECTORS = 8


def square(ref):
    blocks, rows, width = ref.shape
    return ref[...].reshape(blocks * rows, width)


def entry_bias(valid, slots):
    shape = (valid.shape[1], valid.shape[1])
    same = lax.broadcasted_iota(jnp.int32, shape, 0) // slots == lax.broadcasted_iota(
        jnp.int32, shape, 1
    ) // slots
    return jnp.where(jnp.logical_and(same, valid > 0.5), 0.0, -1e30)


def entry_scores(queries, keys, bias):
    return matmul_right_t(queries, keys) * HEAD_DIM ** (-0.5) + bias


def entry_soft(scores):
    expon = jnp.exp(scores - jnp.max(scores, axis=1, keepdims=True))
    return expon / jnp.sum(expon, axis=1, keepdims=True)


def bell(values):
    return 0.5 * (1.0 + lax.erf(values * SQRT_HALF))


def lay_out_vectors(small, vectors, inner_bias):
    blocks, rows, lanes = small.shape

    def spread_rows(values, each, width):
        shape = (lanes, width)
        line = lax.broadcasted_iota(jnp.int32, shape, 0)
        column = lax.broadcasted_iota(jnp.int32, shape, 1)
        copies = jnp.where(column % each == line, 1.0, 0.0).astype(BF16)
        wide = matmul(values, copies).reshape(blocks, values.shape[0] // blocks, width)
        block = lax.broadcasted_iota(jnp.int32, wide.shape, 0)
        column = lax.broadcasted_iota(jnp.int32, wide.shape, 2)
        return jnp.sum(jnp.where(column // each == block, wide, 0.0), axis=0)

    count, width = vectors.shape
    layers, inner_width = inner_bias.shape
    values = small[...]
    vectors[...] = spread_rows(values.reshape(blocks * rows, lanes), UNIT, width)[:count]
    line = lax.broadcasted_iota(jnp.int32, values.shape, 1)
    for layer in range(layers):
        chosen = jnp.where(line == count + layer, values.astype(F32), 0.0)
        chosen = jnp.sum(chosen, axis=1).astype(BF16)
        inner_bias[layer : layer + 1, :] = spread_rows(chosen, 4 * UNIT, inner_width)


def hyper_kernel(
    slots, place, _a0, _a1, _a2, _a3, _a4, _a5, _a6, _a7, _a8, _a9, _a10, _a11, part0, part1, part2, part3, valid, small, outer, w_q, w_k, w_v, w_o, in0, in1, in2, in3,
    pr0, pr1, pr2, pr3,
    vectors, inner_bias, below, mixed, context, middle, inner, pooled, pooled_norm, embeds,
    state, joined,
):
    layer = pl.program_id(0)
    layers = pl.num_programs(0)
    rows, width = state.shape

    @pl.when(layer == 0)
    def _():
        columns = part0.shape[1]
        for k, part in enumerate((part0, part1, part2, part3)):
            at = pl.multiple_of((place[0] ^ k) * columns, columns)
            state[:, pl.ds(at, columns)] = part[...].astype(F32)
        lay_out_vectors(small, vectors, inner_bias)

    def vector(index):
        return vectors[pl.ds(index * layers + layer, 1), :]

    hidden = state[...]
    below[0] = hidden
    normed, _ = norm_parts(hidden)
    normed_in = (normed * vector(0) + vector(1)).astype(BF16)
    queries = (matmul(normed_in, square(w_q)) + vector(2)).astype(BF16)
    keys = matmul(normed_in, square(w_k)).astype(BF16)
    values = (matmul(normed_in, square(w_v)) + vector(3)).astype(BF16)
    mixed[0, :, :width] = queries
    mixed[0, :, width : 2 * width] = keys
    mixed[0, :, 2 * width :] = values
    bias = entry_bias(valid[...], slots)
    heads = [slice(i, i + HEAD_DIM) for i in range(0, width, HEAD_DIM)]
    scores = [entry_scores(queries[:, at], keys[:, at], bias) for at in heads]
    soft = [entry_soft(part).astype(BF16) for part in scores]
    parts = [matmul(part, values[:, at]) for part, at in zip(soft, heads)]
    joined[...] = jnp.concatenate(parts, axis=1)
    context_low = joined[...].astype(BF16)
    context[0] = context_low
    centre = hidden + matmul(context_low, square(w_o)) + vector(4)
    middle[0] = centre
    normed, _ = norm_parts(centre)
    normed_mid = (normed * vector(5) + vector(6)).astype(BF16)
    total = centre + vector(7)
    for j, piece in enumerate((in0, in1, in2, in3)):
        at = slice(j * width, (j + 1) * width)
        part = matmul(normed_mid, square(piece)) + inner_bias[pl.ds(layer, 1), at]
        inner[0, :, at] = part
        activated = (part * bell(part)).astype(BF16)
        blocks = BLOCKS // 4
        total = total + matmul(
            activated, outer[j * blocks : (j + 1) * blocks].reshape(width, width)
        )
    state[...] = total

    @pl.when(layer == layers - 1)
    def _():
        slot = lax.broadcasted_iota(jnp.int32, (rows, width), 0) % slots
        first = jnp.where(slot == 0, total, 0.0).reshape(rows // slots, slots, width)
        first = jnp.sum(first, axis=1)
        pooled[...] = first
        normed, _ = norm_parts(first)
        low = (normed * vectors[VECTORS * layers : VECTORS * layers + 1, :]
               + vectors[VECTORS * layers + 1 : VECTORS * layers + 2, :]).astype(BF16)
        pooled_norm[...] = low
        for j, piece in enumerate((pr0, pr1, pr2, pr3)):
            embeds[:, j * width : (j + 1) * width] = matmul(low, square(piece)).astype(BF16)


def layer_specs(width, which):
    specs = [pl.BlockSpec((BLOCKS, 4 * UNIT, width), lambda i: (0, which(i) * LAYER_UNITS // 4, 0))]
    for j in range(4, LAYER_UNITS):
        specs.append(
            pl.BlockSpec((BLOCKS, UNIT, width), lambda i, j=j: (0, which(i) * LAYER_UNITS + j, 0))
        )
    return specs


def proj_specs(width, layers):
    return [
        pl.BlockSpec((BLOCKS, UNIT, width), lambda i, j=j: (0, layers * LAYER_UNITS + j, 0))
        for j in range(4)
    ]


def whole_spec(*shape):
    return pl.BlockSpec(shape, lambda i: (0,) * len(shape))


def hyper_forward(where, after, parts, valid, packed, slots, layers):
    rows, width = parts[0].shape[0], len(parts) * parts[0].shape[1]
    inner_width = 4 * width
    count = VECTORS * layers + 2
    last_rows = packed.shape[1] // (2 * UNIT) - 1
    entries = rows // slots
    by_layer = lambda *shape: pl.BlockSpec((1,) + shape, lambda i: (i,) + (0,) * len(shape))
    return pl.pallas_call(
        lambda *refs: hyper_kernel(slots, *refs),
        grid=(layers,),
        in_specs=[pl.BlockSpec(memory_space=pltpu.SMEM)]
        + [pl.BlockSpec(memory_space=pl.ANY)] * 12
        + [whole_spec(*part.shape) for part in parts]
        + [
            whole_spec(1, rows),
            pl.BlockSpec((BLOCKS, 2 * UNIT, 128), lambda i: (0, last_rows, 0)),
        ]
        + layer_specs(width, lambda i: i)
        + proj_specs(width, layers),
        out_specs=[
            whole_spec(count, width),
            whole_spec(layers, inner_width),
            by_layer(rows, width),
            by_layer(rows, 3 * width),
            by_layer(rows, width),
            by_layer(rows, width),
            by_layer(rows, inner_width),
            whole_spec(entries, width),
            whole_spec(entries, width),
            whole_spec(entries, 4 * width),
        ],
        out_shape=[
            jax.ShapeDtypeStruct((count, width), F32),
            jax.ShapeDtypeStruct((layers, inner_width), F32),
            jax.ShapeDtypeStruct((layers, rows, width), F32),
            jax.ShapeDtypeStruct((layers, rows, 3 * width), BF16),
            jax.ShapeDtypeStruct((layers, rows, width), BF16),
            jax.ShapeDtypeStruct((layers, rows, width), F32),
            jax.ShapeDtypeStruct((layers, rows, inner_width), F32),
            jax.ShapeDtypeStruct((entries, width), F32),
            jax.ShapeDtypeStruct((entries, width), BF16),
            jax.ShapeDtypeStruct((entries, 4 * width), BF16),
        ],
        scratch_shapes=[pltpu.VMEM((rows, width), F32), pltpu.VMEM((rows, width), F32)],
        compiler_params=pltpu.CompilerParams(vmem_limit_bytes=VMEM_LIMIT),
        cost_estimate=pl.CostEstimate(
            flops=8 * 10**9, bytes_accessed=25 * 10**6, transcendentals=4 * 10**6
        ),
        name="hyper",
    )(where, *after, *parts, valid, *([packed] * (1 + LAYER_UNITS - 3 + 4)))


def hyper_back_kernel(
    slots, layer, layers, last,
    *refs,
):
    place, refs = refs[0], refs[1:]
    if last:
        arrivals, (pooled, pooled_norm, pr0, pr1, pr2, pr3) = refs[:8], refs[8:14]
        refs = refs[14:]
    else:
        grad_start = refs[0]
        refs = refs[1:]
    valid, vectors, below, mixed, context, middle, inner = refs[2:9]
    outer, w_q, w_k, w_v, w_o, in0, in1, in2, in3 = refs[9:18]
    refs = refs[18:]
    if layer == 0:
        small_above, inner_above = refs[:2]
        refs = refs[2:]
    packed = refs[:4]
    grad_below, small, inner_small, grad_mixed = refs[4:8]
    _, rows, width = below.shape
    blocks = BLOCKS // 4
    core, chip, side, line = place[0], place[1], place[2], place[3]
    half = packed[0].shape[3]

    def vector(index):
        at = index * layers + layer
        return vectors[at : at + 1, :]

    def put_rows(lines, at, rows_each, values):
        for i, z in enumerate(lines):
            for x in range(2):
                for y in range(2):
                    left, right = values[i, x, y, 0], values[i, x, y, 1]
                    mine = jnp.where(core == 0, left, right)
                    other = jnp.where(core == 0, right, left)
                    for kind, part in enumerate((mine, other)):
                        if at < half:
                            where = pl.ds(at, rows_each)
                            packed[kind][y ^ chip, x ^ side, (z - line) & 3, where, :] = part
                        else:
                            where = pl.ds(at - half, rows_each)
                            packed[2 + kind][x ^ side, y ^ chip, (z - line) & 3, where, :] = part

    def put(unit, grads):
        grads = grads.astype(BF16).reshape(4, 2, 2, 2, UNIT, width)
        put_rows(range(4), unit * UNIT, UNIT, grads)

    def column_sum(values):
        return jnp.sum(values, axis=0, keepdims=True)

    if last:
        normed, inverse = norm_parts(pooled[...])
        grad_norm = jnp.zeros(normed.shape, F32)
        sums = []
        for group in (arrivals[:4], arrivals[4:]):
            total = group[0][...].astype(F32)
            for part in group[1:]:
                total = total + part[...].astype(F32)
            sums.append(total)
        grad_embeds = jnp.concatenate(sums, axis=0).astype(BF16)
        for j, piece in enumerate((pr0, pr1, pr2, pr3)):
            part = grad_embeds[:, j * width : (j + 1) * width]
            put(LAYER_UNITS + j, matmul_left_t(pooled_norm[...], part))
            grad_norm = grad_norm + matmul_right_t(part, square(piece))
        small[VECTORS : VECTORS + 1, :] = column_sum(grad_norm * normed)
        small[VECTORS + 1 : VECTORS + 2, :] = column_sum(grad_norm)
        final_gain = vectors[VECTORS * layers : VECTORS * layers + 1, :]
        grad_pooled = norm_back(normed, inverse, grad_norm * final_gain)
        slot = lax.broadcasted_iota(jnp.int32, (rows, width), 0) % slots
        grad_rows = jnp.broadcast_to(grad_pooled[:, None, :], (rows // slots, slots, width))
        grad_rows = jnp.where(slot == 0, grad_rows.reshape(rows, width), 0.0)
    else:
        grad_rows = grad_start[...]

    low = grad_rows.astype(BF16)
    small[7:8, :] = column_sum(grad_rows)
    normed_two, inverse_two = norm_parts(middle[0])
    normed_mid = (normed_two * vector(5) + vector(6)).astype(BF16)
    grad_mid = jnp.zeros(grad_rows.shape, F32)
    for j, piece in enumerate((in0, in1, in2, in3)):
        at = slice(j * width, (j + 1) * width)
        part = inner[0, :, at]
        share = bell(part)
        activated = (part * share).astype(BF16)
        slope = share + part * jnp.exp(-0.5 * part * part) * INV_SQRT_TAU
        where = slice(j * blocks, (j + 1) * blocks)
        grad_outer = matmul_left_t(activated, low).astype(BF16)
        put_rows((j,), 0, 4 * UNIT, grad_outer.reshape(1, 2, 2, 2, 4 * UNIT, width))
        grad_part = matmul_right_t(low, outer[where].reshape(width, width)) * slope
        inner_small[:, at] = column_sum(grad_part)
        grad_part = grad_part.astype(BF16)
        put(8 + j, matmul_left_t(normed_mid, grad_part))
        grad_mid = grad_mid + matmul_right_t(grad_part, square(piece))
    small[5:6, :] = column_sum(grad_mid * normed_two)
    small[6:7, :] = column_sum(grad_mid)
    grad_rows = grad_rows + norm_back(normed_two, inverse_two, grad_mid * vector(5))
    small[4:5, :] = column_sum(grad_rows)
    low = grad_rows.astype(BF16)
    put(7, matmul_left_t(context[0], low))
    grad_context = matmul_right_t(low, square(w_o)).astype(BF16)
    bias = entry_bias(valid[...], slots)
    heads = [slice(i, i + HEAD_DIM) for i in range(0, width, HEAD_DIM)]
    queries, keys, values = (
        [mixed[0, :, i * width + at.start : i * width + at.stop] for at in heads] for i in range(3)
    )
    grads = [grad_context[:, at] for at in heads]
    scores = [entry_scores(q, k, bias) for q, k in zip(queries, keys)]
    grad_soft = [matmul_right_t(g, v) for g, v in zip(grads, values)]
    soft = [entry_soft(part) for part in scores]
    grad_scores = []
    for part, grad in zip(soft, grad_soft):
        offset = jnp.sum(part * grad, axis=1, keepdims=True)
        grad_scores.append((part * (grad - offset) * HEAD_DIM ** (-0.5)).astype(BF16))
    soft = [part.astype(BF16) for part in soft]
    grad_mixed[:, :width] = jnp.concatenate(
        [matmul(g, k) for g, k in zip(grad_scores, keys)], axis=1
    )
    grad_mixed[:, width : 2 * width] = jnp.concatenate(
        [matmul_left_t(g, q) for g, q in zip(grad_scores, queries)], axis=1
    )
    grad_mixed[:, 2 * width :] = jnp.concatenate(
        [matmul_left_t(p, g) for p, g in zip(soft, grads)], axis=1
    )
    normed_one, inverse_one = norm_parts(below[0])
    normed_in = (normed_one * vector(0) + vector(1)).astype(BF16)
    grad_in = jnp.zeros(grad_rows.shape, F32)
    for i, piece in enumerate((w_q, w_k, w_v)):
        part = grad_mixed[:, i * width : (i + 1) * width]
        if i != 1:
            small[2 + i // 2 : 3 + i // 2, :] = column_sum(part)
        part = part.astype(BF16)
        put(4 + i, matmul_left_t(normed_in, part))
        grad_in = grad_in + matmul_right_t(part, square(piece))
    small[0:1, :] = column_sum(grad_in * normed_one)
    small[1:2, :] = column_sum(grad_in)
    grad_rows = grad_rows + norm_back(normed_one, inverse_one, grad_in * vector(0))
    if layer == 0:
        part = grad_rows.astype(BF16)
        columns = grad_below.shape[2]
        for t in range(grad_below.shape[0]):
            grad_below[t ^ (2 * chip + core)] = part[:, t * columns : (t + 1) * columns]
        wide = refs[8]
        wide[...] = jnp.zeros_like(wide)
        own = small[...]
        above = small_above[...]
        for b in range(BLOCKS):
            at = slice(b * UNIT, (b + 1) * UNIT)
            for i in range(layers):
                source = own if i == 0 else above
                wide[b, i * VECTORS : (i + 1) * VECTORS, 0:UNIT] = source[:VECTORS, at]
            wide[b, VECTORS * layers : VECTORS * layers + 2, 0:UNIT] = above[VECTORS:, at]
            at = slice(b * 4 * UNIT, (b + 1) * 4 * UNIT)
            wide[b, VECTORS * layers + 2 : VECTORS * layers + 3, 0 : 4 * UNIT] = inner_small[:, at]
            wide[b, VECTORS * layers + 3 : VECTORS * layers + 4, 0 : 4 * UNIT] = inner_above[:, at]
        base = LAYER_UNITS * UNIT
        spare = jnp.zeros((BLOCKS, 2 * UNIT, width - wide.shape[2]), F32)
        full = jnp.concatenate([wide[...], spare], axis=2).astype(BF16)
        put_rows(range(4), base, 2 * UNIT, full.reshape(4, 2, 2, 2, 2 * UNIT, width))
    else:
        grad_below[...] = grad_rows


def hyper_backward(place, layer, source, valid, vectors, kept, packed, slots, above, columns, after):
    below, mixed, context, middle, inner = kept
    layers, rows, width = below.shape
    inner_width = inner.shape[2]
    last = layer == layers - 1
    at_layer = lambda *shape: pl.BlockSpec((1,) + shape, lambda i: (layer,) + (0,) * len(shape))
    inputs, specs = [place], [pl.BlockSpec(memory_space=pltpu.SMEM)]
    if last:
        arrivals, pooled, pooled_norm = source
        inputs += [*arrivals, pooled, pooled_norm] + [packed] * 4
        specs += [whole_spec(*part.shape) for part in arrivals] + [whole_spec(*pooled.shape)]
        specs += [whole_spec(*pooled_norm.shape)] + proj_specs(width, layers)
    else:
        inputs += [source]
        specs += [whole_spec(rows, width)]
    inputs += [*after, valid, vectors, below, mixed, context, middle, inner]
    specs += [pl.BlockSpec(memory_space=pl.ANY)] * 2
    specs += [whole_spec(1, rows), whole_spec(*vectors.shape), at_layer(rows, width)]
    specs += [at_layer(rows, 3 * width), at_layer(rows, width), at_layer(rows, width)]
    specs += [at_layer(rows, inner_width)]
    inputs += [packed] * (LAYER_UNITS - 3)
    specs += layer_specs(width, lambda i: layer)
    scratch = [pltpu.VMEM((rows, 3 * width), F32)]
    units = LAYER_UNITS + (4 if last else 0) + (2 if layer == 0 else 0)
    below_shape = jax.ShapeDtypeStruct((rows, width), F32)
    if layer == 0:
        inputs += list(above)
        specs += [whole_spec(*part.shape) for part in above]
        below_shape = jax.ShapeDtypeStruct((width // columns, rows, columns), BF16)
        scratch.append(pltpu.VMEM((BLOCKS, 2 * UNIT, 128), F32))
    half = units // 2 * UNIT
    out_shape = [
        jax.ShapeDtypeStruct((2, 2, 4, half, width), BF16),
        jax.ShapeDtypeStruct((2, 2, 4, half, width), BF16),
        jax.ShapeDtypeStruct((2, 2, 4, units * UNIT - half, width), BF16),
        jax.ShapeDtypeStruct((2, 2, 4, units * UNIT - half, width), BF16),
        below_shape,
        jax.ShapeDtypeStruct((VECTORS + (2 if last else 0), width), F32),
        jax.ShapeDtypeStruct((1, inner_width), F32),
    ]
    return pl.pallas_call(
        lambda *refs: hyper_back_kernel(slots, layer, layers, last, *refs),
        grid=(1,),
        in_specs=specs,
        out_specs=[whole_spec(*shape.shape) for shape in out_shape],
        out_shape=out_shape,
        scratch_shapes=scratch,
        compiler_params=pltpu.CompilerParams(vmem_limit_bytes=VMEM_LIMIT),
        cost_estimate=pl.CostEstimate(
            flops=8 * 10**9, bytes_accessed=25 * 10**6, transcendentals=4 * 10**6
        ),
        name="hyper_back",
    )(*inputs)


def pack_kernel(layers, *refs):
    (g1, b1, w_qkv, bq, bv, w_ao, bao, g2, b2, w_in, b_in, w_out, bout, fg, fb, w_proj) = refs[:16]
    packed, wide = refs[16:]
    width = packed.shape[1]
    for layer in range(layers):
        base = layer * LAYER_UNITS * UNIT
        packed[base : base + 4 * UNIT] = w_out[layer]
        for j in range(3):
            at = base + (4 + j) * UNIT
            packed[at : at + UNIT] = w_qkv[layer, :, j * width : (j + 1) * width]
        packed[base + 7 * UNIT : base + 8 * UNIT] = w_ao[layer]
        for j in range(4):
            at = base + (8 + j) * UNIT
            packed[at : at + UNIT] = w_in[layer, :, j * width : (j + 1) * width]
    base = layers * LAYER_UNITS * UNIT
    for j in range(4):
        packed[base + j * UNIT : base + (j + 1) * UNIT] = w_proj[:, j * width : (j + 1) * width]
    wide[...] = jnp.zeros_like(wide)
    for j, ref in enumerate((g1, b1, bq, bv, bao, g2, b2, bout)):
        wide[j * layers : (j + 1) * layers, 0:UNIT] = ref[...].astype(F32)
    at = VECTORS * layers
    wide[at : at + 1, 0:UNIT] = fg[...].astype(F32)
    wide[at + 1 : at + 2, 0:UNIT] = fb[...].astype(F32)
    wide[at + 2 : at + 2 + layers, 0 : 4 * UNIT] = b_in[...].astype(F32)
    base = base + 4 * UNIT
    packed[base:] = jnp.zeros((2 * UNIT, width), BF16)
    packed[base:, : wide.shape[1]] = wide[...].astype(BF16)


def pack_shards(shards):
    (g1, b1, w_qkv, bq, bv, w_ao, bao, g2, b2, w_in, b_in, w_out, bout, fg, fb, w_proj) = shards
    layers, own, _ = w_qkv.shape
    width = w_ao.shape[2]
    if own == UNIT:
        inputs = list(shards)
        inputs[13], inputs[14] = fg[None], fb[None]
        return pl.pallas_call(
            lambda *refs: pack_kernel(layers, *refs),
            out_shape=jax.ShapeDtypeStruct(((layers * LAYER_UNITS + 6) * UNIT, width), BF16),
            scratch_shapes=[pltpu.VMEM((2 * UNIT, 128), F32)],
            name="pack",
        )(*inputs)
    pieces = []
    for layer in range(layers):
        pieces += [w_out[layer]]
        pieces += [w_qkv[layer, :, i * width : (i + 1) * width] for i in range(3)]
        pieces += [w_ao[layer]]
        pieces += [w_in[layer, :, i * width : (i + 1) * width] for i in range(4)]
    pieces += [w_proj[:, i * width : (i + 1) * width] for i in range(4)]
    small = [jnp.concatenate([g1, b1, bq, bv, bao, g2, b2, bout, fg[None], fb[None]]), b_in]
    small = [jnp.pad(part, ((0, 0), (0, width - part.shape[1]))) for part in small]
    small = jnp.concatenate(small)
    small = jnp.pad(small, ((0, 2 * UNIT - small.shape[0]), (0, 0)))
    return jnp.concatenate(pieces + [small])


def piece_rows(layers, own, first_layer=0, last_layer=None):
    return [4 * own] + [own] * (LAYER_UNITS - 4)


def canonical(gathered, own, layers):
    if own == UNIT:
        return gathered
    devices, _, width = gathered.shape
    count = VECTORS * layers + 2
    pieces, at = [], 0
    for rows in piece_rows(layers, own) * layers + [own] * 4:
        pieces.append(gathered[:, at : at + rows].reshape(BLOCKS, -1, width))
        at += rows
    small = []
    for first, rows, each in ((at, count, own), (at + count, layers, 4 * own)):
        part = gathered[:, first : first + rows, :each].reshape(BLOCKS, -1, rows, each)
        part = part.transpose(0, 2, 1, 3).reshape(BLOCKS, rows, -1)
        small.append(jnp.pad(part, ((0, 0), (0, 0), (0, width - part.shape[2]))))
    small = jnp.concatenate(small, axis=1)
    pieces.append(jnp.pad(small, ((0, 0), (0, 2 * UNIT - small.shape[1]), (0, 0))))
    return jnp.concatenate(pieces, axis=1)


def to_devices(packed, devices, rows_list, vector_rows):
    if devices == BLOCKS:
        return packed
    width = packed.shape[2]
    split = devices // BLOCKS
    pieces, at = [], 0
    for rows in rows_list:
        pieces.append(packed[:, at : at + rows].reshape(devices, rows // split, width))
        at += rows
    if vector_rows:
        small = packed[:, at : at + vector_rows]
        narrow = small[:, : vector_rows - 14, :UNIT].reshape(BLOCKS, -1, split, UNIT // split)
        broad = small[:, vector_rows - 14 : vector_rows - 12, : 4 * UNIT]
        broad = broad.reshape(BLOCKS, -1, split, 4 * UNIT // split)
        parts = []
        for part in (narrow, broad):
            part = part.transpose(0, 2, 1, 3).reshape(devices, part.shape[1], part.shape[3])
            parts.append(jnp.pad(part, ((0, 0), (0, 0), (0, width - part.shape[2]))))
        small = jnp.concatenate(parts, axis=1)
        pieces.append(jnp.pad(small, ((0, 0), (0, vector_rows - small.shape[1]), (0, 0))))
    return jnp.concatenate(pieces, axis=1)


def unpack_kernel(layers, above_kept, above_got, below_kept, below_got, g_qkv, g_ao, g_in, g_out, g_proj, *vectors):
    width = above_kept.shape[2]
    above = above_kept[0].astype(F32) + above_got[...].astype(F32)
    below = below_kept[0].astype(F32) + below_got[...].astype(F32)
    for layer, ref in ((0, below), (1, above)):
        g_out[layer] = ref[: 4 * UNIT]
        for j in range(3):
            at = (4 + j) * UNIT
            g_qkv[layer, :, j * width : (j + 1) * width] = ref[at : at + UNIT]
        g_ao[layer] = ref[7 * UNIT : 8 * UNIT]
        for j in range(4):
            at = (8 + j) * UNIT
            g_in[layer, :, j * width : (j + 1) * width] = ref[at : at + UNIT]
    base = LAYER_UNITS * UNIT
    for j in range(4):
        at = base + j * UNIT
        g_proj[:, j * width : (j + 1) * width] = above[at : at + UNIT]
    small = below[base : base + 2 * UNIT, :128]
    for j in range(VECTORS):
        for i in range(layers):
            vectors[j][i : i + 1, :] = small[i * VECTORS + j : i * VECTORS + j + 1, :UNIT]
    count = VECTORS * layers
    vectors[VECTORS][...] = small[count : count + 1, :UNIT]
    vectors[VECTORS + 1][...] = small[count + 1 : count + 2, :UNIT]
    vectors[VECTORS + 2][...] = small[count + 2 : count + 2 + layers, : 4 * UNIT]


def unpack_grads(above, below, own, layers):
    width = above[0].shape[-1]
    count = VECTORS * layers
    if own == UNIT:
        shapes = [
            (layers, own, 3 * width),
            (layers, own, width),
            (layers, own, 4 * width),
            (layers, 4 * own, width),
            (own, 4 * width),
        ]
        shapes += [(layers, own)] * VECTORS + [(1, own), (1, own), (layers, 4 * own)]
        outs = pl.pallas_call(
            lambda *refs: unpack_kernel(layers, *refs),
            out_shape=[jax.ShapeDtypeStruct(shape, F32) for shape in shapes],
            name="unpack",
        )(*above, *below)
        return outs[:5], outs[5:13], outs[13][0], outs[14][0], outs[15]
    parts = []
    for ref in (below, above):
        cuts, at = [], 0
        for rows in piece_rows(layers, own):
            cuts.append(ref[at : at + rows].astype(F32))
            at += rows
        parts.append(cuts)
    mats = [
        jnp.stack([jnp.concatenate(cuts[1:4], axis=1) for cuts in parts]),
        jnp.stack([cuts[4] for cuts in parts]),
        jnp.stack([jnp.concatenate(cuts[5:9], axis=1) for cuts in parts]),
        jnp.stack([cuts[0] for cuts in parts]),
        jnp.concatenate(
            [above[at + i * own : at + (i + 1) * own].astype(F32) for i in range(4)], axis=1
        ),
    ]
    small = below[at : at + 2 * UNIT, :128].astype(F32)
    vectors = [
        jnp.stack([small[i * VECTORS + j, :own] for i in range(layers)]) for j in range(VECTORS)
    ]
    inner_bias = small[count + 2 : count + 2 + layers, : 4 * own]
    return mats, vectors, small[count, :own], small[count + 1, :own], inner_bias


def pair_swap(values, bit):
    return swap(values, "tensor", bit)


def halve_kernel(mine_a, got_a, mine_b, got_b, _after_one, _after_two, keep_a, send_a, keep_b, send_b):
    for mine, got, keep, send in ((mine_a, got_a, keep_a, send_a), (mine_b, got_b, keep_b, send_b)):
        for i, out in enumerate((keep, send)):
            out[...] = (mine[i].astype(F32) + got[i].astype(F32)).astype(BF16)


def halve_after(mine_a, got_a, mine_b, got_b, *after):
    width = mine_a.shape[-1]
    count = mine_a[0].size // (mine_a.shape[-2] * width)
    together = 2
    inputs, specs, outs, out_specs = [], [], [], []
    for mine, got in ((mine_a, got_a), (mine_b, got_b)):
        rows = mine.shape[-2]
        inputs += [part.reshape(2, count, rows, width) for part in (mine, got)]
        specs += [pl.BlockSpec((2, together, rows, width), lambda i: (0, i, 0, 0))] * 2
        outs += [jax.ShapeDtypeStruct((count, rows, width), BF16)] * 2
        out_specs += [pl.BlockSpec((together, rows, width), lambda i: (i, 0, 0))] * 2
    halves = pl.pallas_call(
        halve_kernel,
        grid=(count // together,),
        in_specs=specs + [pl.BlockSpec(memory_space=pl.ANY)] * 2,
        out_specs=out_specs,
        out_shape=outs,
        name="halve_after",
    )(*inputs, after[0], after[-1])
    shapes = [part.shape[1:] for part in (mine_a, mine_a, mine_b, mine_b)]
    return [half.reshape(shape) for half, shape in zip(halves, shapes)]


def join_kernel(kept_a, got_a, kept_b, got_b, _after_one, _after_two, rest, last):
    rows = kept_a.shape[1]
    for at, kept, got in ((slice(0, rows), kept_a, got_a), (slice(rows, None), kept_b, got_b)):
        total = (kept[...].astype(F32) + got[...].astype(F32)).astype(BF16)
        rest[:, at, :] = total[:-1]
        last[at, :] = total[-1]


def join_after(kept_a, got_a, kept_b, got_b, *after):
    line, rows_a, width = kept_a.shape
    rows = rows_a + kept_b.shape[1]
    vmem = pl.BlockSpec(memory_space=pltpu.VMEM)
    return pl.pallas_call(
        join_kernel,
        in_specs=[vmem] * 4 + [pl.BlockSpec(memory_space=pl.ANY)] * 2,
        out_specs=[vmem] * 2,
        out_shape=[
            jax.ShapeDtypeStruct((line - 1, rows, width), BF16),
            jax.ShapeDtypeStruct((rows, width), BF16),
        ],
        name="join_after",
    )(kept_a, got_a, kept_b, got_b, after[0], after[-1])


def stack_kernel(p0, p1, p2, p3, _after_one, _after_two, out):
    for k, part in enumerate((p0, p1, p2, p3)):
        out[k] = part[...]


def stack_after(parts, *after):
    vmem = pl.BlockSpec(memory_space=pltpu.VMEM)
    return pl.pallas_call(
        stack_kernel,
        in_specs=[vmem] * 4 + [pl.BlockSpec(memory_space=pl.ANY)] * 2,
        out_specs=vmem,
        out_shape=jax.ShapeDtypeStruct((4,) + parts[0].shape, parts[0].dtype),
        name="stack_after",
    )(*parts, *after)


def next_on_line(values):
    size = lax.axis_size("dp")
    return lax.ppermute(values, "dp", [(i, (i + 2) % size) for i in range(size)])


def scatter_line(rest, last):
    totals = [last]
    for ahead in (2, 1):
        got = next_on_line(totals[-1])
        totals.append((rest[ahead].astype(F32) + got.astype(F32)).astype(BF16))
    return totals[1], totals[2], next_on_line(totals[2])


def gather_line(values, *after):
    parts = [values]
    for step in range(lax.axis_size("dp") // 2 - 1):
        sent = parts[-1] if step >= len(after) else tie(parts[-1], after[step])
        parts.append(next_on_line(sent))
    return parts


def sum_grads(packed, rows_list, vector_rows):
    packed_a = jnp.stack(packed[:2]).transpose(3, 2, 1, 0, 4, 5)
    packed_b = jnp.stack(packed[2:]).transpose(3, 1, 2, 0, 4, 5)
    packed = jnp.concatenate([packed_a, packed_b], axis=4)
    packed = packed.reshape((BLOCKS,) + packed.shape[4:])
    packed = to_devices(packed, 4 * lax.axis_size("dp"), rows_list, vector_rows)
    return lax.psum_scatter(packed, BOTH, scatter_dimension=0, tiled=True)[0]


def dp_bits():
    size = lax.axis_size("dp")
    return [1 << i for i in range(size.bit_length() - 1)]


def dp_places():
    bits = dp_bits()
    return [
        sum(bit for i, bit in enumerate(reversed(bits)) if (place >> i) & 1)
        for place in range(lax.axis_size("dp"))
    ]


def gather_relative(values, first, last):
    for bit in list(reversed(dp_bits()))[first:last]:
        values = jnp.concatenate([values, swap(values, "dp", bit)])
    return values


def reduce_relative(keep, send):
    bits = dp_bits()
    first = keep = keep + swap(send, "dp", bits[0])
    for bit in bits[1:]:
        half = keep.shape[0] // 2
        keep = keep[:half] + swap(keep[half:], "dp", bit)
    return keep[0], first


def exchange_relative(first, second, third):
    return [pair_swap(first, 1), pair_swap(second, 2), pair_swap(third, 3)]


def local(
    piece_table,
    piece_ids,
    piece_counts,
    text_ids,
    cotangent,
    rms_gain_one,
    w_query,
    w_key,
    w_value,
    w_output,
    rms_gain_two,
    w_gate,
    w_up,
    w_down,
    *shard_params,
):
    tensor_index = lax.axis_index("tensor")
    dp_index = lax.axis_index("dp")
    tensor_size = lax.axis_size("tensor")
    dp_size = lax.axis_size("dp")
    devices = tensor_size * dp_size
    micro_count, group_entries, slot_count = piece_ids.shape
    own_entries = group_entries // tensor_size
    seq_length = text_ids.shape[1]
    share = cotangent.shape[1]
    layer_count, own, _ = shard_params[2].shape
    width = shard_params[5].shape[2]
    lm_width = cotangent.shape[2]
    table_rows, table_cols = piece_table.shape
    gain_first = rms_gain_one[None, :]
    gain_second = rms_gain_two[None, :]
    cosine, sine = rotary_tables(seq_length)
    trig = jnp.concatenate([cosine.T, sine.T], axis=0)
    w_kv = jnp.concatenate([w_key, w_value], axis=1)

    where = tensor_index.astype(jnp.int32)[None]

    gathered = lax.all_gather(pack_shards(shard_params), BOTH, axis=0)

    stages = len(dp_bits())
    ids_rel = gather_relative(piece_ids[None], 0, stages)
    ids_rel = ids_rel.reshape(dp_size, micro_count, tensor_size, own_entries, slot_count)
    ids_rel = jnp.take(ids_rel, tensor_index ^ jnp.arange(tensor_size), axis=2)
    ids_rel = ids_rel.transpose(0, 2, 1, 3, 4) - dp_index * table_rows
    places = jnp.asarray(dp_places())
    ids_back = jnp.zeros_like(ids_rel).at[dp_index ^ places].set(ids_rel)
    if dp_size == 8:
        behind = (dp_index + dp_size - 2 * jnp.arange(dp_size // 2)) % dp_size
        ids_back = jnp.take(ids_back, jnp.stack([behind, behind ^ 1], axis=1).reshape(-1), axis=0)
    ids_back = ids_back.reshape(4, -1)
    ids_columns = [ids[:, None] for ids in ids_back]
    ids_rel = ids_rel.reshape(2, -1)
    own_rows = micro_count * own_entries * slot_count
    looked = []
    for i in (1, 0):
        rows = lookup(ids_rel[i], piece_table, looked[0] if looked else ids_rel)
        looked.append(rows.reshape(dp_size // 2, tensor_size, own_rows, table_cols))
    near_looked = looked[1]
    looked, _ = reduce_relative(looked[1], looked[0])
    pieces = [looked[0], *exchange_relative(*looked[1:])]

    text_rel = text_ids ^ (tensor_index * own_entries)
    micros = range(micro_count)
    ids_row, ids_own, ids_peer = [], [], []
    for micro in micros:
        row = text_rel[micro][None, :]
        ids_row.append(row)
        ids_own.append(lax.dynamic_slice_in_dim(row, tensor_index * share, share, 1))
        ids_peer.append(lax.dynamic_slice_in_dim(row, (tensor_index ^ 2) * share, share, 1))
    ids_small = jnp.stack(ids_own + ids_peer)

    packed = canonical(gathered, own, layer_count)
    counts_own = lax.dynamic_slice_in_dim(piece_counts, tensor_index * own_entries, own_entries, 1)
    valid = jnp.arange(slot_count)[None, :] < counts_own.reshape(-1)[:, None]
    valid = valid.astype(F32).reshape(1, own_rows)
    w_out = [w_output, pair_swap(w_output, 1), pair_swap(w_output, 2)]
    cots = [cast_after(micro, cotangent, near_looked) for micro in range(micro_count)]
    grads_near = [
        [matmul_right_t(part, w_down).astype(BF16) for part in (cot, pair_swap(cot, 1))]
        for cot in cots
    ]
    vectors, _, *kept_hyper, pooled, pooled_norm, embeds = hyper_forward(
        where, (w_out[2], *grads_near[0], *grads_near[1], trig, ids_small, *ids_columns, ids_back), pieces, valid, packed, slot_count, layer_count
    )

    w_out.append(pair_swap(w_out[2], 1))
    embeds = embeds.reshape(micro_count, own_entries, lm_width)
    embeds = [embeds] + [pair_swap(embeds, k) for k in (1, 2, 3)]

    def peer_cot(micro, after):
        cot = pair_swap(tie(cots[micro], after), 2)
        return cot, pair_swap(cot, 1)

    cots_peer = [peer_cot(0, embeds[3])]
    kept_attn, contexts = [], []
    after = (embeds[0], embeds[0])
    for micro in micros:
        near, far, *kept = attend(
            where, micro, embeds, gain_first, w_query, w_kv, ids_row[micro], trig, after
        )
        kept_attn.append(kept)
        contexts.append([near, *exchange_relative(far, near, far)])
        after = (near, near)

    def after_attention(micro, after):
        own, peer, rows = hidden_rows_of(
            kept_attn[micro][-1], ids_own[micro], ids_peer[micro], gain_second,
            contexts[micro], w_out, after,
        )
        return (own, pair_swap(own, 1)), (peer, pair_swap(peer, 1)), rows

    def feed_forward(normed, grads_in, *after):
        after = (after + after[:1] * 2)[:3]
        return mlp(*normed, *grads_in, w_gate, w_up, w_down, after)

    def travel(part):
        from_core = jnp.concatenate([pair_swap(half, 1) for half in part[3:]])
        away = (part[2].astype(F32) + from_core.astype(F32)).astype(BF16)
        return away, pair_swap(away, 2)

    def back_of(micro, rows, near, arrived):
        low, *parts = hidden_back(
            micro, cotangent, rows, near[2], [pair_swap(half, 1) for half in near[3:]], arrived,
            gain_second, w_out,
        )
        return low, [parts[0], *exchange_relative(*parts[1:])]

    def send_result(peer, after):
        total = (peer[0].astype(F32) + pair_swap(peer[1], 1).astype(F32)).astype(BF16)
        return pair_swap(tie(total, after), 2)

    near_in, peer_in, rows_a = after_attention(0, (contexts[1][0], cots_peer[0][0]))
    near_a = feed_forward(near_in, grads_near[0], rows_a)
    cots_peer.append(peer_cot(1, near_a[2]))
    peer_a = feed_forward(peer_in, cots_peer[0], near_a[2], contexts[1][2], contexts[1][3])
    away_a, arrived_a = travel(peer_a)
    near_in, peer_in, rows_b = after_attention(1, (away_a, cots_peer[1][0]))
    peer_b = feed_forward(peer_in, cots_peer[1], rows_b)
    away_b, arrived_b = travel(peer_b)
    low_a, parts_a = back_of(0, rows_a, near_a, arrived_a)
    near_b = feed_forward(near_in, grads_near[1], low_a, away_b)
    result_a = send_result(peer_a, near_b[2])
    low_b, parts_b = back_of(1, rows_b, near_b, arrived_b)

    place = jnp.stack([tensor_index % 2, tensor_index // 2, dp_index % 2, dp_index // 2])
    place = place.astype(jnp.int32)
    grad_embeds = []
    after = (low_b,) * 5
    near_swapped = [pair_swap(near[1], 1) for near in (near_a, near_b)]
    for micro, parts, low in ((0, parts_a, low_a), (1, parts_b, low_b)):
        grads = attend_back(
            where, parts, kept_attn[micro], ids_row[micro], ids_own[micro], trig,
            w_query, w_kv, gain_first, low, after,
        )
        after = (grads[0], result_a, parts_b[2], *near_swapped)
        if micro == 0:
            result_b = send_result(peer_b, grads[0])
        grad_embeds += [grads[0], *exchange_relative(*grads[1:])]

    if dp_size != 8:
        place = place * 0
    source = (grad_embeds, pooled, pooled_norm)
    packs, above, after = [None] * layer_count, (), (result_b, result_b)
    near_side, near_chip = ("dp", 1), ("tensor", 2)
    for layer in range(layer_count - 1, -1, -1):
        *parts, source, small, inner_small = hyper_backward(
            place, layer, source, valid, vectors, kept_hyper, packed, slot_count, above,
            table_cols, after,
        )
        above = (small, inner_small)
        packs[layer] = parts
        if dp_size == 8 and layer == layer_count - 1:
            upper = halve_after(
                parts[0], pair_swap(parts[1], 1), parts[2], pair_swap(parts[3], 1), small
            )
            after = (upper[1], upper[3])
    if dp_size == 8:
        parts = packs[0]
        from_chip = pair_swap(source[2:], 2)
        results = add_results(
            (rows_a, near_a[0], near_swapped[0], result_a),
            (rows_b, near_b[0], near_swapped[1], result_b),
            parts[0],
        )
        upper = halve_after(
            upper[0], swap(upper[1], *near_chip), upper[2], swap(upper[3], *near_side), results
        )
        upper_got = swap(upper[3], *near_chip)
        other_a, other_b = tie(parts[1], upper[1]), tie(parts[3], upper[1])
        from_chip = pair_swap(source[2:], 2)
        lower = halve_after(
            parts[0], pair_swap(other_a, 1), parts[2], pair_swap(other_b, 1), upper[1]
        )
        near_piece, forward = tie(source[1], lower[1]), tie(from_chip[1], lower[1])
        pieces = [source[0], pair_swap(near_piece, 1), from_chip[0], pair_swap(forward, 1)]
        pieces = stack_after(pieces, upper_got, lower[1])
        upper_rest, last = join_after(
            upper[0], swap(upper[1], *near_side), upper[2], upper_got, pieces
        )
        sent = [tie(lower[1], last), tie(lower[3], last)]
        pieces = gather_line(jnp.stack([pieces, swap(pieces, "dp", 1)]), last)
        pieces = [part.reshape(-1, table_cols) for part in pieces]
        step_one, step_two, upper_got = scatter_line(upper_rest, last)
        table_grad = collect(ids_back[:2], ids_columns[:2], pieces[0], pieces[1], table_rows, None)
        lower = halve_after(
            lower[0], swap(sent[0], *near_chip), lower[2], swap(sent[1], *near_side), last
        )
        lower_rest, last = join_after(
            lower[0], swap(lower[1], *near_side), lower[2], swap(lower[3], *near_chip), table_grad, step_two
        )
        *_, lower_got = scatter_line(lower_rest, last)
        reduced = [(lower_rest, lower_got), (upper_rest, upper_got)]
    else:
        pieces = jnp.take(source, tensor_index ^ jnp.arange(tensor_size), axis=0)
        pieces = jnp.stack([pieces[0], *exchange_relative(*pieces[1:])])
        pieces = lax.all_gather(pieces, "dp", axis=0).reshape(4, -1, table_cols)
        rows_list = piece_rows(layer_count, UNIT)
        reduced = [
            sum_grads(packs[0], rows_list, 2 * UNIT),
            sum_grads(packs[1], rows_list + [UNIT] * 4, 0),
        ]
        table_grad = collect(ids_back[:2], ids_columns[:2], pieces[0], pieces[1], table_rows, None)
        results = add_results(
            (rows_a, near_a[0], near_swapped[0], result_a),
            (rows_b, near_b[0], near_swapped[1], result_b),
            table_grad,
        )
    table_grad = collect(ids_back[2:], ids_columns[2:], pieces[2], pieces[3], table_rows, table_grad)

    mats, vecs, out_final_gain, out_final_bias, out_inner_bias = unpack_grads(
        reduced[1], reduced[0], own, layer_count
    )
    return (
        results,
        table_grad,
        vecs[0],
        vecs[1],
        mats[0],
        vecs[2],
        vecs[3],
        mats[1],
        vecs[4],
        vecs[5],
        vecs[6],
        mats[2],
        out_inner_bias,
        mats[3],
        vecs[7],
        out_final_gain,
        out_final_bias,
        mats[4],
    )


def solution(mesh):
    return jax.shard_map(
        local,
        mesh=mesh,
        in_specs=(
            P("dp", "tensor"),
            P(None, "dp", None),
            P(None, "dp"),
            P(None, "dp"),
            P(None, ("dp", "tensor"), None),
            P(),
            P(None, "tensor"),
            P(None, "tensor"),
            P(None, "tensor"),
            P("tensor", None),
            P(),
            P(None, "tensor"),
            P(None, "tensor"),
            P("tensor", None),
            P(None, ("dp", "tensor")),
            P(None, ("dp", "tensor")),
            P(None, ("dp", "tensor"), None),
            P(None, ("dp", "tensor")),
            P(None, ("dp", "tensor")),
            P(None, ("dp", "tensor"), None),
            P(None, ("dp", "tensor")),
            P(None, ("dp", "tensor")),
            P(None, ("dp", "tensor")),
            P(None, ("dp", "tensor"), None),
            P(None, ("dp", "tensor")),
            P(None, ("dp", "tensor"), None),
            P(None, ("dp", "tensor")),
            P(("dp", "tensor")),
            P(("dp", "tensor")),
            P(("dp", "tensor"), None),
        ),
        out_specs=(
            P(None, ("dp", "tensor"), None),
            P("dp", "tensor"),
            P(None, ("dp", "tensor")),
            P(None, ("dp", "tensor")),
            P(None, ("dp", "tensor"), None),
            P(None, ("dp", "tensor")),
            P(None, ("dp", "tensor")),
            P(None, ("dp", "tensor"), None),
            P(None, ("dp", "tensor")),
            P(None, ("dp", "tensor")),
            P(None, ("dp", "tensor")),
            P(None, ("dp", "tensor"), None),
            P(None, ("dp", "tensor")),
            P(None, ("dp", "tensor"), None),
            P(None, ("dp", "tensor")),
            P(("dp", "tensor")),
            P(("dp", "tensor")),
            P(("dp", "tensor"), None),
        ),
        check_vma=False,
    )
```
